256 devices in a mesh: strip: 4 (over y_lo, core), depth: 64 (over y_hi, x, z).
Axes of the slice: x: 4, y: 4 (y_hi: 2, y_lo: 2; y = y_hi * 2 + y_lo), z: 8, core: 2. Of those that a mesh axis runs over, the one named last changes fastest.
Arguments:
- position: float32 [4, 64, 3, 32, 128], P('strip', 'depth'), may hold values from -2.4 to 2.4
- velocity: float32 [4, 64, 3, 32, 128], P('strip', 'depth'), may hold values from -3 to 3
- stress: float32 [4, 64, 6, 32, 128], P('strip', 'depth'), may hold values from -6 to 6
- plastic: float32 [4, 64, 32, 128], P('strip', 'depth'), may hold values from 0.005 to 0.2
- particle_mass: float32 [4, 64, 32, 128], P('strip', 'depth'), may hold values from 0.004 to 0.016
- density: float32 [4, 64, 32, 128], P('strip', 'depth'), may hold values from 0.6 to 1.6
- cohesion: float32 [4, 64, 32, 128], P('strip', 'depth'), may hold values from 0.3 to 1.2
- counts: int32 [4, 64, 32], P('strip', 'depth'), may hold values from 32 to 128, as said below
- block_pairs: int32 [4, 64, 128, 2], P('strip', 'depth'), may hold values from 0 to 31, as said below
- pair_count: int32 [4, 64], P('strip', 'depth'), may hold values from 32 to 128, as said below
- send_lists: int32 [4, 64, 4, 16], P('strip', 'depth'), may hold values from 0 to 31, as said below
- cross_links: int32 [4, 64, 2, 48, 2], P('strip', 'depth'), may hold values from 0 to 15, as said below
- contact: int32 [4, 64, 16], P('strip', 'depth'), may hold values from 0 to 32, as said below
Outputs:
- new_position: float32 [4, 64, 3, 32, 128], P('strip', 'depth')
- new_velocity: float32 [4, 64, 3, 32, 128], P('strip', 'depth')
- new_stress: float32 [4, 64, 6, 32, 128], P('strip', 'depth')
- new_plastic: float32 [4, 64, 32, 128], P('strip', 'depth')
The draws below stay inside these ranges and needn't reach their ends.
Inputs may be any that keep to these rules, and one draw needn't show every extreme that they name: A block's live particles are its first counts slots; every device has a full block. `pair_count`: at least 32; some device reaches 128. `block_pairs`: the first pair_count entries of a device hold each of its blocks paired with itself once and distinct unordered pairs of different blocks, each at most once, in either order; later entries are to be ignored. `send_lists`: each face lists 16 distinct blocks; faces 0, 1 look to the next and previous device along depth, 2, 3 along strip. `cross_links`: entry (f, q) = (a, b): slot a of the device's list 2f meets slot b of the next device's list 2f + 1; a face's entries are distinct. `contact`: 32 stands for no block; a device's entries are either all 32 or 16 distinct blocks.
All inputs are finite; a program needn't handle non-finite values.
Results may differ from the reference program's by a relative error of at most 0.0003.
Values sent between devices are 32-bit elements; how exact they have to be, the bound alone decides.
No kernel may reach another device: no remote copies, remote signals or barrier semaphores. Data moves between devices by JAX's collectives and lax.ppermute only.
A program may use at most 64 MiB of HBM per device.

```python
import math
import jax
import jax.numpy as jnp
import numpy as np
from jax import lax

BLOCKS = 32
PARTICLES = 128
PAIR_RATIO = 3
RIM = 16
CROSS = 48
CONTACT = 16
RETURN_ITERS = 4
N_STRIP = 4
N_DEPTH = 64


def band_distance(key):
    centre = jax.random.randint(jax.random.fold_in(key, 101), (N_STRIP, 1), 0, N_DEPTH)
    depth_index = jnp.arange(N_DEPTH, dtype=jnp.int32)[None, :]
    return jnp.abs(depth_index - centre)


def pair_totals(key):
    distance = band_distance(key)
    band_width = max(N_DEPTH // 8, 1)
    off_most = PAIR_RATIO * BLOCKS
    jitter = jax.random.randint(jax.random.fold_in(key, 102), (N_STRIP, N_DEPTH), 0, off_most // 16 + 1)
    jitter = jnp.where(distance > 0, jitter, 0)
    off_live = off_most - jnp.minimum(distance, band_width) * (2 * off_most // 3) // band_width - jitter
    return (BLOCKS + off_live).astype(jnp.int32)


def draw_pair_count(key, part):
    return pair_totals(key)


def draw_block_pairs(key, part):
    totals = pair_totals(key).reshape(-1)
    upper_np, lower_np = np.triu_indices(BLOCKS, 1)
    upper_rows = jnp.asarray(upper_np, jnp.int32)
    upper_cols = jnp.asarray(lower_np, jnp.int32)
    off_most = PAIR_RATIO * BLOCKS
    slot_total = BLOCKS + off_most
    device_keys = jax.random.split(jax.random.fold_in(key, 103), N_STRIP * N_DEPTH)

    def one_device(device_key, live_total):
        pick_key, order_key, swap_key = jax.random.split(device_key, 3)
        chosen = jax.random.permutation(pick_key, upper_np.shape[0])[:off_most]
        diagonal_blocks = jnp.arange(BLOCKS, dtype=jnp.int32)
        row_block = jnp.concatenate([diagonal_blocks, upper_rows[chosen]])
        col_block = jnp.concatenate([diagonal_blocks, upper_cols[chosen]])
        reversed_pair = jax.random.randint(swap_key, (slot_total,), 0, 2)
        row_final = jnp.where(reversed_pair == 1, col_block, row_block)
        col_final = jnp.where(reversed_pair == 1, row_block, col_block)
        slot_index = jnp.arange(slot_total, dtype=jnp.int32)
        ranking = jax.random.permutation(order_key, slot_total).astype(jnp.int32)
        priority = jnp.where(slot_index < live_total, ranking, slot_total + slot_index)
        ordering = jnp.argsort(priority)
        return jnp.stack([row_final[ordering], col_final[ordering]], axis=-1).astype(jnp.int32)
    return jax.vmap(one_device)(device_keys, totals).reshape(N_STRIP, N_DEPTH, slot_total, 2)


def draw_send_lists(key, part):
    face_keys = jax.random.split(jax.random.fold_in(key, 104), N_STRIP * N_DEPTH * 4)

    def one_face(face_key):
        return jax.random.permutation(face_key, BLOCKS)[:RIM].astype(jnp.int32)
    return jax.vmap(one_face)(face_keys).reshape(N_STRIP, N_DEPTH, 4, RIM)


def draw_cross_links(key, part):
    face_keys = jax.random.split(jax.random.fold_in(key, 105), N_STRIP * N_DEPTH * 2)

    def one_face(face_key):
        picked = jax.random.permutation(face_key, RIM * RIM)[:CROSS].astype(jnp.int32)
        return jnp.stack([picked // RIM, picked % RIM], axis=-1)
    return jax.vmap(one_face)(face_keys).reshape(N_STRIP, N_DEPTH, 2, CROSS, 2)


def draw_contact(key, part):
    distance = band_distance(key).reshape(-1)
    device_keys = jax.random.split(jax.random.fold_in(key, 107), N_STRIP * N_DEPTH)

    def one_device(device_key, distance_one):
        picked = jax.random.permutation(device_key, BLOCKS)[:CONTACT].astype(jnp.int32)
        return jnp.where(distance_one <= 1, picked, BLOCKS).astype(jnp.int32)
    return jax.vmap(one_device)(device_keys, distance).reshape(N_STRIP, N_DEPTH, CONTACT)


def draw_counts(key, part):
    fill_key, full_key = jax.random.split(jax.random.fold_in(key, 106))
    counts = jax.random.randint(fill_key, (N_STRIP, N_DEPTH, BLOCKS), 32, PARTICLES + 1)
    full_block = jax.random.randint(full_key, (N_STRIP, N_DEPTH, 1), 0, BLOCKS)
    block_index = jnp.arange(BLOCKS, dtype=jnp.int32)[None, None, :]
    return jnp.where(block_index == full_block, PARTICLES, counts).astype(jnp.int32)


def level_of(key, extent, cuts, low, largest):
    def one(dim, shards_of):
        steps = jax.random.uniform(jax.random.fold_in(jax.random.fold_in(key, 6), dim), (shards_of,), jnp.float32, low / len(cuts), largest / len(cuts))
        return jnp.repeat(jnp.exp(steps), extent[dim] // shards_of).reshape((-1,) + (1,) * (len(extent) - dim - 1))

    loudness = one(*cuts[0])
    for cut in cuts[1:]:
        loudness = loudness * one(*cut)
    return loudness


def bell_draw(key, extent, scale, limit, cuts=(), kind=jnp.bfloat16):
    loudness = level_of(key, extent, cuts, -0.22, 0.18) if cuts else 1.0
    values = jax.random.normal(key, extent, jnp.float32) * scale * loudness
    return jnp.minimum(jnp.maximum(values, -limit), limit).astype(kind)


def setup_inputs(seed: int = 0) -> dict:
    key_of = jax.random.split(jax.random.key(seed), 14)
    position = bell_draw(key_of[0], (N_STRIP, N_DEPTH, 3, BLOCKS, PARTICLES), 0.4, 2.4, ((0, 4), (1, 64)), jnp.float32)
    velocity = bell_draw(key_of[1], (N_STRIP, N_DEPTH, 3, BLOCKS, PARTICLES), 0.5, 3.0, ((0, 4), (1, 64)), jnp.float32)
    stress = bell_draw(key_of[2], (N_STRIP, N_DEPTH, 6, BLOCKS, PARTICLES), 1.0, 6.0, ((0, 4), (1, 64)), jnp.float32)
    plastic = jnp.clip(jnp.exp(math.log(0.2) - 3.6888795 * jax.random.uniform(key_of[3], (N_STRIP, N_DEPTH, BLOCKS, PARTICLES), jnp.float32) ** level_of(key_of[3], (N_STRIP, N_DEPTH, BLOCKS, PARTICLES), ((0, 4), (1, 64)), -0.2, 0.2)), 0.005, 0.2)
    particle_mass = jnp.clip(jnp.exp(math.log(0.016) - 1.3862944 * jax.random.uniform(key_of[4], (N_STRIP, N_DEPTH, BLOCKS, PARTICLES), jnp.float32) ** level_of(key_of[4], (N_STRIP, N_DEPTH, BLOCKS, PARTICLES), ((0, 4), (1, 64)), -0.2, 0.2)), 0.004, 0.016)
    density = jnp.clip(jnp.exp(math.log(1.6) - 0.98082923 * jax.random.uniform(key_of[5], (N_STRIP, N_DEPTH, BLOCKS, PARTICLES), jnp.float32) ** level_of(key_of[5], (N_STRIP, N_DEPTH, BLOCKS, PARTICLES), ((0, 4), (1, 64)), -0.2, 0.2)), 0.6, 1.6)
    cohesion = jnp.clip(jnp.exp(math.log(1.2) - 1.3862944 * jax.random.uniform(key_of[6], (N_STRIP, N_DEPTH, BLOCKS, PARTICLES), jnp.float32) ** level_of(key_of[6], (N_STRIP, N_DEPTH, BLOCKS, PARTICLES), ((0, 4), (1, 64)), -0.2, 0.2)), 0.3, 1.2)
    counts = draw_counts(jax.random.fold_in(key_of[13], 71), 0)
    block_pairs = draw_block_pairs(jax.random.fold_in(key_of[13], 71), 0)
    pair_count = draw_pair_count(jax.random.fold_in(key_of[13], 71), 0)
    send_lists = draw_send_lists(jax.random.fold_in(key_of[13], 71), 0)
    cross_links = draw_cross_links(jax.random.fold_in(key_of[13], 71), 0)
    contact = draw_contact(jax.random.fold_in(key_of[13], 71), 0)
    return dict(position=position, velocity=velocity, stress=stress, plastic=plastic, particle_mass=particle_mass, density=density, cohesion=cohesion, counts=counts, block_pairs=block_pairs, pair_count=pair_count, send_lists=send_lists, cross_links=cross_links, contact=contact)


smooth_len = 1.5
kernel_coef = -105.0 / (3.141592653589793 * 1.5 ** 5)
time_step = 0.25
gravity = 1.0
spin_rate = 2.0
blade_stiff = 4.0
bulk_mod = 2.0
shear_mod = 1.5
friction = 0.25
harden_scale = 0.05
harden_mod = 0.5
relax_rate = 0.7
tau_floor = 0.5
voigt_index = ((0, 3, 5), (3, 1, 4), (5, 4, 2))
voigt_pairs = ((0, 0), (1, 1), (2, 2), (0, 1), (1, 2), (0, 2))

def source_rows(places, motion, stress, particle_mass, density, occupied):
    safe_density = jnp.where(occupied > 0.0, density, 1.0)
    weighted_mass = particle_mass * occupied
    volume = weighted_mass / safe_density
    scaled = stress / (safe_density * safe_density)[..., None, :]
    feature_rows = [weighted_mass]
    for row_axis in range(3):
        feature_rows.append(weighted_mass * places[..., row_axis, :])
    for component in range(6):
        feature_rows.append(weighted_mass * scaled[..., component, :])
    for row_axis in range(3):
        dotted = scaled[..., voigt_index[row_axis][0], :] * places[..., 0, :]
        dotted = dotted + scaled[..., voigt_index[row_axis][1], :] * places[..., 1, :]
        dotted = dotted + scaled[..., voigt_index[row_axis][2], :] * places[..., 2, :]
        feature_rows.append(weighted_mass * dotted)
    feature_rows.append(volume)
    for row_axis in range(3):
        feature_rows.append(volume * motion[..., row_axis, :])
    for row_axis in range(3):
        feature_rows.append(volume * places[..., row_axis, :])
    for row_axis, col_axis in voigt_pairs:
        paired = motion[..., row_axis, :] * places[..., col_axis, :] + motion[..., col_axis, :] * places[..., row_axis, :]
        feature_rows.append(volume * (0.5 * paired))
    return jnp.stack(feature_rows, axis=-2)

def pair_kernel(row_places, col_places, weight):
    squared = jnp.zeros(row_places.shape[:-2] + (row_places.shape[-1], col_places.shape[-1]), jnp.float32)
    for row_axis in range(3):
        spread = row_places[..., row_axis, :, None] - col_places[..., row_axis, None, :]
        squared = squared + spread * spread
    closeness = jnp.maximum(1.0 - jnp.sqrt(squared) / smooth_len, 0.0)
    return kernel_coef * closeness * closeness * closeness * weight[..., None, None]

def tile_terms(row_sources, row_places, col_sources, col_places, weight):
    kernel = pair_kernel(row_places, col_places, weight)
    to_rows = jnp.einsum('tkj,tij->tki', col_sources, kernel, precision=lax.Precision.HIGHEST)
    to_cols = jnp.einsum('tki,tij->tkj', row_sources, kernel, precision=lax.Precision.HIGHEST)
    return (to_rows, to_cols)

def section_rates(summed, places, motion, stress, density, contact_flag):
    scaled = stress / (density * density)[..., None, :]
    blade_motion = (spin_rate * places[..., 2, :], jnp.zeros_like(places[..., 1, :]), -spin_rate * places[..., 0, :])
    acceleration = []
    for row_axis in range(3):
        total_force = jnp.zeros_like(summed[..., 0, :])
        for col_axis in range(3):
            voigt_slot = voigt_index[row_axis][col_axis]
            total_force = total_force + scaled[..., voigt_slot, :] * (places[..., col_axis, :] * summed[..., 0, :] - summed[..., 1 + col_axis, :])
            total_force = total_force + places[..., col_axis, :] * summed[..., 4 + voigt_slot, :]
        total_force = total_force - summed[..., 10 + row_axis, :]
        total_force = total_force + blade_stiff * contact_flag * (blade_motion[row_axis] - motion[..., row_axis, :])
        if row_axis == 2:
            total_force = total_force - gravity
        acceleration.append(total_force)
    strain = []
    for component, (row_axis, col_axis) in enumerate(voigt_pairs):
        strain_rate = 0.5 * (places[..., col_axis, :] * summed[..., 14 + row_axis, :] + places[..., row_axis, :] * summed[..., 14 + col_axis, :])
        strain_rate = strain_rate - summed[..., 20 + component, :]
        strain_rate = strain_rate - 0.5 * summed[..., 13, :] * (motion[..., row_axis, :] * places[..., col_axis, :] + motion[..., col_axis, :] * places[..., row_axis, :])
        strain_rate = strain_rate + 0.5 * (motion[..., row_axis, :] * summed[..., 17 + col_axis, :] + motion[..., col_axis, :] * summed[..., 17 + row_axis, :])
        strain.append(strain_rate)
    return (jnp.stack(acceleration, axis=-2), jnp.stack(strain, axis=-2))

def elastic_step(stress, strain, fraction):
    volumetric = strain[..., 0, :] + strain[..., 1, :] + strain[..., 2, :]
    lame_first = bulk_mod - 2.0 * shear_mod / 3.0
    components = []
    for component in range(6):
        change = 2.0 * shear_mod * strain[..., component, :]
        if component < 3:
            change = change + lame_first * volumetric
        components.append(stress[..., component, :] + fraction * time_step * change)
    return components

def plastic_return(components, plastic, cohesion):
    for iteration in range(RETURN_ITERS):
        mean_stress = (components[0] + components[1] + components[2]) / 3.0
        deviator = [components[0] - mean_stress, components[1] - mean_stress, components[2] - mean_stress, components[3], components[4], components[5]]
        second = 0.5 * (deviator[0] * deviator[0] + deviator[1] * deviator[1] + deviator[2] * deviator[2])
        second = second + deviator[3] * deviator[3] + deviator[4] * deviator[4] + deviator[5] * deviator[5]
        shear_norm = jnp.sqrt(second)
        yield_limit = cohesion * (1.0 + plastic / (plastic + harden_scale))
        excess = jnp.maximum(shear_norm + friction * 3.0 * mean_stress - yield_limit, 0.0)
        multiplier = relax_rate * excess / (shear_mod + 9.0 * bulk_mod * friction * friction + harden_mod)
        shrink = jnp.maximum(1.0 - shear_mod * multiplier / jnp.maximum(shear_norm, tau_floor), 0.0)
        mean_stress = mean_stress - 3.0 * bulk_mod * friction * multiplier
        components = [deviator[0] * shrink + mean_stress, deviator[1] * shrink + mean_stress, deviator[2] * shrink + mean_stress, deviator[3] * shrink, deviator[4] * shrink, deviator[5] * shrink]
        plastic = plastic + multiplier
    return (jnp.stack(components, axis=-2), plastic)

def device_sums(sources, places, block_pairs, pair_count, send_lists, cross_links, depth_sources, depth_places, strip_sources, strip_places):
    slot_index = jnp.arange(block_pairs.shape[0], dtype=jnp.int32)
    row_block = block_pairs[:, 0]
    col_block = block_pairs[:, 1]
    weight = jnp.where(slot_index < pair_count, jnp.where(row_block == col_block, 0.5, 1.0), 0.0).astype(jnp.float32)
    to_rows, to_cols = tile_terms(sources[row_block], places[row_block], sources[col_block], places[col_block], weight)
    summed = jnp.zeros(sources.shape, jnp.float32).at[row_block].add(to_rows).at[col_block].add(to_cols)
    returned = []
    for face_index, far_sources, far_places in ((0, depth_sources, depth_places), (1, strip_sources, strip_places)):
        own_blocks = send_lists[2 * face_index][cross_links[face_index, :, 0]]
        far_slots = cross_links[face_index, :, 1]
        unit_weight = jnp.ones(far_slots.shape, jnp.float32)
        to_rows, to_cols = tile_terms(sources[own_blocks], places[own_blocks], far_sources[far_slots], far_places[far_slots], unit_weight)
        summed = summed.at[own_blocks].add(to_rows)
        returned.append(jnp.zeros(far_sources.shape, jnp.float32).at[far_slots].add(to_cols))
    return (summed, returned[0], returned[1])

def take_rows(table_in, index_list):
    return table_in[index_list]

def add_rows(table_in, index_list, extra):
    return table_in.at[index_list].add(extra)

def flatten_devices(values_in):
    return values_in.reshape((N_STRIP * N_DEPTH,) + values_in.shape[2:])

def unflatten_devices(values_in):
    return values_in.reshape((N_STRIP, N_DEPTH) + values_in.shape[1:])

def reference(position, velocity, stress, plastic, particle_mass, density, cohesion, counts, block_pairs, pair_count, send_lists, cross_links, contact):
    places = jnp.swapaxes(position, 2, 3)
    motion = jnp.swapaxes(velocity, 2, 3)
    stress_blocks = jnp.swapaxes(stress, 2, 3)
    occupied = (jnp.arange(PARTICLES, dtype=jnp.int32)[None, None, None, :] < counts[..., None]).astype(jnp.float32)
    contact_flag = lax.optimization_barrier(jnp.sum((contact[..., :, None] == jnp.arange(BLOCKS, dtype=jnp.int32)).astype(jnp.float32), axis=-2))[..., None]
    take_rim = jax.vmap(jax.vmap(take_rows))
    add_rim = jax.vmap(jax.vmap(add_rows))
    depth_keep = (jnp.arange(N_DEPTH) < N_DEPTH - 1).astype(jnp.float32)[None, :, None, None, None]
    depth_first = (jnp.arange(N_DEPTH) > 0).astype(jnp.float32)[None, :, None, None, None]

    def interact(cur_places, cur_motion, cur_stress):
        sources = source_rows(cur_places, cur_motion, cur_stress, particle_mass, density, occupied)
        depth_sources = jnp.roll(take_rim(sources, send_lists[:, :, 1]), -1, axis=1) * depth_keep
        depth_places = jnp.roll(take_rim(cur_places, send_lists[:, :, 1]), -1, axis=1) * depth_keep
        strip_sources = jnp.roll(take_rim(sources, send_lists[:, :, 3]), -1, axis=0)
        strip_places = jnp.roll(take_rim(cur_places, send_lists[:, :, 3]), -1, axis=0)

        def device_step(device_items):
            return device_sums(*device_items)
        gathered = tuple((flatten_devices(values_in) for values_in in (sources, cur_places, block_pairs, pair_count, send_lists, cross_links, depth_sources, depth_places, strip_sources, strip_places)))
        summed, back_depth, back_strip = lax.map(device_step, gathered)
        summed = unflatten_devices(summed)
        back_depth = jnp.roll(unflatten_devices(back_depth), 1, axis=1) * depth_first
        back_strip = jnp.roll(unflatten_devices(back_strip), 1, axis=0)
        summed = add_rim(summed, send_lists[:, :, 1], back_depth)
        summed = add_rim(summed, send_lists[:, :, 3], back_strip)
        return summed
    summed = interact(places, motion, stress_blocks)
    acceleration, strain = section_rates(summed, places, motion, stress_blocks, density, contact_flag)
    half_motion = motion + 0.5 * time_step * acceleration
    half_places = places + 0.5 * time_step * motion
    half_stress = plastic_return(elastic_step(stress_blocks, strain, 0.5), plastic, cohesion)[0]
    summed = interact(half_places, half_motion, half_stress)
    acceleration, strain = section_rates(summed, half_places, half_motion, half_stress, density, contact_flag)
    new_motion = motion + time_step * acceleration
    new_places = places + time_step * half_motion
    new_stress, new_plastic = plastic_return(elastic_step(stress_blocks, strain, 1.0), plastic, cohesion)
    particle_keep = occupied[..., None, :]
    return (jnp.swapaxes(new_places * particle_keep, 2, 3), jnp.swapaxes(new_motion * particle_keep, 2, 3), jnp.swapaxes(new_stress * particle_keep, 2, 3), new_plastic * occupied)
```

```python
import functools

import jax
import jax.numpy as jnp
from jax import lax
from jax.experimental import pallas as pl
from jax.experimental.pallas import tpu as pltpu
from jax.sharding import PartitionSpec as P

RETURN_ITERS = 4
ROWS = 16
GROUP = 16

smooth_len = 1.5
kernel_coef = -105.0 / (3.141592653589793 * 1.5**5)
time_step = 0.25
gravity = 1.0
spin_rate = 2.0
blade_stiff = 4.0
bulk_mod = 2.0
shear_mod = 1.5
friction = 0.25
harden_scale = 0.05
harden_mod = 0.5
relax_rate = 0.7
tau_floor = 0.5
voigt_index = ((0, 3, 5), (3, 1, 4), (5, 4, 2))
voigt_pairs = ((0, 0), (1, 1), (2, 2), (0, 1), (1, 2), (0, 2))
bf16 = jnp.bfloat16
f32 = jnp.float32


def by_axis(value, axis, steps, closed):
    count = lax.axis_size(axis)
    pairs = [(i, (i + steps) % count) for i in range(count)]
    if not closed:
        pairs = [(i, j) for i, j in pairs if j == i + steps]
    return lax.ppermute(value, axis, pairs)


def halves(value):
    high = value.astype(bf16).astype(f32)
    return high, value - high


def source_rows(row):
    places = [row(k) for k in range(3)]
    motion = [row(3 + k) for k in range(3)]
    scaled = [row(6 + k) for k in range(6)]
    mass, volume = row(12), row(13)
    out = [mass]
    out += [mass * x for x in places]
    out += [mass * s for s in scaled]
    for k in range(3):
        dotted = scaled[voigt_index[k][0]] * places[0]
        dotted = dotted + scaled[voigt_index[k][1]] * places[1]
        dotted = dotted + scaled[voigt_index[k][2]] * places[2]
        out.append(mass * dotted)
    out.append(volume)
    out += [volume * v for v in motion]
    out += [volume * x for x in places]
    for a, b in voigt_pairs:
        out.append(volume * (0.5 * (motion[a] * places[b] + motion[b] * places[a])))
    return out


def distance_rows(row):
    places = [row(k) * (1.0 / smooth_len) for k in range(3)]
    square = places[0] * places[0] + places[1] * places[1] + places[2] * places[2]
    high, low = zip(*[halves(x) for x in places])
    n0, rest = halves(square)
    n1, n2 = halves(rest)
    one = jnp.ones_like(square)
    zero = jnp.zeros_like(square)
    from_side = [-2.0 * x for x in high + low + high] + [n0, n1, n2, one, one, one, zero]
    to_side = list(high + high + low) + [one, one, one, n0, n1, n2, zero]
    return from_side, to_side


def build_tables(row, base, count, src32, far32, S_ref, A_ref, to32, B_ref):
    for f, value in enumerate(source_rows(row)):
        src32[pl.ds(base * 32 + f, count, stride=32), :] = value
    from_side, to_side = distance_rows(row)
    for f, value in enumerate(from_side):
        far32[pl.ds(base * 16 + f, count, stride=16), :] = value
    if B_ref is not None:
        for f, value in enumerate(to_side):
            to32[pl.ds(base * 16 + f, count, stride=16), :] = value


def finish_tables(total, src32, far32, S_ref, A_ref, to32, B_ref):
    unroll = 4

    def some(i, carry):
        for u in range(unroll):
            b = i * unroll + u
            value = src32[pl.ds(pl.multiple_of(b * 32, 32), 32), :]
            high = value.astype(bf16)
            S_ref[b, 0:32, :] = high
            S_ref[b, 32:64, :] = (value - high.astype(f32)).astype(bf16)
            A_ref[b] = far32[pl.ds(pl.multiple_of(b * 16, 16), 16), :].T.astype(bf16)
            if B_ref is not None:
                B_ref[b] = to32[pl.ds(pl.multiple_of(b * 16, 16), 16), :].astype(bf16)
        return carry

    lax.fori_loop(0, total // unroll, some, 0)


def closeness_cubed(square):
    square = jnp.maximum(square, 1e-30)
    close = jnp.maximum(1.0 - square * lax.rsqrt(square), 0.0)
    return close * close * close


def tile_loop(item, groups, S_ref, A_ref, B_ref, acc_ref):
    def one_group(g, carry):
        outs = []
        for u in range(GROUP):
            target, source = item(g, u)
            square = jnp.dot(A_ref[source], B_ref[target[0]], preferred_element_type=f32)
            kernel = closeness_cubed(square)
            high = kernel.astype(bf16)
            low = (kernel - high.astype(f32)).astype(bf16)
            rows = S_ref[source]
            both = jnp.dot(
                jnp.concatenate([rows, rows], 1),
                jnp.concatenate([high, low], 0),
                preferred_element_type=f32,
            )
            outs.append((target[1], both[:32] + both[32:]))
        for target, value in outs:
            acc_ref[target] += value
        return carry

    lax.fori_loop(0, groups, one_group, 0)


def lanes_to_column(values):
    n = values.shape[1]
    rows = lax.broadcasted_iota(jnp.int32, (n, n), 0)
    cols = lax.broadcasted_iota(jnp.int32, (n, n), 1)
    return jnp.sum(jnp.where(rows == cols, values, 0.0), axis=1, keepdims=True)


def gather_rims(send_ref, state_ref, msgs):
    for face in range(4):
        for slot in range(16):
            block = send_ref[face, slot]
            msgs[face][pl.ds(slot, ROWS, stride=16), :] = state_ref[
                pl.ds(block, ROWS, stride=32), :
            ]


def start_kernel(send_ref, counts_ref, pos_ref, vel_ref, sig_ref, mass_ref, dens_ref, state_ref, *msgs):
    column = lanes_to_column(counts_ref[...].astype(f32))
    lane = lax.broadcasted_iota(jnp.int32, (32, 128), 1).astype(f32)
    mass = jnp.where(lane < column, mass_ref[...], 0.0)
    dens = dens_ref[...]
    state_ref[0:96, :] = pos_ref[...]
    state_ref[96:192, :] = vel_ref[...]
    square = dens * dens
    for k in range(6):
        state_ref[192 + 32 * k : 224 + 32 * k, :] = sig_ref[32 * k : 32 * k + 32, :] / square
    state_ref[384:416, :] = mass
    state_ref[416:448, :] = mass / dens
    state_ref[448:512, :] = jnp.zeros((64, 128), f32)
    gather_rims(send_ref, state_ref, msgs)


def own_kernel(count_ref, pairs_ref, state_ref, acc_ref, B_ref, S_ref, A_ref, src32, far32, to32, acc33):
    def row(k):
        return state_ref[32 * k : 32 * k + 32, :]

    build_tables(row, 0, 32, src32, far32, S_ref, A_ref, to32, B_ref)
    finish_tables(32, src32, far32, S_ref, A_ref, to32, B_ref)
    acc33[...] = jnp.zeros_like(acc33)
    total = count_ref[0]

    def item(g, u):
        q = g * (GROUP // 2) + u // 2
        a = pairs_ref[q, 0]
        b = pairs_ref[q, 1]
        live = q < total
        if u % 2 == 0:
            return (a, jnp.where(live, a, 32)), b
        return (b, jnp.where(jnp.logical_and(live, a != b), b, 32)), a

    groups = (total + GROUP // 2 - 1) // (GROUP // 2)
    tile_loop(item, groups, S_ref, A_ref, B_ref, acc33)
    acc_ref[...] = acc33[0:32]


def cross_terms(send_ref, link_ref, back_depth, back_strip, msgs, B_ref, S_ref, A_ref, src32, far32, acc):
    for face in range(4):
        def row(k, face=face):
            return msgs[face][16 * k : 16 * k + 16, :]

        build_tables(row, 16 * face, 16, src32, far32, S_ref, A_ref, None, None)
    finish_tables(64, src32, far32, S_ref, A_ref, None, None)
    acc[...] = jnp.zeros_like(acc)

    def item(g, u):
        q = g * (GROUP // 4) + u // 4
        if u % 4 == 0:
            target = send_ref[0, link_ref[0, q, 0]]
            source = link_ref[0, q, 1]
        elif u % 4 == 1:
            target = send_ref[1, back_depth[q, 1]]
            source = 16 + back_depth[q, 0]
        elif u % 4 == 2:
            target = send_ref[2, link_ref[1, q, 0]]
            source = 32 + link_ref[1, q, 1]
        else:
            target = send_ref[3, back_strip[q, 1]]
            source = 48 + back_strip[q, 0]
        return (target, target), source

    tile_loop(item, 48 // (GROUP // 4), S_ref, A_ref, B_ref, acc)


def rates(state_ref, own_acc, acc, flag, c):
    def total(f):
        at = pl.ds(8 * c * 32 + f, 8, stride=32)
        return kernel_coef * (own_acc[at, :] + acc[at, :])

    def row(k):
        return state_ref[32 * k + 8 * c : 32 * k + 8 * c + 8, :]

    places = [row(k) for k in range(3)]
    motion = [row(3 + k) for k in range(3)]
    scaled = [row(6 + k) for k in range(6)]
    blade = (spin_rate * places[2], jnp.zeros_like(places[1]), -spin_rate * places[0])
    mass_sum = total(0)
    lever = [places[l] * mass_sum - total(1 + l) for l in range(3)]
    stress_sum = [total(4 + s) for s in range(6)]
    acceleration = []
    for k in range(3):
        force = jnp.zeros_like(mass_sum)
        for l in range(3):
            slot = voigt_index[k][l]
            force = force + scaled[slot] * lever[l]
            force = force + places[l] * stress_sum[slot]
        force = force - total(10 + k)
        force = force + blade_stiff * flag * (blade[k] - motion[k])
        if k == 2:
            force = force - gravity
        acceleration.append(force)
    volume_sum = total(13)
    motion_sum = [total(14 + k) for k in range(3)]
    place_sum = [total(17 + k) for k in range(3)]
    strain = []
    for comp, (a, b) in enumerate(voigt_pairs):
        rate = 0.5 * (places[b] * motion_sum[a] + places[a] * motion_sum[b])
        rate = rate - total(20 + comp)
        rate = rate - 0.5 * volume_sum * (motion[a] * places[b] + motion[b] * places[a])
        rate = rate + 0.5 * (motion[a] * place_sum[b] + motion[b] * place_sum[a])
        strain.append(rate)
    return acceleration, strain


def elastic_step(stress, strain, fraction):
    volumetric = strain[0] + strain[1] + strain[2]
    lame_first = bulk_mod - 2.0 * shear_mod / 3.0
    components = []
    for comp in range(6):
        change = 2.0 * shear_mod * strain[comp]
        if comp < 3:
            change = change + lame_first * volumetric
        components.append(stress[comp] + fraction * time_step * change)
    return components


def plastic_return(components, plastic, cohesion):
    for _ in range(RETURN_ITERS):
        mean = (components[0] + components[1] + components[2]) / 3.0
        dev = [components[k] - mean for k in range(3)] + list(components[3:])
        second = 0.5 * (dev[0] * dev[0] + dev[1] * dev[1] + dev[2] * dev[2])
        second = second + dev[3] * dev[3] + dev[4] * dev[4] + dev[5] * dev[5]
        shear = jnp.sqrt(second)
        limit = cohesion * (1.0 + plastic / (plastic + harden_scale))
        excess = jnp.maximum(shear + friction * 3.0 * mean - limit, 0.0)
        multiplier = (relax_rate / (shear_mod + 9.0 * bulk_mod * friction * friction + harden_mod)) * excess
        shrink = jnp.maximum(1.0 - shear_mod * multiplier / jnp.maximum(shear, tau_floor), 0.0)
        mean = mean - 3.0 * bulk_mod * friction * multiplier
        components = [dev[k] * shrink + mean for k in range(3)] + [dev[k] * shrink for k in range(3, 6)]
        plastic = plastic + multiplier
    return components, plastic


def contact_column(contact_ref):
    rows = lax.broadcasted_iota(jnp.int32, (32, 16), 0)
    hit = jnp.where(contact_ref[...] == rows, 1.0, 0.0)
    return jnp.sum(hit, axis=1, keepdims=True)


def half_kernel(
    send_ref, link_ref, back_depth, back_strip, contact_ref, state_ref, own_acc, B_ref,
    m0, m1, m2, m3, sig_ref, plastic_ref, cohesion_ref, dens_ref,
    next_ref, n0, n1, n2, n3, S_ref, A_ref, src32, far32, acc,
):
    cross_terms(send_ref, link_ref, back_depth, back_strip, (m0, m1, m2, m3), B_ref, S_ref, A_ref, src32, far32, acc)
    flags = contact_column(contact_ref)
    own2 = own_acc.reshape(1024, 128)
    acc2 = acc.reshape(1024, 128)
    for c in range(4):
        at = slice(8 * c, 8 * c + 8)
        acceleration, strain = rates(state_ref, own2, acc2, flags[at], c)
        stress = [sig_ref[32 * k + 8 * c : 32 * k + 8 * c + 8, :] for k in range(6)]
        trial = elastic_step(stress, strain, 0.5)
        half_stress, _ = plastic_return(trial, plastic_ref[at, :], cohesion_ref[at, :])
        dens = dens_ref[at, :]
        square = dens * dens
        for k in range(3):
            x = slice(32 * k + 8 * c, 32 * k + 8 * c + 8)
            v = slice(96 + 32 * k + 8 * c, 96 + 32 * k + 8 * c + 8)
            motion = state_ref[v, :]
            next_ref[x, :] = state_ref[x, :] + 0.5 * time_step * motion
            next_ref[v, :] = motion + 0.5 * time_step * acceleration[k]
        for k in range(6):
            next_ref[192 + 32 * k + 8 * c : 200 + 32 * k + 8 * c, :] = half_stress[k] / square
    next_ref[384:512, :] = state_ref[384:512, :]
    gather_rims(send_ref, next_ref, (n0, n1, n2, n3))


def last_kernel(
    send_ref, link_ref, back_depth, back_strip, contact_ref, counts_ref, state_ref, own_acc, B_ref,
    m0, m1, m2, m3, sig_ref, plastic_ref, cohesion_ref, pos_ref, vel_ref,
    pos_out, vel_out, sig_out, plastic_out, S_ref, A_ref, src32, far32, acc,
):
    cross_terms(send_ref, link_ref, back_depth, back_strip, (m0, m1, m2, m3), B_ref, S_ref, A_ref, src32, far32, acc)
    flags = contact_column(contact_ref)
    column = lanes_to_column(counts_ref[...].astype(f32))
    lane = lax.broadcasted_iota(jnp.int32, (8, 128), 1).astype(f32)
    own2 = own_acc.reshape(1024, 128)
    acc2 = acc.reshape(1024, 128)
    for c in range(4):
        at = slice(8 * c, 8 * c + 8)
        keep = lane < column[at]
        acceleration, strain = rates(state_ref, own2, acc2, flags[at], c)
        stress = [sig_ref[32 * k + 8 * c : 32 * k + 8 * c + 8, :] for k in range(6)]
        trial = elastic_step(stress, strain, 1.0)
        new_stress, new_plastic = plastic_return(trial, plastic_ref[at, :], cohesion_ref[at, :])
        for k in range(3):
            x = slice(32 * k + 8 * c, 32 * k + 8 * c + 8)
            v = slice(96 + 32 * k + 8 * c, 96 + 32 * k + 8 * c + 8)
            pos_out[x, :] = jnp.where(keep, pos_ref[x, :] + time_step * state_ref[v, :], 0.0)
            vel_out[x, :] = jnp.where(keep, vel_ref[x, :] + time_step * acceleration[k], 0.0)
        for k in range(6):
            sig_out[32 * k + 8 * c : 32 * k + 8 * c + 8, :] = jnp.where(keep, new_stress[k], 0.0)
        plastic_out[at, :] = jnp.where(keep, new_plastic, 0.0)


SMEM = pl.BlockSpec(memory_space=pltpu.SMEM)
VMEM = pl.BlockSpec(memory_space=pltpu.VMEM)
params = pltpu.CompilerParams(vmem_limit_bytes=48 * 1024 * 1024)


def shape(*dims, dtype=f32):
    return jax.ShapeDtypeStruct(dims, dtype)


def tables(count):
    return [
        pltpu.VMEM((count, 64, 128), bf16),
        pltpu.VMEM((count, 128, 16), bf16),
        pltpu.VMEM((count * 32, 128), f32),
        pltpu.VMEM((count * 16, 128), f32),
    ]


def call(kernel, smem, vmem, outs, scratch):
    return pl.pallas_call(
        kernel,
        out_shape=outs,
        in_specs=[SMEM] * len(smem) + [VMEM] * len(vmem),
        out_specs=[VMEM] * len(outs),
        scratch_shapes=scratch,
        compiler_params=params,
    )(*smem, *vmem)


def shards(
    position, velocity, stress, plastic, particle_mass, density, cohesion,
    counts, block_pairs, pair_count, send_lists, cross_links, contact,
):
    pos = position.reshape(96, 128)
    vel = velocity.reshape(96, 128)
    sig = stress.reshape(192, 128)
    plastic_now = plastic.reshape(32, 128)
    mass = particle_mass.reshape(32, 128)
    dens = density.reshape(32, 128)
    cohesion_now = cohesion.reshape(32, 128)
    counts_now = counts.reshape(1, 32)
    pairs = block_pairs.reshape(128, 2)
    total = pair_count.reshape(1)
    send = send_lists.reshape(4, 16)
    links = cross_links.reshape(2, 48, 2)
    touched = contact.reshape(1, 16)

    back_depth = by_axis(links[0], "depth", 1, False)
    back_strip = by_axis(links[1], "strip", 1, True)
    rim = [shape(16 * ROWS, 128)] * 4
    state, *msgs = call(
        start_kernel, [send], [counts_now, pos, vel, sig, mass, dens], [shape(512, 128)] + rim, []
    )

    def swap(msgs):
        return (
            by_axis(msgs[1], "depth", -1, False),
            by_axis(msgs[0], "depth", 1, False),
            by_axis(msgs[3], "strip", -1, True),
            by_axis(msgs[2], "strip", 1, True),
        )

    def own(state):
        return call(
            own_kernel,
            [total, pairs],
            [state],
            [shape(32, 32, 128), shape(32, 16, 128, dtype=bf16)],
            tables(32) + [pltpu.VMEM((512, 128), f32), pltpu.VMEM((33, 32, 128), f32)],
        )

    cross_scratch = tables(64) + [pltpu.VMEM((32, 32, 128), f32)]
    far = swap(msgs)
    own_acc, to_side = own(state)
    state, *msgs = call(
        half_kernel,
        [send, links, back_depth, back_strip],
        [touched, state, own_acc, to_side, *far, sig, plastic_now, cohesion_now, dens],
        [shape(512, 128)] + rim,
        cross_scratch,
    )
    far = swap(msgs)
    own_acc, to_side = own(state)
    new_pos, new_vel, new_sig, new_plastic = call(
        last_kernel,
        [send, links, back_depth, back_strip],
        [touched, counts_now, state, own_acc, to_side, *far, sig, plastic_now, cohesion_now, pos, vel],
        [shape(96, 128), shape(96, 128), shape(192, 128), shape(32, 128)],
        cross_scratch,
    )
    return (
        new_pos.reshape(position.shape),
        new_vel.reshape(velocity.shape),
        new_sig.reshape(stress.shape),
        new_plastic.reshape(plastic.shape),
    )


def solution(mesh):
    def spec(rank):
        return P("strip", "depth", *([None] * (rank - 2)))

    return jax.shard_map(
        shards,
        mesh=mesh,
        in_specs=tuple(spec(r) for r in (5, 5, 5, 4, 4, 4, 4, 3, 4, 2, 4, 5, 3)),
        out_specs=tuple(spec(r) for r in (5, 5, 5, 4)),
        check_vma=False,
    )
```

```python
import functools

import jax
import jax.numpy as jnp
from jax import lax
from jax.experimental import pallas as pl
from jax.experimental.pallas import tpu as pltpu
from jax.sharding import PartitionSpec as P

RETURN_ITERS = 4
ROWS = 16
GROUP = 32

smooth_len = 1.5
kernel_coef = -105.0 / (3.141592653589793 * 1.5**5)
time_step = 0.25
gravity = 1.0
spin_rate = 2.0
blade_stiff = 4.0
bulk_mod = 2.0
shear_mod = 1.5
friction = 0.25
harden_scale = 0.05
harden_mod = 0.5
relax_rate = 0.7
tau_floor = 0.5
voigt_index = ((0, 3, 5), (3, 1, 4), (5, 4, 2))
voigt_pairs = ((0, 0), (1, 1), (2, 2), (0, 1), (1, 2), (0, 2))
bf16 = jnp.bfloat16
f32 = jnp.float32


def by_axis(value, axis, steps, closed):
    count = lax.axis_size(axis)
    pairs = [(i, (i + steps) % count) for i in range(count)]
    if not closed:
        pairs = [(i, j) for i, j in pairs if j == i + steps]
    return lax.ppermute(value, axis, pairs)


def halves(value):
    high = value.astype(bf16).astype(f32)
    return high, value - high


def source_rows(row):
    places = [row(k) for k in range(3)]
    motion = [row(3 + k) for k in range(3)]
    scaled = [row(6 + k) for k in range(6)]
    mass, volume = row(12), row(13)
    out = [mass]
    out += [mass * x for x in places]
    out += [mass * s for s in scaled]
    for k in range(3):
        dotted = scaled[voigt_index[k][0]] * places[0]
        dotted = dotted + scaled[voigt_index[k][1]] * places[1]
        dotted = dotted + scaled[voigt_index[k][2]] * places[2]
        out.append(mass * dotted)
    out.append(volume)
    out += [volume * v for v in motion]
    out += [volume * x for x in places]
    for a, b in voigt_pairs:
        out.append(volume * (0.5 * (motion[a] * places[b] + motion[b] * places[a])))
    return out


def distance_rows(row):
    places = [row(k) * (1.0 / smooth_len) for k in range(3)]
    square = places[0] * places[0] + places[1] * places[1] + places[2] * places[2]
    high, low = zip(*[halves(x) for x in places])
    n0, rest = halves(square)
    n1, n2 = halves(rest)
    one = jnp.ones_like(square)
    zero = jnp.zeros_like(square)
    from_side = [-2.0 * x for x in high + low + high] + [n0, n1, n2, one, one, one, zero]
    to_side = list(high + high + low) + [one, one, one, n0, n1, n2, zero]
    return from_side, to_side


def fill_rows(row, base, count, src32, far32, to32):
    for f, value in enumerate(source_rows(row)):
        src32[pl.ds(base * 32 + f, count, stride=32), :] = value
    from_side, to_side = distance_rows(row)
    for f, value in enumerate(from_side):
        far32[pl.ds(base * 16 + f, count, stride=16), :] = value
    if to32 is not None:
        for f, value in enumerate(to_side):
            to32[pl.ds(base * 16 + f, count, stride=16), :] = value


def finish_tables(count, src32, far32, S_ref, A_ref):
    def eight(i, carry):
        flipped = far32[pl.ds(pl.multiple_of(i * 128, 128), 128), :].T
        A_ref[i] = flipped.astype(bf16)
        for u in range(8):
            b = i * 8 + u
            value = src32[pl.ds(pl.multiple_of(b * 32, 32), 32), :]
            high = value.astype(bf16)
            S_ref[b, 0:32, :] = high
            S_ref[b, 32:64, :] = (value - high.astype(f32)).astype(bf16)
        return carry

    lax.fori_loop(0, count // 8, eight, 0)


def pad_targets(B_ref, rows_of):
    def one(b, carry):
        B_ref[b, 0:112, :] = jnp.zeros((112, 128), bf16)
        B_ref[b, 128:240, :] = jnp.zeros((112, 128), bf16)
        B_ref[b, 112:128, :] = rows_of(b)
        return carry

    lax.fori_loop(0, 32, one, 0)


def closeness_cubed(square):
    square = jnp.maximum(square, 1e-30)
    close = jnp.maximum(1.0 - square * lax.rsqrt(square), 0.0)
    return close * close * close


def tile_loop(item, groups, S_ref, A_ref, B_ref, acc_ref):
    def one_group(g, carry):
        outs = []
        for u in range(GROUP):
            target, source = item(g, u)
            start = pl.multiple_of(112 - 16 * lax.rem(source, 8), 16)
            square = jnp.dot(
                A_ref[lax.div(source, 8)],
                B_ref[target[0], pl.ds(start, 128), :],
                preferred_element_type=f32,
            )
            kernel = closeness_cubed(square)
            high = kernel.astype(bf16)
            low = (kernel - high.astype(f32)).astype(bf16)
            rows = S_ref[source]
            both = jnp.dot(
                jnp.concatenate([rows, rows], 1),
                jnp.concatenate([high, low], 0),
                preferred_element_type=f32,
            )
            outs.append((target[1], both[:32] + both[32:]))
        for target, value in outs:
            acc_ref[target] += value
        return carry

    lax.fori_loop(0, groups, one_group, 0)


def lanes_to_column(values):
    n = values.shape[1]
    rows = lax.broadcasted_iota(jnp.int32, (n, n), 0)
    cols = lax.broadcasted_iota(jnp.int32, (n, n), 1)
    return jnp.sum(jnp.where(rows == cols, values, 0.0), axis=1, keepdims=True)


def gather_rims(send_ref, state_ref, msgs):
    for face in range(4):
        for slot in range(16):
            block = send_ref[face, slot]
            msgs[face][pl.ds(slot, ROWS, stride=16), :] = state_ref[
                pl.ds(block, ROWS, stride=32), :
            ]


def fetch(pairs, sem):
    copies = [pltpu.make_async_copy(a, b, sem.at[i]) for i, (a, b) in enumerate(pairs)]
    for copy in copies:
        copy.start()
    return copies


def start_kernel(
    send_hbm, counts_ref, links_ref, pos_hbm, vel_hbm, sig_hbm, mass_hbm, dens_hbm,
    state_ref, m0, m1, m2, m3, send_ref, sig_ref, mass_ref, dens_ref, sem,
):
    copies = fetch(
        [
            (send_hbm, send_ref),
            (pos_hbm, state_ref.at[0:96]),
            (vel_hbm, state_ref.at[96:192]),
            (sig_hbm, sig_ref),
            (mass_hbm, mass_ref),
            (dens_hbm, dens_ref),
        ],
        sem,
    )
    column = lanes_to_column(counts_ref[...].astype(f32))
    lane = lax.broadcasted_iota(jnp.int32, (32, 128), 1).astype(f32)
    for copy in copies:
        copy.wait()
    mass = jnp.where(lane < column, mass_ref[...], 0.0)
    dens = dens_ref[...]
    square = dens * dens
    for k in range(6):
        state_ref[192 + 32 * k : 224 + 32 * k, :] = sig_ref[32 * k : 32 * k + 32, :] / square
    state_ref[384:416, :] = mass
    state_ref[416:448, :] = mass / dens
    state_ref[448:512, :] = jnp.zeros((64, 128), f32)
    gather_rims(send_ref, state_ref, (m0, m1, m2, m3))
    m0[224:232, :] = links_ref[...]
    m2[224:232, :] = links_ref[...]


def own_kernel(count_ref, pairs_ref, state_ref, acc_ref, to_ref, S_ref, A_ref, B_ref, src32, far32, to32, acc33):
    def row(k):
        return state_ref[32 * k : 32 * k + 32, :]

    fill_rows(row, 0, 32, src32, far32, to32)
    finish_tables(32, src32, far32, S_ref, A_ref)

    def rows_of(b):
        rows = to32[pl.ds(pl.multiple_of(b * 16, 16), 16), :].astype(bf16)
        to_ref[b] = rows
        return rows

    pad_targets(B_ref, rows_of)
    acc33[...] = jnp.zeros_like(acc33)
    total = count_ref[0]

    def item(g, u):
        q = g * (GROUP // 2) + u // 2
        a = pairs_ref[q, 0]
        b = pairs_ref[q, 1]
        live = q < total
        if u % 2 == 0:
            return (a, jnp.where(live, a, 32)), b
        return (b, jnp.where(jnp.logical_and(live, a != b), b, 32)), a

    groups = (total + GROUP // 2 - 1) // (GROUP // 2)
    tile_loop(item, groups, S_ref, A_ref, B_ref, acc33)
    acc_ref[...] = acc33[0:32]


def cross_terms(send_ref, link_ref, back_ref, msgs, to_ref, S_ref, A_ref, B_ref, src32, far32, acc, ready):
    for face in range(4):
        def row(k, face=face):
            return msgs[face][16 * k : 16 * k + 16, :]

        fill_rows(row, 16 * face, 16, src32, far32, None)
    finish_tables(64, src32, far32, S_ref, A_ref)
    pad_targets(B_ref, lambda b: to_ref[b])
    acc[...] = jnp.zeros_like(acc)
    ready()

    def item(g, u):
        q = g * (GROUP // 4) + u // 4
        if u % 4 == 0:
            target = send_ref[0, link_ref[0, q]]
            source = link_ref[1, q]
        elif u % 4 == 1:
            target = send_ref[1, back_ref[1, q]]
            source = 16 + back_ref[0, q]
        elif u % 4 == 2:
            target = send_ref[2, link_ref[2, q]]
            source = 32 + link_ref[3, q]
        else:
            target = send_ref[3, back_ref[11, q]]
            source = 48 + back_ref[10, q]
        return (target, target), source

    tile_loop(item, 48 // (GROUP // 4), S_ref, A_ref, B_ref, acc)


def rates(state_ref, own_acc, acc, flag, c):
    def total(f):
        at = pl.ds(8 * c * 32 + f, 8, stride=32)
        return kernel_coef * (own_acc[at, :] + acc[at, :])

    def row(k):
        return state_ref[32 * k + 8 * c : 32 * k + 8 * c + 8, :]

    places = [row(k) for k in range(3)]
    motion = [row(3 + k) for k in range(3)]
    scaled = [row(6 + k) for k in range(6)]
    blade = (spin_rate * places[2], jnp.zeros_like(places[1]), -spin_rate * places[0])
    mass_sum = total(0)
    lever = [places[l] * mass_sum - total(1 + l) for l in range(3)]
    stress_sum = [total(4 + s) for s in range(6)]
    acceleration = []
    for k in range(3):
        force = jnp.zeros_like(mass_sum)
        for l in range(3):
            slot = voigt_index[k][l]
            force = force + scaled[slot] * lever[l]
            force = force + places[l] * stress_sum[slot]
        force = force - total(10 + k)
        force = force + blade_stiff * flag * (blade[k] - motion[k])
        if k == 2:
            force = force - gravity
        acceleration.append(force)
    volume_sum = total(13)
    motion_sum = [total(14 + k) for k in range(3)]
    place_sum = [total(17 + k) for k in range(3)]
    strain = []
    for comp, (a, b) in enumerate(voigt_pairs):
        rate = 0.5 * (places[b] * motion_sum[a] + places[a] * motion_sum[b])
        rate = rate - total(20 + comp)
        rate = rate - 0.5 * volume_sum * (motion[a] * places[b] + motion[b] * places[a])
        rate = rate + 0.5 * (motion[a] * place_sum[b] + motion[b] * place_sum[a])
        strain.append(rate)
    return acceleration, strain


def elastic_step(stress, strain, fraction):
    volumetric = strain[0] + strain[1] + strain[2]
    lame_first = bulk_mod - 2.0 * shear_mod / 3.0
    components = []
    for comp in range(6):
        change = 2.0 * shear_mod * strain[comp]
        if comp < 3:
            change = change + lame_first * volumetric
        components.append(stress[comp] + fraction * time_step * change)
    return components


def plastic_return(components, plastic, cohesion):
    for _ in range(RETURN_ITERS):
        mean = (components[0] + components[1] + components[2]) / 3.0
        dev = [components[k] - mean for k in range(3)] + list(components[3:])
        second = 0.5 * (dev[0] * dev[0] + dev[1] * dev[1] + dev[2] * dev[2])
        second = second + dev[3] * dev[3] + dev[4] * dev[4] + dev[5] * dev[5]
        shear = jnp.sqrt(second)
        limit = cohesion * (1.0 + plastic / (plastic + harden_scale))
        excess = jnp.maximum(shear + friction * 3.0 * mean - limit, 0.0)
        multiplier = (relax_rate / (shear_mod + 9.0 * bulk_mod * friction * friction + harden_mod)) * excess
        shrink = jnp.maximum(1.0 - shear_mod * multiplier / jnp.maximum(shear, tau_floor), 0.0)
        mean = mean - 3.0 * bulk_mod * friction * multiplier
        components = [dev[k] * shrink + mean for k in range(3)] + [dev[k] * shrink for k in range(3, 6)]
        plastic = plastic + multiplier
    return components, plastic


def contact_column(contact_ref):
    rows = lax.broadcasted_iota(jnp.int32, (32, 16), 0)
    hit = jnp.where(contact_ref[...] == rows, 1.0, 0.0)
    return jnp.sum(hit, axis=1, keepdims=True)


def half_kernel(
    send_ref, link_ref, contact_ref, state_ref, own_acc, to_ref,
    m0, m1, m2, m3, sig_ref, plastic_ref, cohesion_ref, dens_ref,
    next_ref, n0, n1, n2, n3, back_out, S_ref, A_ref, B_ref, src32, far32, acc, back_ref, sem,
):
    back_out[0:8, :] = m1[224:232, :].astype(jnp.int32)
    back_out[8:16, :] = m3[224:232, :].astype(jnp.int32)
    copies = fetch([(back_out, back_ref)], sem)
    cross_terms(
        send_ref, link_ref, back_ref, (m0, m1, m2, m3), to_ref, S_ref, A_ref, B_ref, src32, far32, acc,
        copies[0].wait,
    )
    flags = contact_column(contact_ref)
    own2 = own_acc.reshape(1024, 128)
    acc2 = acc.reshape(1024, 128)
    for c in range(4):
        at = slice(8 * c, 8 * c + 8)
        acceleration, strain = rates(state_ref, own2, acc2, flags[at], c)
        stress = [sig_ref[32 * k + 8 * c : 32 * k + 8 * c + 8, :] for k in range(6)]
        trial = elastic_step(stress, strain, 0.5)
        half_stress, _ = plastic_return(trial, plastic_ref[at, :], cohesion_ref[at, :])
        dens = dens_ref[at, :]
        square = dens * dens
        for k in range(3):
            x = slice(32 * k + 8 * c, 32 * k + 8 * c + 8)
            v = slice(96 + 32 * k + 8 * c, 96 + 32 * k + 8 * c + 8)
            motion = state_ref[v, :]
            next_ref[x, :] = state_ref[x, :] + 0.5 * time_step * motion
            next_ref[v, :] = motion + 0.5 * time_step * acceleration[k]
        for k in range(6):
            next_ref[192 + 32 * k + 8 * c : 200 + 32 * k + 8 * c, :] = half_stress[k] / square
    next_ref[384:512, :] = state_ref[384:512, :]
    gather_rims(send_ref, next_ref, (n0, n1, n2, n3))


def last_kernel(
    send_ref, link_ref, back_ref, contact_ref, counts_ref, state_ref, own_acc, to_ref,
    m0, m1, m2, m3, sig_ref, plastic_ref, cohesion_ref, pos_ref, vel_ref,
    pos_out, vel_out, sig_out, plastic_out, S_ref, A_ref, B_ref, src32, far32, acc,
):
    cross_terms(
        send_ref, link_ref, back_ref, (m0, m1, m2, m3), to_ref, S_ref, A_ref, B_ref, src32, far32, acc,
        lambda: None,
    )
    flags = contact_column(contact_ref)
    column = lanes_to_column(counts_ref[...].astype(f32))
    lane = lax.broadcasted_iota(jnp.int32, (8, 128), 1).astype(f32)
    own2 = own_acc.reshape(1024, 128)
    acc2 = acc.reshape(1024, 128)
    for c in range(4):
        at = slice(8 * c, 8 * c + 8)
        keep = lane < column[at]
        acceleration, strain = rates(state_ref, own2, acc2, flags[at], c)
        stress = [sig_ref[32 * k + 8 * c : 32 * k + 8 * c + 8, :] for k in range(6)]
        trial = elastic_step(stress, strain, 1.0)
        new_stress, new_plastic = plastic_return(trial, plastic_ref[at, :], cohesion_ref[at, :])
        for k in range(3):
            x = slice(32 * k + 8 * c, 32 * k + 8 * c + 8)
            v = slice(96 + 32 * k + 8 * c, 96 + 32 * k + 8 * c + 8)
            pos_out[x, :] = jnp.where(keep, pos_ref[x, :] + time_step * state_ref[v, :], 0.0)
            vel_out[x, :] = jnp.where(keep, vel_ref[x, :] + time_step * acceleration[k], 0.0)
        for k in range(6):
            sig_out[32 * k + 8 * c : 32 * k + 8 * c + 8, :] = jnp.where(keep, new_stress[k], 0.0)
        plastic_out[at, :] = jnp.where(keep, new_plastic, 0.0)


SMEM = pl.BlockSpec(memory_space=pltpu.SMEM)
VMEM = pl.BlockSpec(memory_space=pltpu.VMEM)
HBM = pl.BlockSpec(memory_space=pl.ANY)
params = pltpu.CompilerParams(vmem_limit_bytes=48 * 1024 * 1024)


def shape(*dims, dtype=f32):
    return jax.ShapeDtypeStruct(dims, dtype)


def tables(count):
    return [
        pltpu.VMEM((count, 64, 128), bf16),
        pltpu.VMEM((count // 8, 128, 128), bf16),
        pltpu.VMEM((32, 240, 128), bf16),
        pltpu.VMEM((count * 32, 128), f32),
        pltpu.VMEM((count * 16, 128), f32),
    ]


def call(kernel, smem, vmem, hbm, outs, scratch):
    return pl.pallas_call(
        kernel,
        out_shape=outs,
        in_specs=[SMEM] * len(smem) + [VMEM] * len(vmem) + [HBM] * len(hbm),
        out_specs=[VMEM] * len(outs),
        scratch_shapes=scratch,
        compiler_params=params,
    )(*smem, *vmem, *hbm)


def shards(
    position, velocity, stress, plastic, particle_mass, density, cohesion,
    counts, block_pairs, pair_count, send_lists, cross_links, contact,
):
    pos = position.reshape(96, 128)
    vel = velocity.reshape(96, 128)
    sig = stress.reshape(192, 128)
    plastic_now = plastic.reshape(32, 128)
    mass = particle_mass.reshape(32, 128)
    dens = density.reshape(32, 128)
    cohesion_now = cohesion.reshape(32, 128)
    counts_now = counts.reshape(1, 32)
    pairs = block_pairs.reshape(128, 2)
    total = pair_count.reshape(1)
    send = send_lists.reshape(4, 16)
    links = jnp.swapaxes(cross_links.reshape(2, 48, 2), 1, 2).reshape(4, 48)
    links_row = jnp.pad(links, ((0, 4), (0, 80))).astype(f32)
    touched = contact.reshape(1, 16)

    rim = [shape(16 * ROWS, 128)] * 4
    state, *msgs = pl.pallas_call(
        start_kernel,
        out_shape=[shape(512, 128)] + rim,
        in_specs=[HBM, VMEM, VMEM] + [HBM] * 5,
        out_specs=[VMEM] * 5,
        scratch_shapes=[
            pltpu.SMEM((4, 16), jnp.int32),
            pltpu.VMEM((192, 128), f32),
            pltpu.VMEM((32, 128), f32),
            pltpu.VMEM((32, 128), f32),
            pltpu.SemaphoreType.DMA((6,)),
        ],
        compiler_params=params,
    )(send, counts_now, links_row, pos, vel, sig, mass, dens)

    def swap(msgs):
        return (
            by_axis(msgs[1], "depth", -1, False),
            by_axis(msgs[0], "depth", 1, False),
            by_axis(msgs[3], "strip", -1, True),
            by_axis(msgs[2], "strip", 1, True),
        )

    def own(state):
        return call(
            own_kernel,
            [total, pairs],
            [state],
            [],
            [shape(32, 32, 128), shape(32, 16, 128, dtype=bf16)],
            tables(32) + [pltpu.VMEM((512, 128), f32), pltpu.VMEM((33, 32, 128), f32)],
        )

    cross_scratch = tables(64) + [pltpu.VMEM((32, 32, 128), f32)]
    far = swap(msgs)
    own_acc, to_side = own(state)
    state, *msgs, back = call(
        half_kernel,
        [send, links],
        [touched, state, own_acc, to_side, *far, sig, plastic_now, cohesion_now, dens],
        [],
        [shape(512, 128)] + rim + [shape(16, 128, dtype=jnp.int32)],
        cross_scratch + [pltpu.SMEM((16, 128), jnp.int32), pltpu.SemaphoreType.DMA((1,))],
    )
    far = swap(msgs)
    own_acc, to_side = own(state)
    new_pos, new_vel, new_sig, new_plastic = call(
        last_kernel,
        [send, links, back],
        [touched, counts_now, state, own_acc, to_side, *far, sig, plastic_now, cohesion_now, pos, vel],
        [],
        [shape(96, 128), shape(96, 128), shape(192, 128), shape(32, 128)],
        cross_scratch,
    )
    return (
        new_pos.reshape(position.shape),
        new_vel.reshape(velocity.shape),
        new_sig.reshape(stress.shape),
        new_plastic.reshape(plastic.shape),
    )


def solution(mesh):
    def spec(rank):
        return P("strip", "depth", *([None] * (rank - 2)))

    return jax.shard_map(
        shards,
        mesh=mesh,
        in_specs=tuple(spec(r) for r in (5, 5, 5, 4, 4, 4, 4, 3, 4, 2, 4, 5, 3)),
        out_specs=tuple(spec(r) for r in (5, 5, 5, 4)),
        check_vma=False,
    )
```

```python
import functools

import jax
import jax.numpy as jnp
from jax import lax
from jax.experimental import pallas as pl
from jax.experimental.pallas import tpu as pltpu
from jax.sharding import PartitionSpec as P

RETURN_ITERS = 4
ROWS = 16
GROUP = 64

smooth_len = 1.5
kernel_coef = -105.0 / (3.141592653589793 * 1.5**5)
time_step = 0.25
gravity = 1.0
spin_rate = 2.0
blade_stiff = 4.0
bulk_mod = 2.0
shear_mod = 1.5
friction = 0.25
harden_scale = 0.05
harden_mod = 0.5
relax_rate = 0.7
tau_floor = 0.5
voigt_index = ((0, 3, 5), (3, 1, 4), (5, 4, 2))
voigt_pairs = ((0, 0), (1, 1), (2, 2), (0, 1), (1, 2), (0, 2))
bf16 = jnp.bfloat16
f32 = jnp.float32


def by_axis(value, axis, steps, closed):
    count = lax.axis_size(axis)
    pairs = [(i, (i + steps) % count) for i in range(count)]
    if not closed:
        pairs = [(i, j) for i, j in pairs if j == i + steps]
    return lax.ppermute(value, axis, pairs)


def halves(value):
    high = value.astype(bf16).astype(f32)
    return high, value - high


def source_rows(row):
    places = [row(k) for k in range(3)]
    motion = [row(3 + k) for k in range(3)]
    scaled = [row(6 + k) for k in range(6)]
    mass, volume = row(12), row(13)
    out = [mass]
    out += [mass * x for x in places]
    out += [mass * s for s in scaled]
    for k in range(3):
        dotted = scaled[voigt_index[k][0]] * places[0]
        dotted = dotted + scaled[voigt_index[k][1]] * places[1]
        dotted = dotted + scaled[voigt_index[k][2]] * places[2]
        out.append(mass * dotted)
    out.append(volume)
    out += [volume * v for v in motion]
    out += [volume * x for x in places]
    for a, b in voigt_pairs:
        out.append(volume * (0.5 * (motion[a] * places[b] + motion[b] * places[a])))
    return out


def distance_rows(row):
    places = [row(k) * (1.0 / smooth_len) for k in range(3)]
    square = places[0] * places[0] + places[1] * places[1] + places[2] * places[2]
    high, low = zip(*[halves(x) for x in places])
    n0, rest = halves(square)
    n1, n2 = halves(rest)
    one = jnp.ones_like(square)
    zero = jnp.zeros_like(square)
    from_side = [-2.0 * x for x in high + low + high] + [n0, n1, n2, one, one, one, zero]
    to_side = list(high + high + low) + [one, one, one, n0, n1, n2, zero]
    return from_side, to_side


def fill_rows(row, base, count, src32, far32, to32):
    for f, value in enumerate(source_rows(row)):
        src32[pl.ds(base * 32 + f, count, stride=32), :] = value
    from_side, to_side = distance_rows(row)
    for f, value in enumerate(from_side):
        far32[pl.ds(base * 16 + f, count, stride=16), :] = value
    if to32 is not None:
        for f, value in enumerate(to_side):
            to32[pl.ds(base * 16 + f, count, stride=16), :] = value


def finish_tables(count, src32, far32, S_ref, A_ref):
    def eight(i, carry):
        flipped = far32[pl.ds(pl.multiple_of(i * 128, 128), 128), :].T
        A_ref[i] = flipped.astype(bf16)
        for u in range(8):
            b = i * 8 + u
            value = src32[pl.ds(pl.multiple_of(b * 32, 32), 32), :]
            high = value.astype(bf16)
            S_ref[b, 0:32, :] = high
            S_ref[b, 32:64, :] = (value - high.astype(f32)).astype(bf16)
        return carry

    lax.fori_loop(0, count // 8, eight, 0)


def pad_targets(B_ref, rows_of):
    def one(b, carry):
        B_ref[b, 0:112, :] = jnp.zeros((112, 128), bf16)
        B_ref[b, 128:240, :] = jnp.zeros((112, 128), bf16)
        B_ref[b, 112:128, :] = rows_of(b)
        return carry

    lax.fori_loop(0, 32, one, 0)


def closeness_cubed(square):
    square = jnp.maximum(square, 1e-30)
    close = jnp.maximum(1.0 - square * lax.rsqrt(square), 0.0)
    return close * close * close


def tile_loop(item, groups, S_ref, A_ref, B_ref, acc_ref):
    def one_group(g, carry):
        outs = []
        for u in range(GROUP):
            target, source = item(g, u)
            start = pl.multiple_of(112 - 16 * lax.rem(source, 8), 16)
            square = jnp.dot(
                A_ref[lax.div(source, 8)],
                B_ref[target[0], pl.ds(start, 128), :],
                preferred_element_type=f32,
            )
            kernel = closeness_cubed(square)
            high = kernel.astype(bf16)
            low = (kernel - high.astype(f32)).astype(bf16)
            rows = S_ref[source]
            both = jnp.dot(
                jnp.concatenate([rows, rows], 1),
                jnp.concatenate([high, low], 0),
                preferred_element_type=f32,
            )
            outs.append((target[1], both[:32] + both[32:]))
        for target, value in outs:
            acc_ref[target] += value
        return carry

    lax.fori_loop(0, groups, one_group, 0)


def lanes_to_column(values):
    n = values.shape[1]
    rows = lax.broadcasted_iota(jnp.int32, (n, n), 0)
    cols = lax.broadcasted_iota(jnp.int32, (n, n), 1)
    return jnp.sum(jnp.where(rows == cols, values, 0.0), axis=1, keepdims=True)


def gather_rims(send_ref, state_ref, msgs):
    for face in range(4):
        for slot in range(16):
            block = send_ref[face, slot]
            msgs[face][pl.ds(slot, ROWS, stride=16), :] = state_ref[
                pl.ds(block, ROWS, stride=32), :
            ]


def fetch(pairs, sem):
    copies = [pltpu.make_async_copy(a, b, sem.at[i]) for i, (a, b) in enumerate(pairs)]
    for copy in copies:
        copy.start()
    return copies


def start_kernel(
    send_hbm, counts_hbm, links_hbm, pos_hbm, vel_hbm, sig_hbm, mass_hbm, dens_hbm,
    state_ref, m0, m1, m2, m3, send_ref, counts_ref, links_ref, sig_ref, mass_ref, dens_ref, sem,
):
    copies = fetch(
        [
            (send_hbm, send_ref),
            (counts_hbm, counts_ref),
            (links_hbm, links_ref),
            (pos_hbm, state_ref.at[0:96]),
            (vel_hbm, state_ref.at[96:192]),
            (sig_hbm, sig_ref),
            (mass_hbm, mass_ref),
            (dens_hbm, dens_ref),
        ],
        sem,
    )
    for copy in copies:
        copy.wait()
    column = lanes_to_column(counts_ref[...].astype(f32))
    lane = lax.broadcasted_iota(jnp.int32, (32, 128), 1).astype(f32)
    mass = jnp.where(lane < column, mass_ref[...], 0.0)
    dens = dens_ref[...]
    square = dens * dens
    for k in range(6):
        state_ref[192 + 32 * k : 224 + 32 * k, :] = sig_ref[32 * k : 32 * k + 32, :] / square
    state_ref[384:416, :] = mass
    state_ref[416:448, :] = mass / dens
    state_ref[448:512, :] = jnp.zeros((64, 128), f32)
    gather_rims(send_ref, state_ref, (m0, m1, m2, m3))
    links = links_ref[...].astype(f32)
    m0[224:228, 0:48] = links
    m2[224:228, 0:48] = links


def own_kernel(
    count_ref, state_ref, pairs_hbm, acc_ref, to_ref,
    S_ref, A_ref, B_ref, src32, far32, to32, acc33, pairs_ref, sem,
):
    copies = fetch([(pairs_hbm, pairs_ref)], sem)

    def row(k):
        return state_ref[32 * k : 32 * k + 32, :]

    fill_rows(row, 0, 32, src32, far32, to32)
    finish_tables(32, src32, far32, S_ref, A_ref)

    def rows_of(b):
        rows = to32[pl.ds(pl.multiple_of(b * 16, 16), 16), :].astype(bf16)
        to_ref[b] = rows
        return rows

    pad_targets(B_ref, rows_of)
    acc33[...] = jnp.zeros_like(acc33)
    total = count_ref[0]
    copies[0].wait()

    def item(g, u):
        q = g * (GROUP // 2) + u // 2
        a = pairs_ref[0, q]
        b = pairs_ref[1, q]
        live = q < total
        if u % 2 == 0:
            return (a, jnp.where(live, a, 32)), b
        return (b, jnp.where(jnp.logical_and(live, a != b), b, 32)), a

    groups = (total + GROUP // 2 - 1) // (GROUP // 2)
    tile_loop(item, groups, S_ref, A_ref, B_ref, acc33)
    acc_ref[...] = acc33[0:32]


def cross_terms(send_ref, link_ref, back_ref, msgs, to_ref, S_ref, A_ref, B_ref, src32, far32, acc, ready):
    for face in range(4):
        def row(k, face=face):
            return msgs[face][16 * k : 16 * k + 16, :]

        fill_rows(row, 16 * face, 16, src32, far32, None)
    finish_tables(64, src32, far32, S_ref, A_ref)
    pad_targets(B_ref, lambda b: to_ref[b])
    acc[...] = jnp.zeros_like(acc)
    ready()

    def item(g, u):
        q = g * (GROUP // 4) + u // 4
        if u % 4 == 0:
            target = send_ref[0, link_ref[0, q]]
            source = link_ref[1, q]
        elif u % 4 == 1:
            target = send_ref[1, back_ref[1, q]]
            source = 16 + back_ref[0, q]
        elif u % 4 == 2:
            target = send_ref[2, link_ref[2, q]]
            source = 32 + link_ref[3, q]
        else:
            target = send_ref[3, back_ref[11, q]]
            source = 48 + back_ref[10, q]
        return (target, target), source

    tile_loop(item, 48 // (GROUP // 4), S_ref, A_ref, B_ref, acc)


def rates(state_ref, own_acc, acc, flag, c):
    def total(f):
        at = pl.ds(8 * c * 32 + f, 8, stride=32)
        return kernel_coef * (own_acc[at, :] + acc[at, :])

    def row(k):
        return state_ref[32 * k + 8 * c : 32 * k + 8 * c + 8, :]

    places = [row(k) for k in range(3)]
    motion = [row(3 + k) for k in range(3)]
    scaled = [row(6 + k) for k in range(6)]
    blade = (spin_rate * places[2], jnp.zeros_like(places[1]), -spin_rate * places[0])
    mass_sum = total(0)
    lever = [places[l] * mass_sum - total(1 + l) for l in range(3)]
    stress_sum = [total(4 + s) for s in range(6)]
    acceleration = []
    for k in range(3):
        force = jnp.zeros_like(mass_sum)
        for l in range(3):
            slot = voigt_index[k][l]
            force = force + scaled[slot] * lever[l]
            force = force + places[l] * stress_sum[slot]
        force = force - total(10 + k)
        force = force + blade_stiff * flag * (blade[k] - motion[k])
        if k == 2:
            force = force - gravity
        acceleration.append(force)
    volume_sum = total(13)
    motion_sum = [total(14 + k) for k in range(3)]
    place_sum = [total(17 + k) for k in range(3)]
    strain = []
    for comp, (a, b) in enumerate(voigt_pairs):
        rate = 0.5 * (places[b] * motion_sum[a] + places[a] * motion_sum[b])
        rate = rate - total(20 + comp)
        rate = rate - 0.5 * volume_sum * (motion[a] * places[b] + motion[b] * places[a])
        rate = rate + 0.5 * (motion[a] * place_sum[b] + motion[b] * place_sum[a])
        strain.append(rate)
    return acceleration, strain


def elastic_step(stress, strain, fraction):
    volumetric = strain[0] + strain[1] + strain[2]
    lame_first = bulk_mod - 2.0 * shear_mod / 3.0
    components = []
    for comp in range(6):
        change = 2.0 * shear_mod * strain[comp]
        if comp < 3:
            change = change + lame_first * volumetric
        components.append(stress[comp] + fraction * time_step * change)
    return components


def plastic_return(components, plastic, cohesion):
    for _ in range(RETURN_ITERS):
        mean = (components[0] + components[1] + components[2]) / 3.0
        dev = [components[k] - mean for k in range(3)] + list(components[3:])
        second = 0.5 * (dev[0] * dev[0] + dev[1] * dev[1] + dev[2] * dev[2])
        second = second + dev[3] * dev[3] + dev[4] * dev[4] + dev[5] * dev[5]
        shear = jnp.sqrt(second)
        limit = cohesion * (1.0 + plastic / (plastic + harden_scale))
        excess = jnp.maximum(shear + friction * 3.0 * mean - limit, 0.0)
        multiplier = (relax_rate / (shear_mod + 9.0 * bulk_mod * friction * friction + harden_mod)) * excess
        shrink = jnp.maximum(1.0 - shear_mod * multiplier / jnp.maximum(shear, tau_floor), 0.0)
        mean = mean - 3.0 * bulk_mod * friction * multiplier
        components = [dev[k] * shrink + mean for k in range(3)] + [dev[k] * shrink for k in range(3, 6)]
        plastic = plastic + multiplier
    return components, plastic


def contact_column(contact_ref):
    rows = lax.broadcasted_iota(jnp.int32, (32, 16), 0)
    hit = jnp.where(contact_ref[...] == rows, 1.0, 0.0)
    return jnp.sum(hit, axis=1, keepdims=True)


def half_kernel(
    state_ref, own_acc, to_ref,
    m0, m1, m2, m3, sig_ref, plastic_ref, cohesion_ref, dens_ref, send_hbm, link_hbm, contact_hbm,
    next_ref, n0, n1, n2, n3, back_out,
    S_ref, A_ref, B_ref, src32, far32, acc, send_ref, link_ref, contact_ref, back_ref, sem,
):
    back_out[0:8, :] = m1[224:232, :].astype(jnp.int32)
    back_out[8:16, :] = m3[224:232, :].astype(jnp.int32)
    copies = fetch(
        [(back_out, back_ref), (send_hbm, send_ref), (link_hbm, link_ref), (contact_hbm, contact_ref)], sem
    )

    def ready():
        for copy in copies:
            copy.wait()

    cross_terms(
        send_ref, link_ref, back_ref, (m0, m1, m2, m3), to_ref, S_ref, A_ref, B_ref, src32, far32, acc, ready
    )
    flags = contact_column(contact_ref)
    own2 = own_acc.reshape(1024, 128)
    acc2 = acc.reshape(1024, 128)
    for c in range(4):
        at = slice(8 * c, 8 * c + 8)
        acceleration, strain = rates(state_ref, own2, acc2, flags[at], c)
        stress = [sig_ref[32 * k + 8 * c : 32 * k + 8 * c + 8, :] for k in range(6)]
        trial = elastic_step(stress, strain, 0.5)
        for k in range(3):
            x = slice(32 * k + 8 * c, 32 * k + 8 * c + 8)
            v = slice(96 + 32 * k + 8 * c, 96 + 32 * k + 8 * c + 8)
            motion = state_ref[v, :]
            next_ref[x, :] = state_ref[x, :] + 0.5 * time_step * motion
            next_ref[v, :] = motion + 0.5 * time_step * acceleration[k]
        for k in range(6):
            next_ref[192 + 32 * k + 8 * c : 200 + 32 * k + 8 * c, :] = trial[k]
    trial = [next_ref[192 + 32 * k : 224 + 32 * k, :] for k in range(6)]
    half_stress, _ = plastic_return(trial, plastic_ref[...], cohesion_ref[...])
    dens = dens_ref[...]
    square = dens * dens
    for k in range(6):
        next_ref[192 + 32 * k : 224 + 32 * k, :] = half_stress[k] / square
    next_ref[384:512, :] = state_ref[384:512, :]
    gather_rims(send_ref, next_ref, (n0, n1, n2, n3))


def last_kernel(
    state_ref, own_acc, to_ref,
    m0, m1, m2, m3, sig_ref, plastic_ref, cohesion_ref, pos_ref, vel_ref, back_vmem,
    send_hbm, link_hbm, contact_hbm, counts_hbm,
    pos_out, vel_out, sig_out, plastic_out,
    S_ref, A_ref, B_ref, src32, far32, acc, send_ref, link_ref, contact_ref, back_ref, counts_ref, sem,
):
    copies = fetch(
        [
            (back_vmem, back_ref),
            (send_hbm, send_ref),
            (link_hbm, link_ref),
            (contact_hbm, contact_ref),
            (counts_hbm, counts_ref),
        ],
        sem,
    )

    def ready():
        for copy in copies:
            copy.wait()

    cross_terms(
        send_ref, link_ref, back_ref, (m0, m1, m2, m3), to_ref, S_ref, A_ref, B_ref, src32, far32, acc, ready
    )
    flags = contact_column(contact_ref)
    column = lanes_to_column(counts_ref[...].astype(f32))
    lane = lax.broadcasted_iota(jnp.int32, (8, 128), 1).astype(f32)
    own2 = own_acc.reshape(1024, 128)
    acc2 = acc.reshape(1024, 128)
    for c in range(4):
        at = slice(8 * c, 8 * c + 8)
        keep = lane < column[at]
        acceleration, strain = rates(state_ref, own2, acc2, flags[at], c)
        stress = [sig_ref[32 * k + 8 * c : 32 * k + 8 * c + 8, :] for k in range(6)]
        trial = elastic_step(stress, strain, 1.0)
        for k in range(3):
            x = slice(32 * k + 8 * c, 32 * k + 8 * c + 8)
            v = slice(96 + 32 * k + 8 * c, 96 + 32 * k + 8 * c + 8)
            pos_out[x, :] = jnp.where(keep, pos_ref[x, :] + time_step * state_ref[v, :], 0.0)
            vel_out[x, :] = jnp.where(keep, vel_ref[x, :] + time_step * acceleration[k], 0.0)
        for k in range(6):
            sig_out[32 * k + 8 * c : 32 * k + 8 * c + 8, :] = trial[k]
    keep = lax.broadcasted_iota(jnp.int32, (32, 128), 1).astype(f32) < column
    trial = [sig_out[32 * k : 32 * k + 32, :] for k in range(6)]
    new_stress, new_plastic = plastic_return(trial, plastic_ref[...], cohesion_ref[...])
    for k in range(6):
        sig_out[32 * k : 32 * k + 32, :] = jnp.where(keep, new_stress[k], 0.0)
    plastic_out[...] = jnp.where(keep, new_plastic, 0.0)


SMEM = pl.BlockSpec(memory_space=pltpu.SMEM)
VMEM = pl.BlockSpec(memory_space=pltpu.VMEM)
HBM = pl.BlockSpec(memory_space=pltpu.HBM)
params = pltpu.CompilerParams(vmem_limit_bytes=48 * 1024 * 1024)


def in_hbm(value):
    return pltpu.with_memory_space_constraint(value, pltpu.HBM)


def shape(*dims, dtype=f32):
    return jax.ShapeDtypeStruct(dims, dtype)


def tables(count):
    return [
        pltpu.VMEM((count, 64, 128), bf16),
        pltpu.VMEM((count // 8, 128, 128), bf16),
        pltpu.VMEM((32, 240, 128), bf16),
        pltpu.VMEM((count * 32, 128), f32),
        pltpu.VMEM((count * 16, 128), f32),
    ]


def call(kernel, smem, vmem, hbm, outs, scratch):
    return pl.pallas_call(
        kernel,
        out_shape=outs,
        in_specs=[SMEM] * len(smem) + [VMEM] * len(vmem) + [HBM] * len(hbm),
        out_specs=[VMEM] * len(outs),
        scratch_shapes=scratch,
        compiler_params=params,
    )(*smem, *vmem, *hbm)


def shards(
    position, velocity, stress, plastic, particle_mass, density, cohesion,
    counts, block_pairs, pair_count, send_lists, cross_links, contact,
):
    pos = position.reshape(96, 128)
    vel = velocity.reshape(96, 128)
    sig = stress.reshape(192, 128)
    plastic_now = plastic.reshape(32, 128)
    mass = particle_mass.reshape(32, 128)
    dens = density.reshape(32, 128)
    cohesion_now = cohesion.reshape(32, 128)
    counts_now = counts.reshape(1, 32)
    pairs = jnp.swapaxes(block_pairs.reshape(128, 2), 0, 1)
    total = pair_count.reshape(1)
    send = send_lists.reshape(4, 16)
    links = jnp.swapaxes(cross_links.reshape(2, 48, 2), 1, 2).reshape(4, 48)
    touched = contact.reshape(1, 16)

    rim = [shape(16 * ROWS, 128)] * 4
    state, *msgs = pl.pallas_call(
        start_kernel,
        out_shape=[shape(512, 128)] + rim,
        in_specs=[HBM] * 8,
        out_specs=[VMEM] * 5,
        scratch_shapes=[
            pltpu.SMEM((4, 16), jnp.int32),
            pltpu.VMEM((1, 32), jnp.int32),
            pltpu.VMEM((4, 48), jnp.int32),
            pltpu.VMEM((192, 128), f32),
            pltpu.VMEM((32, 128), f32),
            pltpu.VMEM((32, 128), f32),
            pltpu.SemaphoreType.DMA((8,)),
        ],
        compiler_params=params,
    )(*[in_hbm(x) for x in (send, counts_now, links, pos, vel, sig, mass, dens)])

    def swap(msgs):
        return (
            by_axis(msgs[1], "depth", -1, False),
            by_axis(msgs[0], "depth", 1, False),
            by_axis(msgs[3], "strip", -1, True),
            by_axis(msgs[2], "strip", 1, True),
        )

    def own(state):
        return call(
            own_kernel,
            [total],
            [state],
            [in_hbm(pairs)],
            [shape(32, 32, 128), shape(32, 16, 128, dtype=bf16)],
            tables(32) + [pltpu.VMEM((512, 128), f32), pltpu.VMEM((33, 32, 128), f32),
                pltpu.SMEM((2, 128), jnp.int32), pltpu.SemaphoreType.DMA((1,))],
        )

    cross_scratch = tables(64) + [
        pltpu.VMEM((32, 32, 128), f32),
        pltpu.SMEM((4, 16), jnp.int32),
        pltpu.SMEM((4, 48), jnp.int32),
        pltpu.VMEM((1, 16), jnp.int32),
        pltpu.SMEM((16, 128), jnp.int32),
    ]
    lists = [in_hbm(x) for x in (send, links, touched)]
    far = swap(msgs)
    own_acc, to_side = own(state)
    state, *msgs, back = call(
        half_kernel,
        [],
        [state, own_acc, to_side, *far, sig, plastic_now, cohesion_now, dens],
        lists,
        [shape(512, 128)] + rim + [shape(16, 128, dtype=jnp.int32)],
        cross_scratch + [pltpu.SemaphoreType.DMA((4,))],
    )
    far = swap(msgs)
    own_acc, to_side = own(state)
    new_pos, new_vel, new_sig, new_plastic = call(
        last_kernel,
        [],
        [state, own_acc, to_side, *far, sig, plastic_now, cohesion_now, pos, vel, back],
        lists + [in_hbm(counts_now)],
        [shape(96, 128), shape(96, 128), shape(192, 128), shape(32, 128)],
        cross_scratch + [pltpu.VMEM((1, 32), jnp.int32), pltpu.SemaphoreType.DMA((5,))],
    )
    return (
        new_pos.reshape(position.shape),
        new_vel.reshape(velocity.shape),
        new_sig.reshape(stress.shape),
        new_plastic.reshape(plastic.shape),
    )


def solution(mesh):
    def spec(rank):
        return P("strip", "depth", *([None] * (rank - 2)))

    return jax.shard_map(
        shards,
        mesh=mesh,
        in_specs=tuple(spec(r) for r in (5, 5, 5, 4, 4, 4, 4, 3, 4, 2, 4, 5, 3)),
        out_specs=tuple(spec(r) for r in (5, 5, 5, 4)),
        check_vma=False,
    )
```

```python
import functools

import jax
import jax.numpy as jnp
from jax import lax
from jax.experimental import pallas as pl
from jax.experimental.pallas import tpu as pltpu
from jax.sharding import PartitionSpec as P

RETURN_ITERS = 4
ROWS = 16
GROUP = 64

smooth_len = 1.5
kernel_coef = -105.0 / (3.141592653589793 * 1.5**5)
time_step = 0.25
gravity = 1.0
spin_rate = 2.0
blade_stiff = 4.0
bulk_mod = 2.0
shear_mod = 1.5
friction = 0.25
harden_scale = 0.05
harden_mod = 0.5
relax_rate = 0.7
tau_floor = 0.5
voigt_index = ((0, 3, 5), (3, 1, 4), (5, 4, 2))
voigt_pairs = ((0, 0), (1, 1), (2, 2), (0, 1), (1, 2), (0, 2))
bf16 = jnp.bfloat16
f32 = jnp.float32


def swap_pairs(value, axis, odd, closed):
    count = lax.axis_size(axis)
    pairs = []
    for i in range(odd, count, 2):
        j = (i + 1) % count
        if j == i + 1 or closed:
            pairs += [(i, j), (j, i)]
    return lax.ppermute(value, axis, pairs)


def parity(axis):
    return lax.rem(lax.axis_index(axis), 2)


def halves(value):
    high = value.astype(bf16).astype(f32)
    return high, value - high


def source_rows(row):
    places = [row(k) for k in range(3)]
    motion = [row(3 + k) for k in range(3)]
    scaled = [row(6 + k) for k in range(6)]
    mass, volume = row(12), row(13)
    out = [mass]
    out += [mass * x for x in places]
    out += [mass * s for s in scaled]
    for k in range(3):
        dotted = scaled[voigt_index[k][0]] * places[0]
        dotted = dotted + scaled[voigt_index[k][1]] * places[1]
        dotted = dotted + scaled[voigt_index[k][2]] * places[2]
        out.append(mass * dotted)
    out.append(volume)
    out += [volume * v for v in motion]
    out += [volume * x for x in places]
    for a, b in voigt_pairs:
        out.append(volume * (0.5 * (motion[a] * places[b] + motion[b] * places[a])))
    return out


def distance_rows(row):
    places = [row(k) * (1.0 / smooth_len) for k in range(3)]
    square = places[0] * places[0] + places[1] * places[1] + places[2] * places[2]
    high, low = zip(*[halves(x) for x in places])
    n0, rest = halves(square)
    n1, n2 = halves(rest)
    one = jnp.ones_like(square)
    zero = jnp.zeros_like(square)
    from_side = [-2.0 * x for x in high + low + high] + [n0, n1, n2, one, one, one, zero]
    to_side = list(high + high + low) + [one, one, one, n0, n1, n2, zero]
    return from_side, to_side


def fill_rows(row, base, count, src32, far32, to32):
    for f, value in enumerate(source_rows(row)):
        src32[pl.ds(base * 32 + f, count, stride=32), :] = value
    from_side, to_side = distance_rows(row)
    for f, value in enumerate(from_side):
        far32[pl.ds(base * 16 + f, count, stride=16), :] = value
    if to32 is not None:
        for f, value in enumerate(to_side):
            to32[pl.ds(base * 16 + f, count, stride=16), :] = value


def finish_tables(count, src32, far32, S_ref, A_ref):
    def eight(i, carry):
        flipped = far32[pl.ds(pl.multiple_of(i * 128, 128), 128), :].T
        A_ref[i] = flipped.astype(bf16)
        for u in range(8):
            b = i * 8 + u
            value = src32[pl.ds(pl.multiple_of(b * 32, 32), 32), :]
            high = value.astype(bf16)
            S_ref[b, 0:32, :] = high
            S_ref[b, 32:64, :] = (value - high.astype(f32)).astype(bf16)
        return carry

    lax.fori_loop(0, count // 8, eight, 0)


def pad_targets(B_ref, rows_of):
    def one(b, carry):
        B_ref[b, 0:112, :] = jnp.zeros((112, 128), bf16)
        B_ref[b, 128:240, :] = jnp.zeros((112, 128), bf16)
        B_ref[b, 112:128, :] = rows_of(b)
        return carry

    lax.fori_loop(0, 32, one, 0)


def closeness_cubed(square):
    square = jnp.maximum(square, 1e-30)
    close = jnp.maximum(1.0 - square * lax.rsqrt(square), 0.0)
    return close * close * close


def tile_loop(item, groups, S_ref, A_ref, B_ref, acc_ref):
    def one_group(g, carry):
        outs = []
        for u in range(GROUP):
            target, source = item(g, u)
            start = pl.multiple_of(112 - 16 * lax.rem(source, 8), 16)
            square = jnp.dot(
                A_ref[lax.div(source, 8)],
                B_ref[target[0], pl.ds(start, 128), :],
                preferred_element_type=f32,
            )
            kernel = closeness_cubed(square)
            high = kernel.astype(bf16)
            low = (kernel - high.astype(f32)).astype(bf16)
            rows = S_ref[source]
            both = jnp.dot(
                jnp.concatenate([rows, rows], 1),
                jnp.concatenate([high, low], 0),
                preferred_element_type=f32,
            )
            outs.append((target[1], both[:32] + both[32:]))
        for target, value in outs:
            acc_ref[target] += value
        return carry

    lax.fori_loop(0, groups, one_group, 0)


def lanes_to_column(values):
    n = values.shape[1]
    rows = lax.broadcasted_iota(jnp.int32, (n, n), 0)
    cols = lax.broadcasted_iota(jnp.int32, (n, n), 1)
    return jnp.sum(jnp.where(rows == cols, values, 0.0), axis=1, keepdims=True)


def gather_rims(send_ref, state_ref, msgs):
    depth, strip = parity("depth"), parity("strip")
    for m, face in enumerate((depth, 1 - depth, 2 + strip, 3 - strip)):
        for slot in range(16):
            block = send_ref[face, slot]
            msgs[m][pl.ds(slot, ROWS, stride=16), :] = state_ref[
                pl.ds(block, ROWS, stride=32), :
            ]


def fetch(pairs, sem):
    copies = [pltpu.make_async_copy(a, b, sem.at[i]) for i, (a, b) in enumerate(pairs)]
    for copy in copies:
        copy.start()
    return copies


def start_kernel(
    send_hbm, counts_hbm, links_hbm, pos_hbm, vel_hbm, sig_hbm, mass_hbm, dens_hbm,
    state_ref, m0, m1, m2, m3, send_ref, counts_ref, links_ref, sig_ref, mass_ref, dens_ref, sem,
):
    copies = fetch(
        [
            (send_hbm, send_ref),
            (counts_hbm, counts_ref),
            (links_hbm, links_ref),
            (pos_hbm, state_ref.at[0:96]),
            (vel_hbm, state_ref.at[96:192]),
            (sig_hbm, sig_ref),
            (mass_hbm, mass_ref),
            (dens_hbm, dens_ref),
        ],
        sem,
    )
    for copy in copies:
        copy.wait()
    column = lanes_to_column(counts_ref[...].astype(f32))
    lane = lax.broadcasted_iota(jnp.int32, (32, 128), 1).astype(f32)
    mass = jnp.where(lane < column, mass_ref[...], 0.0)
    dens = dens_ref[...]
    square = dens * dens
    for k in range(6):
        state_ref[192 + 32 * k : 224 + 32 * k, :] = sig_ref[32 * k : 32 * k + 32, :] / square
    state_ref[384:416, :] = mass
    state_ref[416:448, :] = mass / dens
    state_ref[448:512, :] = jnp.zeros((64, 128), f32)
    gather_rims(send_ref, state_ref, (m0, m1, m2, m3))
    links = links_ref[...].astype(f32)
    for msg in (m0, m1, m2, m3):
        msg[224:228, 0:48] = links


def own_kernel(
    count_ref, state_ref, pairs_hbm, acc_ref, to_ref,
    S_ref, A_ref, B_ref, src32, far32, to32, acc33, pairs_ref, sem,
):
    copies = fetch([(pairs_hbm, pairs_ref)], sem)

    def row(k):
        return state_ref[32 * k : 32 * k + 32, :]

    fill_rows(row, 0, 32, src32, far32, to32)
    finish_tables(32, src32, far32, S_ref, A_ref)

    def rows_of(b):
        rows = to32[pl.ds(pl.multiple_of(b * 16, 16), 16), :].astype(bf16)
        to_ref[b] = rows
        return rows

    pad_targets(B_ref, rows_of)
    acc33[...] = jnp.zeros_like(acc33)
    total = count_ref[0]
    copies[0].wait()

    def item(g, u):
        q = g * (GROUP // 2) + u // 2
        a = pairs_ref[0, q]
        b = pairs_ref[1, q]
        live = q < total
        if u % 2 == 0:
            return (a, jnp.where(live, a, 32)), b
        return (b, jnp.where(jnp.logical_and(live, a != b), b, 32)), a

    groups = (total + GROUP // 2 - 1) // (GROUP // 2)
    tile_loop(item, groups, S_ref, A_ref, B_ref, acc33)
    acc_ref[...] = acc33[0:32]


def cross_terms(send_ref, link_ref, back_ref, msgs, to_ref, S_ref, A_ref, B_ref, src32, far32, acc, ready):
    for face in range(4):
        def row(k, face=face):
            return msgs[face][16 * k : 16 * k + 16, :]

        fill_rows(row, 16 * face, 16, src32, far32, None)
    finish_tables(64, src32, far32, S_ref, A_ref)
    pad_targets(B_ref, lambda b: to_ref[b])
    acc[...] = jnp.zeros_like(acc)
    ready()

    depth, strip = parity("depth"), parity("strip")

    def item(g, u):
        q = g * (GROUP // 4) + u // 4
        if u % 4 == 0:
            target = send_ref[0, link_ref[0, q]]
            source = 16 * depth + link_ref[1, q]
        elif u % 4 == 1:
            row = 8 * (1 - depth)
            target = send_ref[1, back_ref[row + 1, q]]
            source = 16 * (1 - depth) + back_ref[row, q]
        elif u % 4 == 2:
            target = send_ref[2, link_ref[2, q]]
            source = 32 + 16 * strip + link_ref[3, q]
        else:
            row = 16 + 8 * (1 - strip)
            target = send_ref[3, back_ref[row + 3, q]]
            source = 32 + 16 * (1 - strip) + back_ref[row + 2, q]
        return (target, target), source

    tile_loop(item, 48 // (GROUP // 4), S_ref, A_ref, B_ref, acc)


def rates(state_ref, own_acc, acc, flag, c):
    def total(f):
        at = pl.ds(8 * c * 32 + f, 8, stride=32)
        return kernel_coef * (own_acc[at, :] + acc[at, :])

    def row(k):
        return state_ref[32 * k + 8 * c : 32 * k + 8 * c + 8, :]

    places = [row(k) for k in range(3)]
    motion = [row(3 + k) for k in range(3)]
    scaled = [row(6 + k) for k in range(6)]
    blade = (spin_rate * places[2], jnp.zeros_like(places[1]), -spin_rate * places[0])
    mass_sum = total(0)
    lever = [places[l] * mass_sum - total(1 + l) for l in range(3)]
    stress_sum = [total(4 + s) for s in range(6)]
    acceleration = []
    for k in range(3):
        force = jnp.zeros_like(mass_sum)
        for l in range(3):
            slot = voigt_index[k][l]
            force = force + scaled[slot] * lever[l]
            force = force + places[l] * stress_sum[slot]
        force = force - total(10 + k)
        force = force + blade_stiff * flag * (blade[k] - motion[k])
        if k == 2:
            force = force - gravity
        acceleration.append(force)
    volume_sum = total(13)
    motion_sum = [total(14 + k) for k in range(3)]
    place_sum = [total(17 + k) for k in range(3)]
    strain = []
    for comp, (a, b) in enumerate(voigt_pairs):
        rate = 0.5 * (places[b] * motion_sum[a] + places[a] * motion_sum[b])
        rate = rate - total(20 + comp)
        rate = rate - 0.5 * volume_sum * (motion[a] * places[b] + motion[b] * places[a])
        rate = rate + 0.5 * (motion[a] * place_sum[b] + motion[b] * place_sum[a])
        strain.append(rate)
    return acceleration, strain


def elastic_step(stress, strain, fraction):
    volumetric = strain[0] + strain[1] + strain[2]
    lame_first = bulk_mod - 2.0 * shear_mod / 3.0
    components = []
    for comp in range(6):
        change = 2.0 * shear_mod * strain[comp]
        if comp < 3:
            change = change + lame_first * volumetric
        components.append(stress[comp] + fraction * time_step * change)
    return components


def plastic_return(components, plastic, cohesion):
    for _ in range(RETURN_ITERS):
        mean = (components[0] + components[1] + components[2]) / 3.0
        dev = [components[k] - mean for k in range(3)] + list(components[3:])
        second = 0.5 * (dev[0] * dev[0] + dev[1] * dev[1] + dev[2] * dev[2])
        second = second + dev[3] * dev[3] + dev[4] * dev[4] + dev[5] * dev[5]
        shear = jnp.sqrt(second)
        limit = cohesion * (1.0 + plastic / (plastic + harden_scale))
        excess = jnp.maximum(shear + friction * 3.0 * mean - limit, 0.0)
        multiplier = (relax_rate / (shear_mod + 9.0 * bulk_mod * friction * friction + harden_mod)) * excess
        shrink = jnp.maximum(1.0 - shear_mod * multiplier / jnp.maximum(shear, tau_floor), 0.0)
        mean = mean - 3.0 * bulk_mod * friction * multiplier
        components = [dev[k] * shrink + mean for k in range(3)] + [dev[k] * shrink for k in range(3, 6)]
        plastic = plastic + multiplier
    return components, plastic


def contact_column(contact_ref):
    rows = lax.broadcasted_iota(jnp.int32, (32, 16), 0)
    hit = jnp.where(contact_ref[...] == rows, 1.0, 0.0)
    return jnp.sum(hit, axis=1, keepdims=True)


def half_kernel(
    state_ref, own_acc, to_ref,
    m0, m1, m2, m3, sig_ref, plastic_ref, cohesion_ref, dens_ref, send_hbm, link_hbm, contact_hbm,
    next_ref, n0, n1, n2, n3, back_out,
    S_ref, A_ref, B_ref, src32, far32, acc, send_ref, link_ref, contact_ref, back_ref, sem,
):
    for m, msg in enumerate((m0, m1, m2, m3)):
        back_out[8 * m : 8 * m + 8, :] = msg[224:232, :].astype(jnp.int32)
    copies = fetch(
        [(back_out, back_ref), (send_hbm, send_ref), (link_hbm, link_ref), (contact_hbm, contact_ref)], sem
    )

    def ready():
        for copy in copies:
            copy.wait()

    cross_terms(
        send_ref, link_ref, back_ref, (m0, m1, m2, m3), to_ref, S_ref, A_ref, B_ref, src32, far32, acc, ready
    )
    flags = contact_column(contact_ref)
    own2 = own_acc.reshape(1024, 128)
    acc2 = acc.reshape(1024, 128)
    for c in range(4):
        at = slice(8 * c, 8 * c + 8)
        acceleration, strain = rates(state_ref, own2, acc2, flags[at], c)
        stress = [sig_ref[32 * k + 8 * c : 32 * k + 8 * c + 8, :] for k in range(6)]
        trial = elastic_step(stress, strain, 0.5)
        for k in range(3):
            x = slice(32 * k + 8 * c, 32 * k + 8 * c + 8)
            v = slice(96 + 32 * k + 8 * c, 96 + 32 * k + 8 * c + 8)
            motion = state_ref[v, :]
            next_ref[x, :] = state_ref[x, :] + 0.5 * time_step * motion
            next_ref[v, :] = motion + 0.5 * time_step * acceleration[k]
        for k in range(6):
            next_ref[192 + 32 * k + 8 * c : 200 + 32 * k + 8 * c, :] = trial[k]
    trial = [next_ref[192 + 32 * k : 224 + 32 * k, :] for k in range(6)]
    half_stress, _ = plastic_return(trial, plastic_ref[...], cohesion_ref[...])
    dens = dens_ref[...]
    square = dens * dens
    for k in range(6):
        next_ref[192 + 32 * k : 224 + 32 * k, :] = half_stress[k] / square
    next_ref[384:512, :] = state_ref[384:512, :]
    gather_rims(send_ref, next_ref, (n0, n1, n2, n3))


def last_kernel(
    state_ref, own_acc, to_ref,
    m0, m1, m2, m3, sig_ref, plastic_ref, cohesion_ref, pos_ref, vel_ref, back_vmem,
    send_hbm, link_hbm, contact_hbm, counts_hbm,
    pos_out, vel_out, sig_out, plastic_out,
    S_ref, A_ref, B_ref, src32, far32, acc, send_ref, link_ref, contact_ref, back_ref, counts_ref, sem,
):
    copies = fetch(
        [
            (back_vmem, back_ref),
            (send_hbm, send_ref),
            (link_hbm, link_ref),
            (contact_hbm, contact_ref),
            (counts_hbm, counts_ref),
        ],
        sem,
    )

    def ready():
        for copy in copies:
            copy.wait()

    cross_terms(
        send_ref, link_ref, back_ref, (m0, m1, m2, m3), to_ref, S_ref, A_ref, B_ref, src32, far32, acc, ready
    )
    flags = contact_column(contact_ref)
    column = lanes_to_column(counts_ref[...].astype(f32))
    lane = lax.broadcasted_iota(jnp.int32, (8, 128), 1).astype(f32)
    own2 = own_acc.reshape(1024, 128)
    acc2 = acc.reshape(1024, 128)
    for c in range(4):
        at = slice(8 * c, 8 * c + 8)
        keep = lane < column[at]
        acceleration, strain = rates(state_ref, own2, acc2, flags[at], c)
        stress = [sig_ref[32 * k + 8 * c : 32 * k + 8 * c + 8, :] for k in range(6)]
        trial = elastic_step(stress, strain, 1.0)
        for k in range(3):
            x = slice(32 * k + 8 * c, 32 * k + 8 * c + 8)
            v = slice(96 + 32 * k + 8 * c, 96 + 32 * k + 8 * c + 8)
            pos_out[x, :] = jnp.where(keep, pos_ref[x, :] + time_step * state_ref[v, :], 0.0)
            vel_out[x, :] = jnp.where(keep, vel_ref[x, :] + time_step * acceleration[k], 0.0)
        for k in range(6):
            sig_out[32 * k + 8 * c : 32 * k + 8 * c + 8, :] = trial[k]
    keep = lax.broadcasted_iota(jnp.int32, (32, 128), 1).astype(f32) < column
    trial = [sig_out[32 * k : 32 * k + 32, :] for k in range(6)]
    new_stress, new_plastic = plastic_return(trial, plastic_ref[...], cohesion_ref[...])
    for k in range(6):
        sig_out[32 * k : 32 * k + 32, :] = jnp.where(keep, new_stress[k], 0.0)
    plastic_out[...] = jnp.where(keep, new_plastic, 0.0)


SMEM = pl.BlockSpec(memory_space=pltpu.SMEM)
VMEM = pl.BlockSpec(memory_space=pltpu.VMEM)
HBM = pl.BlockSpec(memory_space=pltpu.HBM)
params = pltpu.CompilerParams(vmem_limit_bytes=48 * 1024 * 1024)


def in_hbm(value):
    return pltpu.with_memory_space_constraint(value, pltpu.HBM)


def shape(*dims, dtype=f32):
    return jax.ShapeDtypeStruct(dims, dtype)


def tables(count):
    return [
        pltpu.VMEM((count, 64, 128), bf16),
        pltpu.VMEM((count // 8, 128, 128), bf16),
        pltpu.VMEM((32, 240, 128), bf16),
        pltpu.VMEM((count * 32, 128), f32),
        pltpu.VMEM((count * 16, 128), f32),
    ]


def call(kernel, smem, vmem, hbm, outs, scratch):
    return pl.pallas_call(
        kernel,
        out_shape=outs,
        in_specs=[SMEM] * len(smem) + [VMEM] * len(vmem) + [HBM] * len(hbm),
        out_specs=[VMEM] * len(outs),
        scratch_shapes=scratch,
        compiler_params=params,
    )(*smem, *vmem, *hbm)


def shards(
    position, velocity, stress, plastic, particle_mass, density, cohesion,
    counts, block_pairs, pair_count, send_lists, cross_links, contact,
):
    pos = position.reshape(96, 128)
    vel = velocity.reshape(96, 128)
    sig = stress.reshape(192, 128)
    plastic_now = plastic.reshape(32, 128)
    mass = particle_mass.reshape(32, 128)
    dens = density.reshape(32, 128)
    cohesion_now = cohesion.reshape(32, 128)
    counts_now = counts.reshape(1, 32)
    pairs = jnp.swapaxes(block_pairs.reshape(128, 2), 0, 1)
    total = pair_count.reshape(1)
    send = send_lists.reshape(4, 16)
    links = jnp.swapaxes(cross_links.reshape(2, 48, 2), 1, 2).reshape(4, 48)
    touched = contact.reshape(1, 16)

    rim = [shape(16 * ROWS, 128)] * 4
    state, *msgs = pl.pallas_call(
        start_kernel,
        out_shape=[shape(512, 128)] + rim,
        in_specs=[HBM] * 8,
        out_specs=[VMEM] * 5,
        scratch_shapes=[
            pltpu.SMEM((4, 16), jnp.int32),
            pltpu.VMEM((1, 32), jnp.int32),
            pltpu.VMEM((4, 48), jnp.int32),
            pltpu.VMEM((192, 128), f32),
            pltpu.VMEM((32, 128), f32),
            pltpu.VMEM((32, 128), f32),
            pltpu.SemaphoreType.DMA((8,)),
        ],
        compiler_params=params,
    )(*[in_hbm(x) for x in (send, counts_now, links, pos, vel, sig, mass, dens)])

    def swap(msgs):
        return (
            swap_pairs(msgs[0], "depth", 0, False),
            swap_pairs(msgs[1], "depth", 1, False),
            swap_pairs(msgs[2], "strip", 0, True),
            swap_pairs(msgs[3], "strip", 1, True),
        )

    def own(state):
        return call(
            own_kernel,
            [total],
            [state],
            [in_hbm(pairs)],
            [shape(32, 32, 128), shape(32, 16, 128, dtype=bf16)],
            tables(32) + [pltpu.VMEM((512, 128), f32), pltpu.VMEM((33, 32, 128), f32),
                pltpu.SMEM((2, 128), jnp.int32), pltpu.SemaphoreType.DMA((1,))],
        )

    cross_scratch = tables(64) + [
        pltpu.VMEM((32, 32, 128), f32),
        pltpu.SMEM((4, 16), jnp.int32),
        pltpu.SMEM((4, 48), jnp.int32),
        pltpu.VMEM((1, 16), jnp.int32),
        pltpu.SMEM((32, 128), jnp.int32),
    ]
    lists = [in_hbm(x) for x in (send, links, touched)]
    far = swap(msgs)
    own_acc, to_side = own(state)
    state, *msgs, back = call(
        half_kernel,
        [],
        [state, own_acc, to_side, *far, sig, plastic_now, cohesion_now, dens],
        lists,
        [shape(512, 128)] + rim + [shape(32, 128, dtype=jnp.int32)],
        cross_scratch + [pltpu.SemaphoreType.DMA((4,))],
    )
    far = swap(msgs)
    own_acc, to_side = own(state)
    new_pos, new_vel, new_sig, new_plastic = call(
        last_kernel,
        [],
        [state, own_acc, to_side, *far, sig, plastic_now, cohesion_now, pos, vel, back],
        lists + [in_hbm(counts_now)],
        [shape(96, 128), shape(96, 128), shape(192, 128), shape(32, 128)],
        cross_scratch + [pltpu.VMEM((1, 32), jnp.int32), pltpu.SemaphoreType.DMA((5,))],
    )
    return (
        new_pos.reshape(position.shape),
        new_vel.reshape(velocity.shape),
        new_sig.reshape(stress.shape),
        new_plastic.reshape(plastic.shape),
    )


def solution(mesh):
    def spec(rank):
        return P("strip", "depth", *([None] * (rank - 2)))

    return jax.shard_map(
        shards,
        mesh=mesh,
        in_specs=tuple(spec(r) for r in (5, 5, 5, 4, 4, 4, 4, 3, 4, 2, 4, 5, 3)),
        out_specs=tuple(spec(r) for r in (5, 5, 5, 4)),
        check_vma=False,
    )
```

```python
import functools

import jax
import jax.numpy as jnp
from jax import lax
from jax.experimental import pallas as pl
from jax.experimental.pallas import tpu as pltpu
from jax.sharding import PartitionSpec as P

RETURN_ITERS = 4
ROWS = 16
OWN_GROUP = 64
CROSS_GROUP = 96

smooth_len = 1.5
kernel_coef = -105.0 / (3.141592653589793 * 1.5**5)
time_step = 0.25
gravity = 1.0
spin_rate = 2.0
blade_stiff = 4.0
bulk_mod = 2.0
shear_mod = 1.5
friction = 0.25
harden_scale = 0.05
harden_mod = 0.5
relax_rate = 0.7
tau_floor = 0.5
voigt_index = ((0, 3, 5), (3, 1, 4), (5, 4, 2))
voigt_pairs = ((0, 0), (1, 1), (2, 2), (0, 1), (1, 2), (0, 2))
bf16 = jnp.bfloat16
f32 = jnp.float32


def swap_pairs(value, axis, odd, closed):
    count = lax.axis_size(axis)
    pairs = []
    for i in range(odd, count, 2):
        j = (i + 1) % count
        if j == i + 1 or closed:
            pairs += [(i, j), (j, i)]
    return lax.ppermute(value, axis, pairs)


def parity(axis):
    return lax.rem(lax.axis_index(axis), 2)


def halves(value):
    high = value.astype(bf16).astype(f32)
    return high, value - high


def source_rows(row):
    places = [row(k) for k in range(3)]
    motion = [row(3 + k) for k in range(3)]
    scaled = [row(6 + k) for k in range(6)]
    mass, volume = row(12), row(13)
    out = [mass]
    out += [mass * x for x in places]
    out += [mass * s for s in scaled]
    for k in range(3):
        dotted = scaled[voigt_index[k][0]] * places[0]
        dotted = dotted + scaled[voigt_index[k][1]] * places[1]
        dotted = dotted + scaled[voigt_index[k][2]] * places[2]
        out.append(mass * dotted)
    out.append(volume)
    out += [volume * v for v in motion]
    out += [volume * x for x in places]
    for a, b in voigt_pairs:
        out.append(volume * (0.5 * (motion[a] * places[b] + motion[b] * places[a])))
    return out


def distance_rows(row):
    places = [row(k) * (1.0 / smooth_len) for k in range(3)]
    square = places[0] * places[0] + places[1] * places[1] + places[2] * places[2]
    high, low = zip(*[halves(x) for x in places])
    n0, rest = halves(square)
    n1, n2 = halves(rest)
    one = jnp.ones_like(square)
    zero = jnp.zeros_like(square)
    from_side = [-2.0 * x for x in high + low + high] + [n0, n1, n2, one, one, one, zero]
    to_side = list(high + high + low) + [one, one, one, n0, n1, n2, zero]
    return from_side, to_side


def fill_rows(row, base, count, src32, far32, to32):
    for f, value in enumerate(source_rows(row)):
        src32[pl.ds(base * 32 + f, count, stride=32), :] = value
    from_side, to_side = distance_rows(row)
    for f, value in enumerate(from_side):
        far32[pl.ds(base * 16 + f, count, stride=16), :] = value
    if to32 is not None:
        for f, value in enumerate(to_side):
            to32[pl.ds(base * 16 + f, count, stride=16), :] = value


def finish_tables(count, src32, far32, S_ref, A_ref):
    def eight(i, carry):
        flipped = far32[pl.ds(pl.multiple_of(i * 128, 128), 128), :].T
        A_ref[i] = flipped.astype(bf16)
        for u in range(8):
            b = i * 8 + u
            value = src32[pl.ds(pl.multiple_of(b * 32, 32), 32), :]
            high = value.astype(bf16)
            S_ref[b, 0:32, :] = high
            S_ref[b, 32:64, :] = (value - high.astype(f32)).astype(bf16)
        return carry

    lax.fori_loop(0, count // 8, eight, 0)


def pad_targets(B_ref, rows_of):
    def one(b, carry):
        B_ref[b, 0:112, :] = jnp.zeros((112, 128), bf16)
        B_ref[b, 128:240, :] = jnp.zeros((112, 128), bf16)
        B_ref[b, 112:128, :] = rows_of(b)
        return carry

    lax.fori_loop(0, 32, one, 0)


def closeness_cubed(square):
    square = jnp.maximum(square, 1e-30)
    close = jnp.maximum(1.0 - square * lax.rsqrt(square), 0.0)
    return close * close * close


def tile_group(items, S_ref, A_ref, B_ref, acc_ref):
    outs = []
    for target, into, source in items:
        if isinstance(source, int):
            start, octet = 112 - 16 * (source % 8), source // 8
        else:
            start = pl.multiple_of(112 - 16 * lax.rem(source, 8), 16)
            octet = lax.div(source, 8)
        square = jnp.dot(
            A_ref[octet], B_ref[target, pl.ds(start, 128), :], preferred_element_type=f32
        )
        kernel = closeness_cubed(square)
        high = kernel.astype(bf16)
        low = (kernel - high.astype(f32)).astype(bf16)
        rows = S_ref[source]
        both = jnp.dot(
            jnp.concatenate([rows, rows], 1),
            jnp.concatenate([high, low], 0),
            preferred_element_type=f32,
        )
        outs.append((into, both[:32] + both[32:]))
    for into, value in outs:
        acc_ref[into] += value


def lanes_to_column(values):
    n = values.shape[1]
    rows = lax.broadcasted_iota(jnp.int32, (n, n), 0)
    cols = lax.broadcasted_iota(jnp.int32, (n, n), 1)
    return jnp.sum(jnp.where(rows == cols, values, 0.0), axis=1, keepdims=True)


def gather_rims(send_ref, state_ref, msgs):
    depth, strip = parity("depth"), parity("strip")
    for m, face in enumerate((depth, 1 - depth, 2 + strip, 3 - strip)):
        for slot in range(16):
            block = send_ref[face, slot]
            msgs[m][pl.ds(slot, ROWS, stride=16), :] = state_ref[
                pl.ds(block, ROWS, stride=32), :
            ]


def fetch(pairs, sem):
    copies = [pltpu.make_async_copy(a, b, sem.at[i]) for i, (a, b) in enumerate(pairs)]
    for copy in copies:
        copy.start()
    return copies


def own_terms(count_ref, pairs_ref, off_ref, state_ref, acc_ref, to_ref, S_ref, A_ref, B_ref, src32, far32, to32, acc33, ready):
    def row(k):
        return state_ref[32 * k : 32 * k + 32, :]

    fill_rows(row, 0, 32, src32, far32, to32)
    finish_tables(32, src32, far32, S_ref, A_ref)

    def rows_of(b):
        rows = to32[pl.ds(pl.multiple_of(b * 16, 16), 16), :].astype(bf16)
        to_ref[b] = rows
        return rows

    pad_targets(B_ref, rows_of)
    acc33[...] = jnp.zeros_like(acc33)
    ready()
    total = count_ref[0]
    off = jnp.int32(0)
    for q in range(128):
        a = pairs_ref[0, q]
        b = pairs_ref[1, q]
        off_ref[0, off] = a
        off_ref[1, off] = b
        off = off + jnp.where(jnp.logical_and(q < total, a != b), 1, 0)
    tile_group([(b, b, b) for b in range(32)], S_ref, A_ref, B_ref, acc33)

    def one_group(g, carry):
        items = []
        for u in range(OWN_GROUP // 2):
            q = g * (OWN_GROUP // 2) + u
            live = q < off
            a = jnp.where(live, off_ref[0, q], 0)
            b = jnp.where(live, off_ref[1, q], 0)
            items.append((a, jnp.where(live, a, 32), b))
            items.append((b, jnp.where(live, b, 32), a))
        tile_group(items, S_ref, A_ref, B_ref, acc33)
        return carry

    groups = lax.div(off + (OWN_GROUP // 2 - 1), OWN_GROUP // 2)
    lax.fori_loop(0, groups, one_group, 0)
    acc_ref[...] = acc33[0:32]


def start_kernel(
    count_ref, pairs_hbm, send_hbm, counts_hbm, links_hbm, pos_hbm, vel_hbm, sig_hbm, mass_hbm, dens_hbm,
    state_ref, m0, m1, m2, m3, acc_ref, to_ref,
    S_ref, A_ref, B_ref, src32, far32, to32, acc33, off_ref,
    pairs_ref, send_ref, counts_ref, links_ref, sig_ref, mass_ref, dens_ref, sem,
):
    copies = fetch(
        [
            (pairs_hbm, pairs_ref),
            (send_hbm, send_ref),
            (counts_hbm, counts_ref),
            (links_hbm, links_ref),
            (pos_hbm, state_ref.at[0:96]),
            (vel_hbm, state_ref.at[96:192]),
            (sig_hbm, sig_ref),
            (mass_hbm, mass_ref),
            (dens_hbm, dens_ref),
        ],
        sem,
    )
    for copy in copies:
        copy.wait()
    column = lanes_to_column(counts_ref[...].astype(f32))
    lane = lax.broadcasted_iota(jnp.int32, (32, 128), 1).astype(f32)
    mass = jnp.where(lane < column, mass_ref[...], 0.0)
    dens = dens_ref[...]
    square = dens * dens
    for k in range(6):
        state_ref[192 + 32 * k : 224 + 32 * k, :] = sig_ref[32 * k : 32 * k + 32, :] / square
    state_ref[384:416, :] = mass
    state_ref[416:448, :] = mass / dens
    state_ref[448:512, :] = jnp.zeros((64, 128), f32)
    gather_rims(send_ref, state_ref, (m0, m1, m2, m3))
    links = links_ref[...].astype(f32)
    for msg in (m0, m1, m2, m3):
        msg[224:228, 0:48] = links
    own_terms(
        count_ref, pairs_ref, off_ref, state_ref, acc_ref, to_ref, S_ref, A_ref, B_ref, src32, far32, to32, acc33,
        lambda: None,
    )


def own_kernel(
    count_ref, state_ref, pairs_hbm, acc_ref, to_ref,
    S_ref, A_ref, B_ref, src32, far32, to32, acc33, off_ref, pairs_ref, sem,
):
    copies = fetch([(pairs_hbm, pairs_ref)], sem)
    own_terms(
        count_ref, pairs_ref, off_ref, state_ref, acc_ref, to_ref, S_ref, A_ref, B_ref, src32, far32, to32, acc33,
        copies[0].wait,
    )


def cross_terms(send_ref, link_ref, back_ref, msgs, to_ref, S_ref, A_ref, B_ref, src32, far32, acc, ready):
    for face in range(4):
        def row(k, face=face):
            return msgs[face][16 * k : 16 * k + 16, :]

        fill_rows(row, 16 * face, 16, src32, far32, None)
    finish_tables(64, src32, far32, S_ref, A_ref)
    pad_targets(B_ref, lambda b: to_ref[b])
    acc[...] = jnp.zeros_like(acc)
    ready()

    depth, strip = parity("depth"), parity("strip")

    def one_group(g, carry):
        items = []
        for u in range(CROSS_GROUP // 4):
            q = g * (CROSS_GROUP // 4) + u
            back_d, back_s = 8 * (1 - depth), 16 + 8 * (1 - strip)
            for target, source in (
                (send_ref[0, link_ref[0, q]], 16 * depth + link_ref[1, q]),
                (send_ref[1, back_ref[back_d + 1, q]], 16 * (1 - depth) + back_ref[back_d, q]),
                (send_ref[2, link_ref[2, q]], 32 + 16 * strip + link_ref[3, q]),
                (send_ref[3, back_ref[back_s + 3, q]], 32 + 16 * (1 - strip) + back_ref[back_s + 2, q]),
            ):
                items.append((target, target, source))
        tile_group(items, S_ref, A_ref, B_ref, acc)
        return carry

    lax.fori_loop(0, 48 // (CROSS_GROUP // 4), one_group, 0)


def rates(state_ref, own_acc, acc, flag, c):
    def total(f):
        at = pl.ds(8 * c * 32 + f, 8, stride=32)
        return kernel_coef * (own_acc[at, :] + acc[at, :])

    def row(k):
        return state_ref[32 * k + 8 * c : 32 * k + 8 * c + 8, :]

    places = [row(k) for k in range(3)]
    motion = [row(3 + k) for k in range(3)]
    scaled = [row(6 + k) for k in range(6)]
    blade = (spin_rate * places[2], jnp.zeros_like(places[1]), -spin_rate * places[0])
    mass_sum = total(0)
    lever = [places[l] * mass_sum - total(1 + l) for l in range(3)]
    stress_sum = [total(4 + s) for s in range(6)]
    acceleration = []
    for k in range(3):
        force = jnp.zeros_like(mass_sum)
        for l in range(3):
            slot = voigt_index[k][l]
            force = force + scaled[slot] * lever[l]
            force = force + places[l] * stress_sum[slot]
        force = force - total(10 + k)
        force = force + blade_stiff * flag * (blade[k] - motion[k])
        if k == 2:
            force = force - gravity
        acceleration.append(force)
    volume_sum = total(13)
    motion_sum = [total(14 + k) for k in range(3)]
    place_sum = [total(17 + k) for k in range(3)]
    strain = []
    for comp, (a, b) in enumerate(voigt_pairs):
        rate = 0.5 * (places[b] * motion_sum[a] + places[a] * motion_sum[b])
        rate = rate - total(20 + comp)
        rate = rate - 0.5 * volume_sum * (motion[a] * places[b] + motion[b] * places[a])
        rate = rate + 0.5 * (motion[a] * place_sum[b] + motion[b] * place_sum[a])
        strain.append(rate)
    return acceleration, strain


def elastic_step(stress, strain, fraction):
    volumetric = strain[0] + strain[1] + strain[2]
    lame_first = bulk_mod - 2.0 * shear_mod / 3.0
    components = []
    for comp in range(6):
        change = 2.0 * shear_mod * strain[comp]
        if comp < 3:
            change = change + lame_first * volumetric
        components.append(stress[comp] + fraction * time_step * change)
    return components


def plastic_return(components, plastic, cohesion):
    for _ in range(RETURN_ITERS):
        mean = (components[0] + components[1] + components[2]) / 3.0
        dev = [components[k] - mean for k in range(3)] + list(components[3:])
        second = 0.5 * (dev[0] * dev[0] + dev[1] * dev[1] + dev[2] * dev[2])
        second = second + dev[3] * dev[3] + dev[4] * dev[4] + dev[5] * dev[5]
        shear = jnp.sqrt(second)
        limit = cohesion * (1.0 + plastic / (plastic + harden_scale))
        excess = jnp.maximum(shear + friction * 3.0 * mean - limit, 0.0)
        multiplier = (relax_rate / (shear_mod + 9.0 * bulk_mod * friction * friction + harden_mod)) * excess
        shrink = jnp.maximum(1.0 - shear_mod * multiplier / jnp.maximum(shear, tau_floor), 0.0)
        mean = mean - 3.0 * bulk_mod * friction * multiplier
        components = [dev[k] * shrink + mean for k in range(3)] + [dev[k] * shrink for k in range(3, 6)]
        plastic = plastic + multiplier
    return components, plastic


def contact_column(contact_ref):
    rows = lax.broadcasted_iota(jnp.int32, (32, 16), 0)
    hit = jnp.where(contact_ref[...] == rows, 1.0, 0.0)
    return jnp.sum(hit, axis=1, keepdims=True)


def half_kernel(
    state_ref, own_acc, to_ref,
    m0, m1, m2, m3, sig_ref, plastic_ref, cohesion_ref, dens_ref, send_hbm, link_hbm, contact_hbm,
    next_ref, n0, n1, n2, n3, back_out,
    S_ref, A_ref, B_ref, src32, far32, acc, send_ref, link_ref, contact_ref, back_ref, sem,
):
    for m, msg in enumerate((m0, m1, m2, m3)):
        back_out[8 * m : 8 * m + 8, :] = msg[224:232, :].astype(jnp.int32)
    copies = fetch(
        [(back_out, back_ref), (send_hbm, send_ref), (link_hbm, link_ref), (contact_hbm, contact_ref)], sem
    )

    def ready():
        for copy in copies:
            copy.wait()

    cross_terms(
        send_ref, link_ref, back_ref, (m0, m1, m2, m3), to_ref, S_ref, A_ref, B_ref, src32, far32, acc, ready
    )
    flags = contact_column(contact_ref)
    own2 = own_acc.reshape(1024, 128)
    acc2 = acc.reshape(1024, 128)
    for c in range(4):
        at = slice(8 * c, 8 * c + 8)
        acceleration, strain = rates(state_ref, own2, acc2, flags[at], c)
        stress = [sig_ref[32 * k + 8 * c : 32 * k + 8 * c + 8, :] for k in range(6)]
        trial = elastic_step(stress, strain, 0.5)
        for k in range(3):
            x = slice(32 * k + 8 * c, 32 * k + 8 * c + 8)
            v = slice(96 + 32 * k + 8 * c, 96 + 32 * k + 8 * c + 8)
            motion = state_ref[v, :]
            next_ref[x, :] = state_ref[x, :] + 0.5 * time_step * motion
            next_ref[v, :] = motion + 0.5 * time_step * acceleration[k]
        for k in range(6):
            next_ref[192 + 32 * k + 8 * c : 200 + 32 * k + 8 * c, :] = trial[k]
    trial = [next_ref[192 + 32 * k : 224 + 32 * k, :] for k in range(6)]
    half_stress, _ = plastic_return(trial, plastic_ref[...], cohesion_ref[...])
    dens = dens_ref[...]
    square = dens * dens
    for k in range(6):
        next_ref[192 + 32 * k : 224 + 32 * k, :] = half_stress[k] / square
    next_ref[384:512, :] = state_ref[384:512, :]
    gather_rims(send_ref, next_ref, (n0, n1, n2, n3))


def last_kernel(
    state_ref, own_acc, to_ref,
    m0, m1, m2, m3, sig_ref, plastic_ref, cohesion_ref, pos_ref, vel_ref, back_vmem,
    send_hbm, link_hbm, contact_hbm, counts_hbm,
    pos_out, vel_out, sig_out, plastic_out,
    S_ref, A_ref, B_ref, src32, far32, acc, send_ref, link_ref, contact_ref, back_ref, counts_ref, sem,
):
    copies = fetch(
        [
            (back_vmem, back_ref),
            (send_hbm, send_ref),
            (link_hbm, link_ref),
            (contact_hbm, contact_ref),
            (counts_hbm, counts_ref),
        ],
        sem,
    )

    def ready():
        for copy in copies:
            copy.wait()

    cross_terms(
        send_ref, link_ref, back_ref, (m0, m1, m2, m3), to_ref, S_ref, A_ref, B_ref, src32, far32, acc, ready
    )
    flags = contact_column(contact_ref)
    column = lanes_to_column(counts_ref[...].astype(f32))
    lane = lax.broadcasted_iota(jnp.int32, (8, 128), 1).astype(f32)
    own2 = own_acc.reshape(1024, 128)
    acc2 = acc.reshape(1024, 128)
    for c in range(4):
        at = slice(8 * c, 8 * c + 8)
        keep = lane < column[at]
        acceleration, strain = rates(state_ref, own2, acc2, flags[at], c)
        stress = [sig_ref[32 * k + 8 * c : 32 * k + 8 * c + 8, :] for k in range(6)]
        trial = elastic_step(stress, strain, 1.0)
        for k in range(3):
            x = slice(32 * k + 8 * c, 32 * k + 8 * c + 8)
            v = slice(96 + 32 * k + 8 * c, 96 + 32 * k + 8 * c + 8)
            pos_out[x, :] = jnp.where(keep, pos_ref[x, :] + time_step * state_ref[v, :], 0.0)
            vel_out[x, :] = jnp.where(keep, vel_ref[x, :] + time_step * acceleration[k], 0.0)
        for k in range(6):
            sig_out[32 * k + 8 * c : 32 * k + 8 * c + 8, :] = trial[k]
    keep = lax.broadcasted_iota(jnp.int32, (32, 128), 1).astype(f32) < column
    trial = [sig_out[32 * k : 32 * k + 32, :] for k in range(6)]
    new_stress, new_plastic = plastic_return(trial, plastic_ref[...], cohesion_ref[...])
    for k in range(6):
        sig_out[32 * k : 32 * k + 32, :] = jnp.where(keep, new_stress[k], 0.0)
    plastic_out[...] = jnp.where(keep, new_plastic, 0.0)


SMEM = pl.BlockSpec(memory_space=pltpu.SMEM)
VMEM = pl.BlockSpec(memory_space=pltpu.VMEM)
HBM = pl.BlockSpec(memory_space=pltpu.HBM)
params = pltpu.CompilerParams(vmem_limit_bytes=48 * 1024 * 1024)


def in_hbm(value):
    return pltpu.with_memory_space_constraint(value, pltpu.HBM)


def shape(*dims, dtype=f32):
    return jax.ShapeDtypeStruct(dims, dtype)


def tables(count):
    return [
        pltpu.VMEM((count, 64, 128), bf16),
        pltpu.VMEM((count // 8, 128, 128), bf16),
        pltpu.VMEM((32, 240, 128), bf16),
        pltpu.VMEM((count * 32, 128), f32),
        pltpu.VMEM((count * 16, 128), f32),
    ]


def call(kernel, smem, vmem, hbm, outs, scratch):
    return pl.pallas_call(
        kernel,
        out_shape=outs,
        in_specs=[SMEM] * len(smem) + [VMEM] * len(vmem) + [HBM] * len(hbm),
        out_specs=[VMEM] * len(outs),
        scratch_shapes=scratch,
        compiler_params=params,
    )(*smem, *vmem, *hbm)


def shards(
    position, velocity, stress, plastic, particle_mass, density, cohesion,
    counts, block_pairs, pair_count, send_lists, cross_links, contact,
):
    pos = position.reshape(96, 128)
    vel = velocity.reshape(96, 128)
    sig = stress.reshape(192, 128)
    plastic_now = plastic.reshape(32, 128)
    mass = particle_mass.reshape(32, 128)
    dens = density.reshape(32, 128)
    cohesion_now = cohesion.reshape(32, 128)
    counts_now = counts.reshape(1, 32)
    pairs = jnp.swapaxes(block_pairs.reshape(128, 2), 0, 1)
    total = pair_count.reshape(1)
    send = send_lists.reshape(4, 16)
    links = jnp.swapaxes(cross_links.reshape(2, 48, 2), 1, 2).reshape(4, 48)
    touched = contact.reshape(1, 16)

    rim = [shape(16 * ROWS, 128)] * 4
    own_outs = [shape(32, 32, 128), shape(32, 16, 128, dtype=bf16)]
    own_scratch = tables(32) + [
        pltpu.VMEM((512, 128), f32),
        pltpu.VMEM((33, 32, 128), f32),
        pltpu.SMEM((2, 128), jnp.int32),
        pltpu.SMEM((2, 128), jnp.int32),
    ]
    state, *msgs, own_acc, to_side = call(
        start_kernel,
        [total],
        [],
        [in_hbm(x) for x in (pairs, send, counts_now, links, pos, vel, sig, mass, dens)],
        [shape(512, 128)] + rim + own_outs,
        own_scratch
        + [
            pltpu.SMEM((4, 16), jnp.int32),
            pltpu.VMEM((1, 32), jnp.int32),
            pltpu.VMEM((4, 48), jnp.int32),
            pltpu.VMEM((192, 128), f32),
            pltpu.VMEM((32, 128), f32),
            pltpu.VMEM((32, 128), f32),
            pltpu.SemaphoreType.DMA((9,)),
        ],
    )

    def swap(msgs):
        return (
            swap_pairs(msgs[0], "depth", 0, False),
            swap_pairs(msgs[1], "depth", 1, False),
            swap_pairs(msgs[2], "strip", 0, True),
            swap_pairs(msgs[3], "strip", 1, True),
        )

    cross_scratch = tables(64) + [
        pltpu.VMEM((32, 32, 128), f32),
        pltpu.SMEM((4, 16), jnp.int32),
        pltpu.SMEM((4, 48), jnp.int32),
        pltpu.VMEM((1, 16), jnp.int32),
        pltpu.SMEM((32, 128), jnp.int32),
    ]
    lists = [in_hbm(x) for x in (send, links, touched)]
    far = swap(msgs)
    state, *msgs, back = call(
        half_kernel,
        [],
        [state, own_acc, to_side, *far, sig, plastic_now, cohesion_now, dens],
        lists,
        [shape(512, 128)] + rim + [shape(32, 128, dtype=jnp.int32)],
        cross_scratch + [pltpu.SemaphoreType.DMA((4,))],
    )
    far = swap(msgs)
    own_acc, to_side = call(
        own_kernel, [total], [state], [in_hbm(pairs)], own_outs, own_scratch + [pltpu.SemaphoreType.DMA((1,))]
    )
    new_pos, new_vel, new_sig, new_plastic = call(
        last_kernel,
        [],
        [state, own_acc, to_side, *far, sig, plastic_now, cohesion_now, pos, vel, back],
        lists + [in_hbm(counts_now)],
        [shape(96, 128), shape(96, 128), shape(192, 128), shape(32, 128)],
        cross_scratch + [pltpu.VMEM((1, 32), jnp.int32), pltpu.SemaphoreType.DMA((5,))],
    )
    return (
        new_pos.reshape(position.shape),
        new_vel.reshape(velocity.shape),
        new_sig.reshape(stress.shape),
        new_plastic.reshape(plastic.shape),
    )


def solution(mesh):
    def spec(rank):
        return P("strip", "depth", *([None] * (rank - 2)))

    return jax.shard_map(
        shards,
        mesh=mesh,
        in_specs=tuple(spec(r) for r in (5, 5, 5, 4, 4, 4, 4, 3, 4, 2, 4, 5, 3)),
        out_specs=tuple(spec(r) for r in (5, 5, 5, 4)),
        check_vma=False,
    )
```

```python
import functools

import jax
import jax.numpy as jnp
from jax import lax
from jax.experimental import pallas as pl
from jax.experimental.pallas import tpu as pltpu
from jax.sharding import PartitionSpec as P

RETURN_ITERS = 4
ROWS = 16
OWN_GROUP = 64
CROSS_GROUP = 96

smooth_len = 1.5
kernel_coef = -105.0 / (3.141592653589793 * 1.5**5)
time_step = 0.25
gravity = 1.0
spin_rate = 2.0
blade_stiff = 4.0
bulk_mod = 2.0
shear_mod = 1.5
friction = 0.25
harden_scale = 0.05
harden_mod = 0.5
relax_rate = 0.7
tau_floor = 0.5
voigt_index = ((0, 3, 5), (3, 1, 4), (5, 4, 2))
voigt_pairs = ((0, 0), (1, 1), (2, 2), (0, 1), (1, 2), (0, 2))
bf16 = jnp.bfloat16
f32 = jnp.float32


def swap_pairs(value, axis, odd, closed):
    count = lax.axis_size(axis)
    pairs = []
    for i in range(odd, count, 2):
        j = (i + 1) % count
        if j == i + 1 or closed:
            pairs += [(i, j), (j, i)]
    return lax.ppermute(value, axis, pairs)


def parity(axis):
    return lax.rem(lax.axis_index(axis), 2)


def halves(value):
    high = value.astype(bf16).astype(f32)
    return high, value - high


def source_rows(row):
    places = [row(k) for k in range(3)]
    motion = [row(3 + k) for k in range(3)]
    scaled = [row(6 + k) for k in range(6)]
    mass, volume = row(12), row(13)
    out = [mass]
    out += [mass * x for x in places]
    out += [mass * s for s in scaled]
    for k in range(3):
        dotted = scaled[voigt_index[k][0]] * places[0]
        dotted = dotted + scaled[voigt_index[k][1]] * places[1]
        dotted = dotted + scaled[voigt_index[k][2]] * places[2]
        out.append(mass * dotted)
    out.append(volume)
    out += [volume * v for v in motion]
    out += [volume * x for x in places]
    for a, b in voigt_pairs:
        out.append(volume * (0.5 * (motion[a] * places[b] + motion[b] * places[a])))
    return out


def distance_rows(row):
    places = [row(k) * (1.0 / smooth_len) for k in range(3)]
    square = places[0] * places[0] + places[1] * places[1] + places[2] * places[2]
    high, low = zip(*[halves(x) for x in places])
    n0, rest = halves(square)
    n1, n2 = halves(rest)
    one = jnp.ones_like(square)
    zero = jnp.zeros_like(square)
    from_side = [-2.0 * x for x in high + low + high] + [n0, n1, n2, one, one, one, zero]
    to_side = list(high + high + low) + [one, one, one, n0, n1, n2, zero]
    return from_side, to_side


def fill_rows(row, base, count, src32, far32, to32):
    for f, value in enumerate(source_rows(row)):
        src32[pl.ds(base * 32 + f, count, stride=32), :] = value
    from_side, to_side = distance_rows(row)
    for f, value in enumerate(from_side):
        far32[pl.ds(base * 16 + f, count, stride=16), :] = value
    if to32 is not None:
        for f, value in enumerate(to_side):
            to32[pl.ds(base * 16 + f, count, stride=16), :] = value


def finish_tables(count, src32, far32, S_ref, A_ref):
    def eight(i, carry):
        flipped = far32[pl.ds(pl.multiple_of(i * 128, 128), 128), :].T
        A_ref[i] = flipped.astype(bf16)
        for u in range(8):
            b = i * 8 + u
            value = src32[pl.ds(pl.multiple_of(b * 32, 32), 32), :]
            high = value.astype(bf16)
            S_ref[b, 0:32, :] = high
            S_ref[b, 32:64, :] = (value - high.astype(f32)).astype(bf16)
        return carry

    lax.fori_loop(0, count // 8, eight, 0)


def pad_targets(B_ref, to32):
    def one(b, carry):
        B_ref[b, 0:112, :] = jnp.zeros((112, 128), bf16)
        B_ref[b, 128:240, :] = jnp.zeros((112, 128), bf16)
        B_ref[b, 112:128, :] = to32[pl.ds(pl.multiple_of(b * 16, 16), 16), :].astype(bf16)
        return carry

    lax.fori_loop(0, 32, one, 0)


def closeness_cubed(square):
    square = jnp.maximum(square, 1e-30)
    close = jnp.maximum(1.0 - square * lax.rsqrt(square), 0.0)
    return close * close * close


def tile_group(items, S_ref, A_ref, B_ref, acc_ref):
    outs = []
    for target, into, source in items:
        if isinstance(source, int):
            start, octet = 112 - 16 * (source % 8), source // 8
        else:
            start = pl.multiple_of(112 - 16 * lax.rem(source, 8), 16)
            octet = lax.div(source, 8)
        square = jnp.dot(
            A_ref[octet], B_ref[target, pl.ds(start, 128), :], preferred_element_type=f32
        )
        kernel = closeness_cubed(square)
        high = kernel.astype(bf16)
        low = (kernel - high.astype(f32)).astype(bf16)
        rows = S_ref[source]
        both = jnp.dot(
            jnp.concatenate([rows, rows], 1),
            jnp.concatenate([high, low], 0),
            preferred_element_type=f32,
        )
        outs.append((into, both[:32] + both[32:]))
    for into, value in outs:
        acc_ref[into] += value


def lanes_to_column(values):
    n = values.shape[1]
    rows = lax.broadcasted_iota(jnp.int32, (n, n), 0)
    cols = lax.broadcasted_iota(jnp.int32, (n, n), 1)
    return jnp.sum(jnp.where(rows == cols, values, 0.0), axis=1, keepdims=True)


def gather_rims(send_ref, state_ref, msgs):
    depth, strip = parity("depth"), parity("strip")
    for m, face in enumerate((depth, 1 - depth, 2 + strip, 3 - strip)):
        for slot in range(16):
            block = send_ref[face, slot]
            msgs[m][pl.ds(slot, ROWS, stride=16), :] = state_ref[
                pl.ds(block, ROWS, stride=32), :
            ]


def fetch(pairs, sem):
    copies = [pltpu.make_async_copy(a, b, sem.at[i]) for i, (a, b) in enumerate(pairs)]
    for copy in copies:
        copy.start()
    return copies


def own_kernel(
    state_ref, count_ref, pairs_hbm, acc_ref, B_ref,
    S_ref, A_ref, src32, far32, to32, acc33, off_ref, pairs_ref, sem,
):
    copies = fetch([(pairs_hbm, pairs_ref)], sem)

    def row(k):
        return state_ref[32 * k : 32 * k + 32, :]

    fill_rows(row, 0, 32, src32, far32, to32)
    finish_tables(32, src32, far32, S_ref, A_ref)

    pad_targets(B_ref, to32)
    acc33[...] = jnp.zeros_like(acc33)
    for copy in copies:
        copy.wait()
    total = count_ref[0, 0]
    off = jnp.int32(0)
    for q in range(128):
        a = pairs_ref[0, q]
        b = pairs_ref[1, q]
        off_ref[0, off] = a
        off_ref[1, off] = b
        off = off + jnp.where(jnp.logical_and(q < total, a != b), 1, 0)
    tile_group([(b, b, b) for b in range(32)], S_ref, A_ref, B_ref, acc33)

    def one_group(g, carry):
        items = []
        for u in range(OWN_GROUP // 2):
            q = g * (OWN_GROUP // 2) + u
            live = q < off
            a = jnp.where(live, off_ref[0, q], 0)
            b = jnp.where(live, off_ref[1, q], 0)
            items.append((a, jnp.where(live, a, 32), b))
            items.append((b, jnp.where(live, b, 32), a))
        tile_group(items, S_ref, A_ref, B_ref, acc33)
        return carry

    groups = lax.div(off + (OWN_GROUP // 2 - 1), OWN_GROUP // 2)
    lax.fori_loop(0, groups, one_group, 0)
    acc_ref[...] = acc33[0:32]


def start_kernel(
    send_hbm, counts_hbm, links_hbm, pos_hbm, vel_hbm, sig_hbm, mass_hbm, dens_hbm,
    state_ref, m0, m1, m2, m3, send_ref, counts_ref, links_ref, sig_ref, mass_ref, dens_ref, sem,
):
    copies = fetch(
        [
            (send_hbm, send_ref),
            (counts_hbm, counts_ref),
            (links_hbm, links_ref),
            (pos_hbm, state_ref.at[0:96]),
            (vel_hbm, state_ref.at[96:192]),
            (sig_hbm, sig_ref),
            (mass_hbm, mass_ref),
            (dens_hbm, dens_ref),
        ],
        sem,
    )
    for copy in copies:
        copy.wait()
    column = lanes_to_column(counts_ref[...].astype(f32))
    lane = lax.broadcasted_iota(jnp.int32, (32, 128), 1).astype(f32)
    mass = jnp.where(lane < column, mass_ref[...], 0.0)
    dens = dens_ref[...]
    square = dens * dens
    for k in range(6):
        state_ref[192 + 32 * k : 224 + 32 * k, :] = sig_ref[32 * k : 32 * k + 32, :] / square
    state_ref[384:416, :] = mass
    state_ref[416:448, :] = mass / dens
    state_ref[448:512, :] = jnp.zeros((64, 128), f32)
    gather_rims(send_ref, state_ref, (m0, m1, m2, m3))
    links = links_ref[...].astype(f32)
    for msg in (m0, m1, m2, m3):
        msg[224:228, 0:48] = links


def cross_terms(send_ref, link_ref, back_ref, msgs, own_acc, S_ref, A_ref, B_ref, src32, far32, acc, ready):
    for face in range(4):
        def row(k, face=face):
            return msgs[face][16 * k : 16 * k + 16, :]

        fill_rows(row, 16 * face, 16, src32, far32, None)
    finish_tables(64, src32, far32, S_ref, A_ref)
    acc[...] = own_acc[...]
    ready()

    depth, strip = parity("depth"), parity("strip")

    def one_group(g, carry):
        items = []
        for u in range(CROSS_GROUP // 4):
            q = g * (CROSS_GROUP // 4) + u
            back_d, back_s = 8 * (1 - depth), 16 + 8 * (1 - strip)
            for target, source in (
                (send_ref[0, link_ref[0, q]], 16 * depth + link_ref[1, q]),
                (send_ref[1, back_ref[back_d + 1, q]], 16 * (1 - depth) + back_ref[back_d, q]),
                (send_ref[2, link_ref[2, q]], 32 + 16 * strip + link_ref[3, q]),
                (send_ref[3, back_ref[back_s + 3, q]], 32 + 16 * (1 - strip) + back_ref[back_s + 2, q]),
            ):
                items.append((target, target, source))
        tile_group(items, S_ref, A_ref, B_ref, acc)
        return carry

    lax.fori_loop(0, 48 // (CROSS_GROUP // 4), one_group, 0)


def rates(state_ref, acc, flag, c):
    def total(f):
        at = pl.ds(8 * c * 32 + f, 8, stride=32)
        return kernel_coef * acc[at, :]

    def row(k):
        return state_ref[32 * k + 8 * c : 32 * k + 8 * c + 8, :]

    places = [row(k) for k in range(3)]
    motion = [row(3 + k) for k in range(3)]
    scaled = [row(6 + k) for k in range(6)]
    blade = (spin_rate * places[2], jnp.zeros_like(places[1]), -spin_rate * places[0])
    mass_sum = total(0)
    lever = [places[l] * mass_sum - total(1 + l) for l in range(3)]
    stress_sum = [total(4 + s) for s in range(6)]
    acceleration = []
    for k in range(3):
        force = jnp.zeros_like(mass_sum)
        for l in range(3):
            slot = voigt_index[k][l]
            force = force + scaled[slot] * lever[l]
            force = force + places[l] * stress_sum[slot]
        force = force - total(10 + k)
        force = force + blade_stiff * flag * (blade[k] - motion[k])
        if k == 2:
            force = force - gravity
        acceleration.append(force)
    volume_sum = total(13)
    motion_sum = [total(14 + k) for k in range(3)]
    place_sum = [total(17 + k) for k in range(3)]
    strain = []
    for comp, (a, b) in enumerate(voigt_pairs):
        rate = 0.5 * (places[b] * motion_sum[a] + places[a] * motion_sum[b])
        rate = rate - total(20 + comp)
        rate = rate - 0.5 * volume_sum * (motion[a] * places[b] + motion[b] * places[a])
        rate = rate + 0.5 * (motion[a] * place_sum[b] + motion[b] * place_sum[a])
        strain.append(rate)
    return acceleration, strain


def elastic_step(stress, strain, fraction):
    volumetric = strain[0] + strain[1] + strain[2]
    lame_first = bulk_mod - 2.0 * shear_mod / 3.0
    components = []
    for comp in range(6):
        change = 2.0 * shear_mod * strain[comp]
        if comp < 3:
            change = change + lame_first * volumetric
        components.append(stress[comp] + fraction * time_step * change)
    return components


def plastic_return(components, plastic, cohesion):
    for _ in range(RETURN_ITERS):
        mean = (components[0] + components[1] + components[2]) / 3.0
        dev = [components[k] - mean for k in range(3)] + list(components[3:])
        second = 0.5 * (dev[0] * dev[0] + dev[1] * dev[1] + dev[2] * dev[2])
        second = second + dev[3] * dev[3] + dev[4] * dev[4] + dev[5] * dev[5]
        shear = jnp.sqrt(second)
        limit = cohesion * (1.0 + plastic / (plastic + harden_scale))
        excess = jnp.maximum(shear + friction * 3.0 * mean - limit, 0.0)
        multiplier = (relax_rate / (shear_mod + 9.0 * bulk_mod * friction * friction + harden_mod)) * excess
        shrink = jnp.maximum(1.0 - shear_mod * multiplier / jnp.maximum(shear, tau_floor), 0.0)
        mean = mean - 3.0 * bulk_mod * friction * multiplier
        components = [dev[k] * shrink + mean for k in range(3)] + [dev[k] * shrink for k in range(3, 6)]
        plastic = plastic + multiplier
    return components, plastic


def contact_column(contact_ref):
    rows = lax.broadcasted_iota(jnp.int32, (32, 16), 0)
    hit = jnp.where(contact_ref[...] == rows, 1.0, 0.0)
    return jnp.sum(hit, axis=1, keepdims=True)


def half_kernel(
    state_ref, own_acc, B_ref,
    m0, m1, m2, m3, sig_hbm, plastic_hbm, cohesion_hbm, dens_hbm, send_hbm, link_hbm, contact_hbm,
    next_ref, n0, n1, n2, n3, back_out,
    S_ref, A_ref, src32, far32, acc, send_ref, link_ref, contact_ref, back_ref,
    sig_ref, plastic_ref, cohesion_ref, dens_ref, sem,
):
    for m, msg in enumerate((m0, m1, m2, m3)):
        back_out[8 * m : 8 * m + 8, :] = msg[224:232, :].astype(jnp.int32)
    copies = fetch(
        [
            (back_out, back_ref),
            (send_hbm, send_ref),
            (link_hbm, link_ref),
            (contact_hbm, contact_ref),
            (sig_hbm, sig_ref),
            (plastic_hbm, plastic_ref),
            (cohesion_hbm, cohesion_ref),
            (dens_hbm, dens_ref),
        ],
        sem,
    )

    def ready():
        for copy in copies:
            copy.wait()

    cross_terms(
        send_ref, link_ref, back_ref, (m0, m1, m2, m3), own_acc, S_ref, A_ref, B_ref, src32, far32, acc, ready
    )
    flags = contact_column(contact_ref)
    acc2 = acc.reshape(1024, 128)
    for c in range(4):
        at = slice(8 * c, 8 * c + 8)
        acceleration, strain = rates(state_ref, acc2, flags[at], c)
        stress = [sig_ref[32 * k + 8 * c : 32 * k + 8 * c + 8, :] for k in range(6)]
        trial = elastic_step(stress, strain, 0.5)
        for k in range(3):
            x = slice(32 * k + 8 * c, 32 * k + 8 * c + 8)
            v = slice(96 + 32 * k + 8 * c, 96 + 32 * k + 8 * c + 8)
            motion = state_ref[v, :]
            next_ref[x, :] = state_ref[x, :] + 0.5 * time_step * motion
            next_ref[v, :] = motion + 0.5 * time_step * acceleration[k]
        for k in range(6):
            next_ref[192 + 32 * k + 8 * c : 200 + 32 * k + 8 * c, :] = trial[k]
    trial = [next_ref[192 + 32 * k : 224 + 32 * k, :] for k in range(6)]
    half_stress, _ = plastic_return(trial, plastic_ref[...], cohesion_ref[...])
    dens = dens_ref[...]
    square = dens * dens
    for k in range(6):
        next_ref[192 + 32 * k : 224 + 32 * k, :] = half_stress[k] / square
    next_ref[384:512, :] = state_ref[384:512, :]
    gather_rims(send_ref, next_ref, (n0, n1, n2, n3))


def last_kernel(
    state_ref, own_acc, B_ref,
    m0, m1, m2, m3, back_vmem, sig_hbm, plastic_hbm, cohesion_hbm, pos_hbm, vel_hbm,
    send_hbm, link_hbm, contact_hbm, counts_hbm,
    pos_out, vel_out, sig_out, plastic_out,
    S_ref, A_ref, src32, far32, acc, send_ref, link_ref, contact_ref, back_ref,
    sig_ref, plastic_ref, cohesion_ref, pos_ref, vel_ref, counts_ref, sem,
):
    copies = fetch(
        [
            (back_vmem, back_ref),
            (send_hbm, send_ref),
            (link_hbm, link_ref),
            (contact_hbm, contact_ref),
            (counts_hbm, counts_ref),
            (sig_hbm, sig_ref),
            (plastic_hbm, plastic_ref),
            (cohesion_hbm, cohesion_ref),
            (pos_hbm, pos_ref),
            (vel_hbm, vel_ref),
        ],
        sem,
    )

    def ready():
        for copy in copies:
            copy.wait()

    cross_terms(
        send_ref, link_ref, back_ref, (m0, m1, m2, m3), own_acc, S_ref, A_ref, B_ref, src32, far32, acc, ready
    )
    flags = contact_column(contact_ref)
    column = lanes_to_column(counts_ref[...].astype(f32))
    lane = lax.broadcasted_iota(jnp.int32, (8, 128), 1).astype(f32)
    acc2 = acc.reshape(1024, 128)
    for c in range(4):
        at = slice(8 * c, 8 * c + 8)
        keep = lane < column[at]
        acceleration, strain = rates(state_ref, acc2, flags[at], c)
        stress = [sig_ref[32 * k + 8 * c : 32 * k + 8 * c + 8, :] for k in range(6)]
        trial = elastic_step(stress, strain, 1.0)
        for k in range(3):
            x = slice(32 * k + 8 * c, 32 * k + 8 * c + 8)
            v = slice(96 + 32 * k + 8 * c, 96 + 32 * k + 8 * c + 8)
            pos_out[x, :] = jnp.where(keep, pos_ref[x, :] + time_step * state_ref[v, :], 0.0)
            vel_out[x, :] = jnp.where(keep, vel_ref[x, :] + time_step * acceleration[k], 0.0)
        for k in range(6):
            sig_out[32 * k + 8 * c : 32 * k + 8 * c + 8, :] = trial[k]
    keep = lax.broadcasted_iota(jnp.int32, (32, 128), 1).astype(f32) < column
    trial = [sig_out[32 * k : 32 * k + 32, :] for k in range(6)]
    new_stress, new_plastic = plastic_return(trial, plastic_ref[...], cohesion_ref[...])
    for k in range(6):
        sig_out[32 * k : 32 * k + 32, :] = jnp.where(keep, new_stress[k], 0.0)
    plastic_out[...] = jnp.where(keep, new_plastic, 0.0)


VMEM = pl.BlockSpec(memory_space=pltpu.VMEM)
HBM = pl.BlockSpec(memory_space=pltpu.HBM)
params = pltpu.CompilerParams(vmem_limit_bytes=48 * 1024 * 1024)


def in_hbm(value):
    return pltpu.with_memory_space_constraint(value, pltpu.HBM)


def shape(*dims, dtype=f32):
    return jax.ShapeDtypeStruct(dims, dtype)


def tables(count):
    return [
        pltpu.VMEM((count, 64, 128), bf16),
        pltpu.VMEM((count // 8, 128, 128), bf16),
        pltpu.VMEM((count * 32, 128), f32),
        pltpu.VMEM((count * 16, 128), f32),
    ]


def call(kernel, vmem, hbm, outs, scratch):
    return pl.pallas_call(
        kernel,
        out_shape=outs,
        in_specs=[VMEM] * len(vmem) + [HBM] * len(hbm),
        out_specs=[VMEM] * len(outs),
        scratch_shapes=scratch,
        compiler_params=params,
    )(*vmem, *hbm)


def shards(
    position, velocity, stress, plastic, particle_mass, density, cohesion,
    counts, block_pairs, pair_count, send_lists, cross_links, contact,
):
    pos = position.reshape(96, 128)
    vel = velocity.reshape(96, 128)
    sig = stress.reshape(192, 128)
    plastic_now = plastic.reshape(32, 128)
    mass = particle_mass.reshape(32, 128)
    dens = density.reshape(32, 128)
    cohesion_now = cohesion.reshape(32, 128)
    counts_now = counts.reshape(1, 32)
    pairs = jnp.swapaxes(block_pairs.reshape(128, 2), 0, 1)
    send = send_lists.reshape(4, 16)
    links = jnp.swapaxes(cross_links.reshape(2, 48, 2), 1, 2).reshape(4, 48)
    touched = contact.reshape(1, 16)

    rim = [shape(16 * ROWS, 128)] * 4
    def own(state):
        return call(
            own_kernel,
            [state, pair_count],
            [in_hbm(pairs)],
            [shape(32, 32, 128), shape(32, 240, 128, dtype=bf16)],
            tables(32)
            + [
                pltpu.VMEM((512, 128), f32),
                pltpu.VMEM((33, 32, 128), f32),
                pltpu.SMEM((2, 128), jnp.int32),
                pltpu.SMEM((2, 128), jnp.int32),
                pltpu.SemaphoreType.DMA((1,)),
            ],
        )

    state, *msgs = call(
        start_kernel,
        [],
        [in_hbm(x) for x in (send, counts_now, links, pos, vel, sig, mass, dens)],
        [shape(512, 128)] + rim,
        [
            pltpu.SMEM((4, 16), jnp.int32),
            pltpu.VMEM((1, 32), jnp.int32),
            pltpu.VMEM((4, 48), jnp.int32),
            pltpu.VMEM((192, 128), f32),
            pltpu.VMEM((32, 128), f32),
            pltpu.VMEM((32, 128), f32),
            pltpu.SemaphoreType.DMA((8,)),
        ],
    )

    def swap(msgs):
        strips = [swap_pairs(msgs[2 + odd], "strip", odd, True) for odd in range(2)]
        depths = [swap_pairs(msgs[odd], "depth", odd, False) for odd in range(2)]
        return depths + strips

    cross_scratch = tables(64) + [
        pltpu.VMEM((32, 32, 128), f32),
        pltpu.SMEM((4, 16), jnp.int32),
        pltpu.SMEM((4, 48), jnp.int32),
        pltpu.VMEM((1, 16), jnp.int32),
        pltpu.SMEM((32, 128), jnp.int32),
        pltpu.VMEM((192, 128), f32),
        pltpu.VMEM((32, 128), f32),
        pltpu.VMEM((32, 128), f32),
    ]
    fields = [in_hbm(x) for x in (sig, plastic_now, cohesion_now)]
    lists = [in_hbm(x) for x in (send, links, touched)]
    far = swap(msgs)
    own_acc, to_side = own(state)
    state, *msgs, back = call(
        half_kernel,
        [state, own_acc, to_side, *far],
        fields + [in_hbm(dens)] + lists,
        [shape(512, 128)] + rim + [shape(32, 128, dtype=jnp.int32)],
        cross_scratch + [pltpu.VMEM((32, 128), f32), pltpu.SemaphoreType.DMA((8,))],
    )
    far = swap(msgs)
    own_acc, to_side = own(state)
    new_pos, new_vel, new_sig, new_plastic = call(
        last_kernel,
        [state, own_acc, to_side, *far, back],
        fields + [in_hbm(pos), in_hbm(vel)] + lists + [in_hbm(counts_now)],
        [shape(96, 128), shape(96, 128), shape(192, 128), shape(32, 128)],
        cross_scratch
        + [
            pltpu.VMEM((96, 128), f32),
            pltpu.VMEM((96, 128), f32),
            pltpu.VMEM((1, 32), jnp.int32),
            pltpu.SemaphoreType.DMA((10,)),
        ],
    )
    return (
        new_pos.reshape(position.shape),
        new_vel.reshape(velocity.shape),
        new_sig.reshape(stress.shape),
        new_plastic.reshape(plastic.shape),
    )


def solution(mesh):
    def spec(rank):
        return P("strip", "depth", *([None] * (rank - 2)))

    return jax.shard_map(
        shards,
        mesh=mesh,
        in_specs=tuple(spec(r) for r in (5, 5, 5, 4, 4, 4, 4, 3, 4, 2, 4, 5, 3)),
        out_specs=tuple(spec(r) for r in (5, 5, 5, 4)),
        check_vma=False,
    )
```

```python
import functools

import jax
import jax.numpy as jnp
from jax import lax
from jax.experimental import pallas as pl
from jax.experimental.pallas import tpu as pltpu
from jax.sharding import PartitionSpec as P

RETURN_ITERS = 4
ROWS = 16
OWN_GROUP = 64
CROSS_GROUP = 192

smooth_len = 1.5
kernel_coef = -105.0 / (3.141592653589793 * 1.5**5)
time_step = 0.25
gravity = 1.0
spin_rate = 2.0
blade_stiff = 4.0
bulk_mod = 2.0
shear_mod = 1.5
friction = 0.25
harden_scale = 0.05
harden_mod = 0.5
relax_rate = 0.7
tau_floor = 0.5
voigt_index = ((0, 3, 5), (3, 1, 4), (5, 4, 2))
voigt_pairs = ((0, 0), (1, 1), (2, 2), (0, 1), (1, 2), (0, 2))
bf16 = jnp.bfloat16
f32 = jnp.float32


def swap_pairs(value, axis, odd, closed):
    count = lax.axis_size(axis)
    pairs = []
    for i in range(odd, count, 2):
        j = (i + 1) % count
        if j == i + 1 or closed:
            pairs += [(i, j), (j, i)]
    return lax.ppermute(value, axis, pairs)


def parity(axis):
    return lax.rem(lax.axis_index(axis), 2)


def halves(value):
    high = value.astype(bf16).astype(f32)
    return high, value - high


def source_rows(row):
    places = [row(k) for k in range(3)]
    motion = [row(3 + k) for k in range(3)]
    scaled = [row(6 + k) for k in range(6)]
    mass, volume = row(12), row(13)
    out = [mass]
    out += [mass * x for x in places]
    out += [mass * s for s in scaled]
    for k in range(3):
        dotted = scaled[voigt_index[k][0]] * places[0]
        dotted = dotted + scaled[voigt_index[k][1]] * places[1]
        dotted = dotted + scaled[voigt_index[k][2]] * places[2]
        out.append(mass * dotted)
    out.append(volume)
    out += [volume * v for v in motion]
    out += [volume * x for x in places]
    for a, b in voigt_pairs:
        out.append(volume * (0.5 * (motion[a] * places[b] + motion[b] * places[a])))
    return out


def distance_rows(row):
    places = [row(k) * (1.0 / smooth_len) for k in range(3)]
    square = places[0] * places[0] + places[1] * places[1] + places[2] * places[2]
    high, low = zip(*[halves(x) for x in places])
    n0, rest = halves(square)
    n1, n2 = halves(rest)
    one = jnp.ones_like(square)
    zero = jnp.zeros_like(square)
    from_side = [-2.0 * x for x in high + low + high] + [n0, n1, n2, one, one, one, zero]
    to_side = list(high + high + low) + [one, one, one, n0, n1, n2, zero]
    return from_side, to_side


def fill_rows(row, base, count, src32, far32, to32):
    for f, value in enumerate(source_rows(row)):
        src32[pl.ds(base * 32 + f, count, stride=32), :] = value
    from_side, to_side = distance_rows(row)
    for f, value in enumerate(from_side):
        far32[pl.ds(base * 16 + f, count, stride=16), :] = value
    if to32 is not None:
        for f, value in enumerate(to_side):
            to32[pl.ds(base * 16 + f, count, stride=16), :] = value


def finish_tables(count, src32, far32, S_ref, A_ref):
    def eight(i, carry):
        flipped = far32[pl.ds(pl.multiple_of(i * 128, 128), 128), :].T
        A_ref[i] = flipped.astype(bf16)
        for u in range(8):
            b = i * 8 + u
            value = src32[pl.ds(pl.multiple_of(b * 32, 32), 32), :]
            high = value.astype(bf16)
            S_ref[b, 0:32, :] = high
            S_ref[b, 32:64, :] = (value - high.astype(f32)).astype(bf16)
        return carry

    lax.fori_loop(0, count // 8, eight, 0)


def pad_targets(B_ref, to32):
    def one(b, carry):
        B_ref[b, 0:112, :] = jnp.zeros((112, 128), bf16)
        B_ref[b, 128:240, :] = jnp.zeros((112, 128), bf16)
        B_ref[b, 112:128, :] = to32[pl.ds(pl.multiple_of(b * 16, 16), 16), :].astype(bf16)
        return carry

    lax.fori_loop(0, 32, one, 0)


def closeness_cubed(square):
    square = jnp.maximum(square, 1e-30)
    close = jnp.maximum(1.0 - square * lax.rsqrt(square), 0.0)
    return close * close * close


def tile_group(items, S_ref, A_ref, B_ref, acc_ref):
    outs = []
    for target, into, source in items:
        if isinstance(source, int):
            start, octet = 112 - 16 * (source % 8), source // 8
        else:
            start = pl.multiple_of(112 - 16 * lax.rem(source, 8), 16)
            octet = lax.div(source, 8)
        square = jnp.dot(
            A_ref[octet], B_ref[target, pl.ds(start, 128), :], preferred_element_type=f32
        )
        kernel = closeness_cubed(square)
        high = kernel.astype(bf16)
        low = (kernel - high.astype(f32)).astype(bf16)
        rows = S_ref[source]
        both = jnp.dot(
            jnp.concatenate([rows, rows], 1),
            jnp.concatenate([high, low], 0),
            preferred_element_type=f32,
        )
        outs.append((into, both[:32] + both[32:]))
    for into, value in outs:
        acc_ref[into] += value


def lanes_to_column(values):
    n = values.shape[1]
    rows = lax.broadcasted_iota(jnp.int32, (n, n), 0)
    cols = lax.broadcasted_iota(jnp.int32, (n, n), 1)
    return jnp.sum(jnp.where(rows == cols, values, 0.0), axis=1, keepdims=True)


def gather_rims(send_ref, state_ref, msgs):
    send = send_ref[...].astype(f32)
    even_d, even_s = parity("depth") == 0, parity("strip") == 0
    order = [
        jnp.where(even_d, send[0:1], send[1:2]),
        jnp.where(even_d, send[1:2], send[0:1]),
        jnp.where(even_s, send[2:3], send[3:4]),
        jnp.where(even_s, send[3:4], send[2:3]),
    ]
    block = lax.rem(lax.broadcasted_iota(jnp.int32, (64, 96), 1), 32).astype(f32)
    column = jnp.concatenate([lanes_to_column(row) for row in order], 0)
    pick = jnp.where(block == column, 1.0, 0.0).astype(bf16)
    for k in range(14):
        high, rest = halves(state_ref[32 * k : 32 * k + 32, :])
        middle, low = halves(rest)
        parts = jnp.concatenate([x.astype(bf16) for x in (high, middle, low)], 0)
        rows = jnp.dot(pick, parts, preferred_element_type=f32)
        for m in range(4):
            msgs[m][16 * k : 16 * k + 16, :] = rows[16 * m : 16 * m + 16]
    for m in range(4):
        msgs[m][224:256, :] = jnp.zeros((32, 128), f32)


def fetch(pairs, sem):
    copies = [pltpu.make_async_copy(a, b, sem.at[i]) for i, (a, b) in enumerate(pairs)]
    for copy in copies:
        copy.start()
    return copies


def own_kernel(
    state_ref, count_ref, pairs_hbm, acc_ref, B_ref,
    S_ref, A_ref, src32, far32, to32, acc33, off_ref, pairs_ref, sem,
):
    copies = fetch([(pairs_hbm, pairs_ref)], sem)

    def row(k):
        return state_ref[32 * k : 32 * k + 32, :]

    fill_rows(row, 0, 32, src32, far32, to32)
    finish_tables(32, src32, far32, S_ref, A_ref)

    pad_targets(B_ref, to32)
    acc33[...] = jnp.zeros_like(acc33)
    for copy in copies:
        copy.wait()
    total = count_ref[0, 0]
    off = jnp.int32(0)
    for q in range(128):
        a = pairs_ref[0, q]
        b = pairs_ref[1, q]
        off_ref[0, off] = a
        off_ref[1, off] = b
        off = off + jnp.where(jnp.logical_and(q < total, a != b), 1, 0)
    def listed(g):
        items = []
        for u in range(OWN_GROUP // 2):
            q = g * (OWN_GROUP // 2) + u
            live = q < off
            a = jnp.where(live, off_ref[0, q], 0)
            b = jnp.where(live, off_ref[1, q], 0)
            items.append((a, jnp.where(live, a, 32), b))
            items.append((b, jnp.where(live, b, 32), a))
        return items

    def one_group(g, carry):
        tile_group(listed(g), S_ref, A_ref, B_ref, acc33)
        return carry

    tile_group([(b, b, b) for b in range(32)] + listed(0), S_ref, A_ref, B_ref, acc33)
    groups = lax.div(off + (OWN_GROUP // 2 - 1), OWN_GROUP // 2)
    lax.fori_loop(1, groups, one_group, 0)
    acc_ref[...] = acc33[0:32]


def start_kernel(
    send_hbm, counts_hbm, links_hbm, pos_hbm, vel_hbm, sig_hbm, mass_hbm, dens_hbm,
    state_ref, m0, m1, m2, m3, send_ref, counts_ref, links_ref, sig_ref, mass_ref, dens_ref, sem,
):
    copies = fetch(
        [
            (send_hbm, send_ref),
            (counts_hbm, counts_ref),
            (links_hbm, links_ref),
            (pos_hbm, state_ref.at[0:96]),
            (vel_hbm, state_ref.at[96:192]),
            (sig_hbm, sig_ref),
            (mass_hbm, mass_ref),
            (dens_hbm, dens_ref),
        ],
        sem,
    )
    for copy in copies:
        copy.wait()
    column = lanes_to_column(counts_ref[...].astype(f32))
    lane = lax.broadcasted_iota(jnp.int32, (32, 128), 1).astype(f32)
    mass = jnp.where(lane < column, mass_ref[...], 0.0)
    dens = dens_ref[...]
    square = dens * dens
    for k in range(6):
        state_ref[192 + 32 * k : 224 + 32 * k, :] = sig_ref[32 * k : 32 * k + 32, :] / square
    state_ref[384:416, :] = mass
    state_ref[416:448, :] = mass / dens
    state_ref[448:512, :] = jnp.zeros((64, 128), f32)
    gather_rims(send_ref, state_ref, (m0, m1, m2, m3))
    links = links_ref[...].astype(f32)
    for msg in (m0, m1, m2, m3):
        msg[224:228, 0:48] = links


def cross_terms(send_ref, link_ref, back_ref, msgs, own_acc, S_ref, A_ref, B_ref, src32, far32, acc, ready):
    for face in range(4):
        def row(k, face=face):
            return msgs[face][16 * k : 16 * k + 16, :]

        fill_rows(row, 16 * face, 16, src32, far32, None)
    finish_tables(64, src32, far32, S_ref, A_ref)
    acc[...] = own_acc[...]
    ready()

    depth, strip = parity("depth"), parity("strip")

    def one_group(g, carry):
        items = []
        for u in range(CROSS_GROUP // 4):
            q = g * (CROSS_GROUP // 4) + u
            back_d, back_s = 8 * (1 - depth), 16 + 8 * (1 - strip)
            for target, source in (
                (send_ref[0, link_ref[0, q]], 16 * depth + link_ref[1, q]),
                (send_ref[1, back_ref[back_d + 1, q]], 16 * (1 - depth) + back_ref[back_d, q]),
                (send_ref[2, link_ref[2, q]], 32 + 16 * strip + link_ref[3, q]),
                (send_ref[3, back_ref[back_s + 3, q]], 32 + 16 * (1 - strip) + back_ref[back_s + 2, q]),
            ):
                items.append((target, target, source))
        tile_group(items, S_ref, A_ref, B_ref, acc)
        return carry

    for g in range(48 // (CROSS_GROUP // 4)):
        one_group(g, 0)


def rates(state_ref, acc, flag, c):
    def total(f):
        at = pl.ds(8 * c * 32 + f, 8, stride=32)
        return kernel_coef * acc[at, :]

    def row(k):
        return state_ref[32 * k + 8 * c : 32 * k + 8 * c + 8, :]

    places = [row(k) for k in range(3)]
    motion = [row(3 + k) for k in range(3)]
    scaled = [row(6 + k) for k in range(6)]
    blade = (spin_rate * places[2], jnp.zeros_like(places[1]), -spin_rate * places[0])
    mass_sum = total(0)
    lever = [places[l] * mass_sum - total(1 + l) for l in range(3)]
    stress_sum = [total(4 + s) for s in range(6)]
    acceleration = []
    for k in range(3):
        force = jnp.zeros_like(mass_sum)
        for l in range(3):
            slot = voigt_index[k][l]
            force = force + scaled[slot] * lever[l]
            force = force + places[l] * stress_sum[slot]
        force = force - total(10 + k)
        force = force + blade_stiff * flag * (blade[k] - motion[k])
        if k == 2:
            force = force - gravity
        acceleration.append(force)
    volume_sum = total(13)
    motion_sum = [total(14 + k) for k in range(3)]
    place_sum = [total(17 + k) for k in range(3)]
    strain = []
    for comp, (a, b) in enumerate(voigt_pairs):
        rate = 0.5 * (places[b] * motion_sum[a] + places[a] * motion_sum[b])
        rate = rate - total(20 + comp)
        rate = rate - 0.5 * volume_sum * (motion[a] * places[b] + motion[b] * places[a])
        rate = rate + 0.5 * (motion[a] * place_sum[b] + motion[b] * place_sum[a])
        strain.append(rate)
    return acceleration, strain


def elastic_step(stress, strain, fraction):
    volumetric = strain[0] + strain[1] + strain[2]
    lame_first = bulk_mod - 2.0 * shear_mod / 3.0
    components = []
    for comp in range(6):
        change = 2.0 * shear_mod * strain[comp]
        if comp < 3:
            change = change + lame_first * volumetric
        components.append(stress[comp] + fraction * time_step * change)
    return components


def plastic_return(components, plastic, cohesion):
    for _ in range(RETURN_ITERS):
        mean = (components[0] + components[1] + components[2]) / 3.0
        dev = [components[k] - mean for k in range(3)] + list(components[3:])
        second = 0.5 * (dev[0] * dev[0] + dev[1] * dev[1] + dev[2] * dev[2])
        second = second + dev[3] * dev[3] + dev[4] * dev[4] + dev[5] * dev[5]
        shear = jnp.sqrt(second)
        limit = cohesion * (1.0 + plastic / (plastic + harden_scale))
        excess = jnp.maximum(shear + friction * 3.0 * mean - limit, 0.0)
        multiplier = (relax_rate / (shear_mod + 9.0 * bulk_mod * friction * friction + harden_mod)) * excess
        shrink = jnp.maximum(1.0 - shear_mod * multiplier / jnp.maximum(shear, tau_floor), 0.0)
        mean = mean - 3.0 * bulk_mod * friction * multiplier
        components = [dev[k] * shrink + mean for k in range(3)] + [dev[k] * shrink for k in range(3, 6)]
        plastic = plastic + multiplier
    return components, plastic


def contact_column(contact_ref):
    rows = lax.broadcasted_iota(jnp.int32, (32, 16), 0)
    hit = jnp.where(contact_ref[...] == rows, 1.0, 0.0)
    return jnp.sum(hit, axis=1, keepdims=True)


def half_kernel(
    state_ref, own_acc, B_ref,
    m0, m1, m2, m3, sig_hbm, plastic_hbm, cohesion_hbm, dens_hbm, send_hbm, link_hbm, contact_hbm,
    next_ref, n0, n1, n2, n3, back_out,
    S_ref, A_ref, src32, far32, acc, send_ref, link_ref, contact_ref, back_ref,
    sig_ref, plastic_ref, cohesion_ref, dens_ref, send_vmem, sem,
):
    for m, msg in enumerate((m0, m1, m2, m3)):
        back_out[8 * m : 8 * m + 8, :] = msg[224:232, :].astype(jnp.int32)
    copies = fetch(
        [
            (back_out, back_ref),
            (send_hbm, send_ref),
            (link_hbm, link_ref),
            (contact_hbm, contact_ref),
            (sig_hbm, sig_ref),
            (plastic_hbm, plastic_ref),
            (cohesion_hbm, cohesion_ref),
            (dens_hbm, dens_ref),
            (send_hbm, send_vmem),
        ],
        sem,
    )

    def ready():
        for copy in copies:
            copy.wait()

    cross_terms(
        send_ref, link_ref, back_ref, (m0, m1, m2, m3), own_acc, S_ref, A_ref, B_ref, src32, far32, acc, ready
    )
    flags = contact_column(contact_ref)
    acc2 = acc.reshape(1024, 128)
    for c in range(4):
        at = slice(8 * c, 8 * c + 8)
        acceleration, strain = rates(state_ref, acc2, flags[at], c)
        stress = [sig_ref[32 * k + 8 * c : 32 * k + 8 * c + 8, :] for k in range(6)]
        trial = elastic_step(stress, strain, 0.5)
        for k in range(3):
            x = slice(32 * k + 8 * c, 32 * k + 8 * c + 8)
            v = slice(96 + 32 * k + 8 * c, 96 + 32 * k + 8 * c + 8)
            motion = state_ref[v, :]
            next_ref[x, :] = state_ref[x, :] + 0.5 * time_step * motion
            next_ref[v, :] = motion + 0.5 * time_step * acceleration[k]
        for k in range(6):
            next_ref[192 + 32 * k + 8 * c : 200 + 32 * k + 8 * c, :] = trial[k]
    trial = [next_ref[192 + 32 * k : 224 + 32 * k, :] for k in range(6)]
    half_stress, _ = plastic_return(trial, plastic_ref[...], cohesion_ref[...])
    dens = dens_ref[...]
    square = dens * dens
    for k in range(6):
        next_ref[192 + 32 * k : 224 + 32 * k, :] = half_stress[k] / square
    next_ref[384:512, :] = state_ref[384:512, :]
    gather_rims(send_vmem, next_ref, (n0, n1, n2, n3))


def last_kernel(
    state_ref, own_acc, B_ref,
    m0, m1, m2, m3, back_vmem, sig_hbm, plastic_hbm, cohesion_hbm, pos_hbm, vel_hbm,
    send_hbm, link_hbm, contact_hbm, counts_hbm,
    pos_out, vel_out, sig_out, plastic_out,
    S_ref, A_ref, src32, far32, acc, send_ref, link_ref, contact_ref, back_ref,
    sig_ref, plastic_ref, cohesion_ref, pos_ref, vel_ref, counts_ref, sem,
):
    copies = fetch(
        [
            (back_vmem, back_ref),
            (send_hbm, send_ref),
            (link_hbm, link_ref),
            (contact_hbm, contact_ref),
            (counts_hbm, counts_ref),
            (sig_hbm, sig_ref),
            (plastic_hbm, plastic_ref),
            (cohesion_hbm, cohesion_ref),
            (pos_hbm, pos_ref),
            (vel_hbm, vel_ref),
        ],
        sem,
    )

    def ready():
        for copy in copies:
            copy.wait()

    cross_terms(
        send_ref, link_ref, back_ref, (m0, m1, m2, m3), own_acc, S_ref, A_ref, B_ref, src32, far32, acc, ready
    )
    flags = contact_column(contact_ref)
    column = lanes_to_column(counts_ref[...].astype(f32))
    lane = lax.broadcasted_iota(jnp.int32, (8, 128), 1).astype(f32)
    acc2 = acc.reshape(1024, 128)
    for c in range(4):
        at = slice(8 * c, 8 * c + 8)
        keep = lane < column[at]
        acceleration, strain = rates(state_ref, acc2, flags[at], c)
        stress = [sig_ref[32 * k + 8 * c : 32 * k + 8 * c + 8, :] for k in range(6)]
        trial = elastic_step(stress, strain, 1.0)
        for k in range(3):
            x = slice(32 * k + 8 * c, 32 * k + 8 * c + 8)
            v = slice(96 + 32 * k + 8 * c, 96 + 32 * k + 8 * c + 8)
            pos_out[x, :] = jnp.where(keep, pos_ref[x, :] + time_step * state_ref[v, :], 0.0)
            vel_out[x, :] = jnp.where(keep, vel_ref[x, :] + time_step * acceleration[k], 0.0)
        for k in range(6):
            sig_out[32 * k + 8 * c : 32 * k + 8 * c + 8, :] = trial[k]
    keep = lax.broadcasted_iota(jnp.int32, (32, 128), 1).astype(f32) < column
    trial = [sig_out[32 * k : 32 * k + 32, :] for k in range(6)]
    new_stress, new_plastic = plastic_return(trial, plastic_ref[...], cohesion_ref[...])
    for k in range(6):
        sig_out[32 * k : 32 * k + 32, :] = jnp.where(keep, new_stress[k], 0.0)
    plastic_out[...] = jnp.where(keep, new_plastic, 0.0)


VMEM = pl.BlockSpec(memory_space=pltpu.VMEM)
HBM = pl.BlockSpec(memory_space=pltpu.HBM)
params = pltpu.CompilerParams(vmem_limit_bytes=48 * 1024 * 1024)


def in_hbm(value):
    return pltpu.with_memory_space_constraint(value, pltpu.HBM)


def shape(*dims, dtype=f32):
    return jax.ShapeDtypeStruct(dims, dtype)


def tables(count):
    return [
        pltpu.VMEM((count, 64, 128), bf16),
        pltpu.VMEM((count // 8, 128, 128), bf16),
        pltpu.VMEM((count * 32, 128), f32),
        pltpu.VMEM((count * 16, 128), f32),
    ]


def call(kernel, vmem, hbm, outs, scratch):
    return pl.pallas_call(
        kernel,
        out_shape=outs,
        in_specs=[VMEM] * len(vmem) + [HBM] * len(hbm),
        out_specs=[VMEM] * len(outs),
        scratch_shapes=scratch,
        compiler_params=params,
    )(*vmem, *hbm)


def shards(
    position, velocity, stress, plastic, particle_mass, density, cohesion,
    counts, block_pairs, pair_count, send_lists, cross_links, contact,
):
    pos = position.reshape(96, 128)
    vel = velocity.reshape(96, 128)
    sig = stress.reshape(192, 128)
    plastic_now = plastic.reshape(32, 128)
    mass = particle_mass.reshape(32, 128)
    dens = density.reshape(32, 128)
    cohesion_now = cohesion.reshape(32, 128)
    counts_now = counts.reshape(1, 32)
    pairs = jnp.swapaxes(block_pairs.reshape(128, 2), 0, 1)
    send = send_lists.reshape(4, 16)
    links = jnp.swapaxes(cross_links.reshape(2, 48, 2), 1, 2).reshape(4, 48)
    touched = contact.reshape(1, 16)

    rim = [shape(16 * ROWS, 128)] * 4
    def own(state):
        return call(
            own_kernel,
            [state, pair_count],
            [in_hbm(pairs)],
            [shape(32, 32, 128), shape(32, 240, 128, dtype=bf16)],
            tables(32)
            + [
                pltpu.VMEM((512, 128), f32),
                pltpu.VMEM((33, 32, 128), f32),
                pltpu.SMEM((2, 128), jnp.int32),
                pltpu.SMEM((2, 128), jnp.int32),
                pltpu.SemaphoreType.DMA((1,)),
            ],
        )

    state, *msgs = call(
        start_kernel,
        [],
        [in_hbm(x) for x in (send, counts_now, links, pos, vel, sig, mass, dens)],
        [shape(512, 128)] + rim,
        [
            pltpu.VMEM((4, 16), jnp.int32),
            pltpu.VMEM((1, 32), jnp.int32),
            pltpu.VMEM((4, 48), jnp.int32),
            pltpu.VMEM((192, 128), f32),
            pltpu.VMEM((32, 128), f32),
            pltpu.VMEM((32, 128), f32),
            pltpu.SemaphoreType.DMA((8,)),
        ],
    )

    def swap(msgs):
        strips = [swap_pairs(msgs[2 + odd], "strip", odd, True) for odd in range(2)]
        depths = [swap_pairs(msgs[odd], "depth", odd, False) for odd in range(2)]
        return depths + strips

    cross_scratch = tables(64) + [
        pltpu.VMEM((32, 32, 128), f32),
        pltpu.SMEM((4, 16), jnp.int32),
        pltpu.SMEM((4, 48), jnp.int32),
        pltpu.VMEM((1, 16), jnp.int32),
        pltpu.SMEM((32, 128), jnp.int32),
        pltpu.VMEM((192, 128), f32),
        pltpu.VMEM((32, 128), f32),
        pltpu.VMEM((32, 128), f32),
    ]
    fields = [in_hbm(x) for x in (sig, plastic_now, cohesion_now)]
    lists = [in_hbm(x) for x in (send, links, touched)]
    far = swap(msgs)
    own_acc, to_side = own(state)
    state, *msgs, back = call(
        half_kernel,
        [state, own_acc, to_side, *far],
        fields + [in_hbm(dens)] + lists,
        [shape(512, 128)] + rim + [shape(32, 128, dtype=jnp.int32)],
        cross_scratch
        + [pltpu.VMEM((32, 128), f32), pltpu.VMEM((4, 16), jnp.int32), pltpu.SemaphoreType.DMA((9,))],
    )
    far = swap(msgs)
    own_acc, to_side = own(state)
    new_pos, new_vel, new_sig, new_plastic = call(
        last_kernel,
        [state, own_acc, to_side, *far, back],
        fields + [in_hbm(pos), in_hbm(vel)] + lists + [in_hbm(counts_now)],
        [shape(96, 128), shape(96, 128), shape(192, 128), shape(32, 128)],
        cross_scratch
        + [
            pltpu.VMEM((96, 128), f32),
            pltpu.VMEM((96, 128), f32),
            pltpu.VMEM((1, 32), jnp.int32),
            pltpu.SemaphoreType.DMA((10,)),
        ],
    )
    return (
        new_pos.reshape(position.shape),
        new_vel.reshape(velocity.shape),
        new_sig.reshape(stress.shape),
        new_plastic.reshape(plastic.shape),
    )


def solution(mesh):
    def spec(rank):
        return P("strip", "depth", *([None] * (rank - 2)))

    return jax.shard_map(
        shards,
        mesh=mesh,
        in_specs=tuple(spec(r) for r in (5, 5, 5, 4, 4, 4, 4, 3, 4, 2, 4, 5, 3)),
        out_specs=tuple(spec(r) for r in (5, 5, 5, 4)),
        check_vma=False,
    )
```

```python
import functools

import jax
import jax.numpy as jnp
from jax import lax
from jax.experimental import pallas as pl
from jax.experimental.pallas import tpu as pltpu
from jax.sharding import PartitionSpec as P

RETURN_ITERS = 4
ROWS = 16
OWN_GROUP = 96
CROSS_GROUP = 192

smooth_len = 1.5
kernel_coef = -105.0 / (3.141592653589793 * 1.5**5)
time_step = 0.25
gravity = 1.0
spin_rate = 2.0
blade_stiff = 4.0
bulk_mod = 2.0
shear_mod = 1.5
friction = 0.25
harden_scale = 0.05
harden_mod = 0.5
relax_rate = 0.7
tau_floor = 0.5
voigt_index = ((0, 3, 5), (3, 1, 4), (5, 4, 2))
voigt_pairs = ((0, 0), (1, 1), (2, 2), (0, 1), (1, 2), (0, 2))
bf16 = jnp.bfloat16
f32 = jnp.float32


def swap_pairs(value, axis, odd, closed):
    count = lax.axis_size(axis)
    pairs = []
    for i in range(odd, count, 2):
        j = (i + 1) % count
        if j == i + 1 or closed:
            pairs += [(i, j), (j, i)]
    return lax.ppermute(value, axis, pairs)


def parity(axis):
    return lax.rem(lax.axis_index(axis), 2)


def halves(value):
    high = value.astype(bf16).astype(f32)
    return high, value - high


def source_rows(row):
    places = [row(k) for k in range(3)]
    motion = [row(3 + k) for k in range(3)]
    scaled = [row(6 + k) for k in range(6)]
    mass, volume = row(12), row(13)
    out = [mass]
    out += [mass * x for x in places]
    out += [mass * s for s in scaled]
    for k in range(3):
        dotted = scaled[voigt_index[k][0]] * places[0]
        dotted = dotted + scaled[voigt_index[k][1]] * places[1]
        dotted = dotted + scaled[voigt_index[k][2]] * places[2]
        out.append(mass * dotted)
    out.append(volume)
    out += [volume * v for v in motion]
    out += [volume * x for x in places]
    for a, b in voigt_pairs:
        out.append(volume * (0.5 * (motion[a] * places[b] + motion[b] * places[a])))
    return out


def distance_rows(row):
    places = [row(k) * (1.0 / smooth_len) for k in range(3)]
    square = places[0] * places[0] + places[1] * places[1] + places[2] * places[2]
    high, low = zip(*[halves(x) for x in places])
    n0, rest = halves(square)
    n1, n2 = halves(rest)
    one = jnp.ones_like(square)
    zero = jnp.zeros_like(square)
    from_side = [-2.0 * x for x in high + low + high] + [n0, n1, n2, one, one, one, zero]
    to_side = list(high + high + low) + [one, one, one, n0, n1, n2, zero]
    return from_side, to_side


def fill_rows(row, base, count, src32, far32, to32):
    for f, value in enumerate(source_rows(row)):
        src32[pl.ds(base * 32 + f, count, stride=32), :] = value
    from_side, to_side = distance_rows(row)
    for f, value in enumerate(from_side):
        far32[pl.ds(base * 16 + f, count, stride=16), :] = value
    if to32 is not None:
        for f, value in enumerate(to_side):
            to32[pl.ds(base * 16 + f, count, stride=16), :] = value


def finish_tables(count, src32, far32, S_ref, A_ref):
    def eight(i, carry):
        flipped = far32[pl.ds(pl.multiple_of(i * 128, 128), 128), :].T
        A_ref[i] = flipped.astype(bf16)
        for u in range(8):
            b = i * 8 + u
            value = src32[pl.ds(pl.multiple_of(b * 32, 32), 32), :]
            high = value.astype(bf16)
            S_ref[b, 0:32, :] = high
            S_ref[b, 32:64, :] = (value - high.astype(f32)).astype(bf16)
        return carry

    lax.fori_loop(0, count // 8, eight, 0)


def pad_targets(B_ref, to32):
    def one(b, carry):
        B_ref[b, 0:112, :] = jnp.zeros((112, 128), bf16)
        B_ref[b, 128:240, :] = jnp.zeros((112, 128), bf16)
        B_ref[b, 112:128, :] = to32[pl.ds(pl.multiple_of(b * 16, 16), 16), :].astype(bf16)
        return carry

    lax.fori_loop(0, 32, one, 0)


def closeness_cubed(square):
    square = jnp.maximum(square, 1e-30)
    close = jnp.maximum(1.0 - square * lax.rsqrt(square), 0.0)
    return close * close * close


def tile_group(items, S_ref, A_ref, B_ref, acc_ref):
    outs = []
    for target, into, source in items:
        if isinstance(source, int):
            start, octet = 112 - 16 * (source % 8), source // 8
        else:
            start = pl.multiple_of(112 - 16 * lax.rem(source, 8), 16)
            octet = lax.div(source, 8)
        square = jnp.dot(
            A_ref[octet], B_ref[target, pl.ds(start, 128), :], preferred_element_type=f32
        )
        kernel = closeness_cubed(square)
        high = kernel.astype(bf16)
        low = (kernel - high.astype(f32)).astype(bf16)
        rows = S_ref[source]
        both = jnp.dot(
            jnp.concatenate([rows, rows], 1),
            jnp.concatenate([high, low], 0),
            preferred_element_type=f32,
        )
        outs.append((into, both[:32] + both[32:]))
    for into, value in outs:
        acc_ref[into] += value


def lanes_to_column(values):
    n = values.shape[1]
    rows = lax.broadcasted_iota(jnp.int32, (n, n), 0)
    cols = lax.broadcasted_iota(jnp.int32, (n, n), 1)
    return jnp.sum(jnp.where(rows == cols, values, 0.0), axis=1, keepdims=True)


def gather_rims(send_ref, state_ref, msgs):
    send = send_ref[...].astype(f32)
    even_d, even_s = parity("depth") == 0, parity("strip") == 0
    order = [
        jnp.where(even_d, send[0:1], send[1:2]),
        jnp.where(even_d, send[1:2], send[0:1]),
        jnp.where(even_s, send[2:3], send[3:4]),
        jnp.where(even_s, send[3:4], send[2:3]),
    ]
    block = lax.rem(lax.broadcasted_iota(jnp.int32, (64, 96), 1), 32).astype(f32)
    column = jnp.concatenate([lanes_to_column(row) for row in order], 0)
    pick = jnp.where(block == column, 1.0, 0.0).astype(bf16)
    for k in range(14):
        high, rest = halves(state_ref[32 * k : 32 * k + 32, :])
        middle, low = halves(rest)
        parts = jnp.concatenate([x.astype(bf16) for x in (high, middle, low)], 0)
        rows = jnp.dot(pick, parts, preferred_element_type=f32)
        for m in range(4):
            msgs[m][16 * k : 16 * k + 16, :] = rows[16 * m : 16 * m + 16]
    for m in range(4):
        msgs[m][224:256, :] = jnp.zeros((32, 128), f32)


def fetch(pairs, sem):
    copies = [pltpu.make_async_copy(a, b, sem.at[i]) for i, (a, b) in enumerate(pairs)]
    for copy in copies:
        copy.start()
    return copies


def own_kernel(
    state_ref, count_ref, pairs_hbm, acc_ref, B_ref,
    S_ref, A_ref, src32, far32, to32, acc33, off_ref, pairs_ref, sem,
):
    copies = fetch([(pairs_hbm, pairs_ref)], sem)

    def row(k):
        return state_ref[32 * k : 32 * k + 32, :]

    fill_rows(row, 0, 32, src32, far32, to32)
    finish_tables(32, src32, far32, S_ref, A_ref)

    pad_targets(B_ref, to32)
    acc33[...] = jnp.zeros_like(acc33)
    for copy in copies:
        copy.wait()
    total = count_ref[0, 0]
    off = jnp.int32(0)
    for q in range(128):
        a = pairs_ref[0, q]
        b = pairs_ref[1, q]
        off_ref[0, off] = a
        off_ref[1, off] = b
        off = off + jnp.where(jnp.logical_and(q < total, a != b), 1, 0)
    def listed(g):
        items = []
        for u in range(OWN_GROUP // 2):
            q = g * (OWN_GROUP // 2) + u
            live = q < off
            a = jnp.where(live, off_ref[0, q], 0)
            b = jnp.where(live, off_ref[1, q], 0)
            items.append((a, jnp.where(live, a, 32), b))
            items.append((b, jnp.where(live, b, 32), a))
        return items

    def one_group(g, carry):
        tile_group(listed(g), S_ref, A_ref, B_ref, acc33)
        return carry

    tile_group([(b, b, b) for b in range(32)] + listed(0), S_ref, A_ref, B_ref, acc33)
    groups = lax.div(off + (OWN_GROUP // 2 - 1), OWN_GROUP // 2)
    lax.fori_loop(1, groups, one_group, 0)
    acc_ref[...] = acc33[0:32]


def start_kernel(
    send_hbm, counts_hbm, links_hbm, pos_hbm, vel_hbm, sig_hbm, mass_hbm, dens_hbm,
    state_ref, m2, m3, m0, m1, send_ref, counts_ref, links_ref, sig_ref, mass_ref, dens_ref, sem,
):
    copies = fetch(
        [
            (send_hbm, send_ref),
            (counts_hbm, counts_ref),
            (links_hbm, links_ref),
            (pos_hbm, state_ref.at[0:96]),
            (vel_hbm, state_ref.at[96:192]),
            (sig_hbm, sig_ref),
            (mass_hbm, mass_ref),
            (dens_hbm, dens_ref),
        ],
        sem,
    )
    for copy in copies:
        copy.wait()
    column = lanes_to_column(counts_ref[...].astype(f32))
    lane = lax.broadcasted_iota(jnp.int32, (32, 128), 1).astype(f32)
    mass = jnp.where(lane < column, mass_ref[...], 0.0)
    dens = dens_ref[...]
    square = dens * dens
    for k in range(6):
        state_ref[192 + 32 * k : 224 + 32 * k, :] = sig_ref[32 * k : 32 * k + 32, :] / square
    state_ref[384:416, :] = mass
    state_ref[416:448, :] = mass / dens
    state_ref[448:512, :] = jnp.zeros((64, 128), f32)
    gather_rims(send_ref, state_ref, (m0, m1, m2, m3))
    links = links_ref[...].astype(f32)
    for msg in (m0, m1, m2, m3):
        msg[224:228, 0:48] = links


def cross_terms(send_ref, link_ref, back_ref, msgs, own_acc, S_ref, A_ref, B_ref, src32, far32, acc, ready):
    for face in range(4):
        def row(k, face=face):
            return msgs[face][16 * k : 16 * k + 16, :]

        fill_rows(row, 16 * face, 16, src32, far32, None)
    finish_tables(64, src32, far32, S_ref, A_ref)
    acc[...] = own_acc[...]
    ready()

    depth, strip = parity("depth"), parity("strip")

    def one_group(g, carry):
        items = []
        for u in range(CROSS_GROUP // 4):
            q = g * (CROSS_GROUP // 4) + u
            back_d, back_s = 8 * (1 - depth), 16 + 8 * (1 - strip)
            for target, source in (
                (send_ref[0, link_ref[0, q]], 16 * depth + link_ref[1, q]),
                (send_ref[1, back_ref[back_d + 1, q]], 16 * (1 - depth) + back_ref[back_d, q]),
                (send_ref[2, link_ref[2, q]], 32 + 16 * strip + link_ref[3, q]),
                (send_ref[3, back_ref[back_s + 3, q]], 32 + 16 * (1 - strip) + back_ref[back_s + 2, q]),
            ):
                items.append((target, target, source))
        tile_group(items, S_ref, A_ref, B_ref, acc)
        return carry

    for g in range(48 // (CROSS_GROUP // 4)):
        one_group(g, 0)


def rates(state_ref, acc, flag, c):
    def total(f):
        at = pl.ds(8 * c * 32 + f, 8, stride=32)
        return kernel_coef * acc[at, :]

    def row(k):
        return state_ref[32 * k + 8 * c : 32 * k + 8 * c + 8, :]

    places = [row(k) for k in range(3)]
    motion = [row(3 + k) for k in range(3)]
    scaled = [row(6 + k) for k in range(6)]
    blade = (spin_rate * places[2], jnp.zeros_like(places[1]), -spin_rate * places[0])
    mass_sum = total(0)
    lever = [places[l] * mass_sum - total(1 + l) for l in range(3)]
    stress_sum = [total(4 + s) for s in range(6)]
    acceleration = []
    for k in range(3):
        force = jnp.zeros_like(mass_sum)
        for l in range(3):
            slot = voigt_index[k][l]
            force = force + scaled[slot] * lever[l]
            force = force + places[l] * stress_sum[slot]
        force = force - total(10 + k)
        force = force + blade_stiff * flag * (blade[k] - motion[k])
        if k == 2:
            force = force - gravity
        acceleration.append(force)
    volume_sum = total(13)
    motion_sum = [total(14 + k) for k in range(3)]
    place_sum = [total(17 + k) for k in range(3)]
    strain = []
    for comp, (a, b) in enumerate(voigt_pairs):
        rate = 0.5 * (places[b] * motion_sum[a] + places[a] * motion_sum[b])
        rate = rate - total(20 + comp)
        rate = rate - 0.5 * volume_sum * (motion[a] * places[b] + motion[b] * places[a])
        rate = rate + 0.5 * (motion[a] * place_sum[b] + motion[b] * place_sum[a])
        strain.append(rate)
    return acceleration, strain


def elastic_step(stress, strain, fraction):
    volumetric = strain[0] + strain[1] + strain[2]
    lame_first = bulk_mod - 2.0 * shear_mod / 3.0
    components = []
    for comp in range(6):
        change = 2.0 * shear_mod * strain[comp]
        if comp < 3:
            change = change + lame_first * volumetric
        components.append(stress[comp] + fraction * time_step * change)
    return components


def plastic_return(components, plastic, cohesion):
    for _ in range(RETURN_ITERS):
        mean = (components[0] + components[1] + components[2]) / 3.0
        dev = [components[k] - mean for k in range(3)] + list(components[3:])
        second = 0.5 * (dev[0] * dev[0] + dev[1] * dev[1] + dev[2] * dev[2])
        second = second + dev[3] * dev[3] + dev[4] * dev[4] + dev[5] * dev[5]
        shear = jnp.sqrt(second)
        limit = cohesion * (1.0 + plastic / (plastic + harden_scale))
        excess = jnp.maximum(shear + friction * 3.0 * mean - limit, 0.0)
        multiplier = (relax_rate / (shear_mod + 9.0 * bulk_mod * friction * friction + harden_mod)) * excess
        shrink = jnp.maximum(1.0 - shear_mod * multiplier / jnp.maximum(shear, tau_floor), 0.0)
        mean = mean - 3.0 * bulk_mod * friction * multiplier
        components = [dev[k] * shrink + mean for k in range(3)] + [dev[k] * shrink for k in range(3, 6)]
        plastic = plastic + multiplier
    return components, plastic


def contact_column(contact_ref):
    rows = lax.broadcasted_iota(jnp.int32, (32, 16), 0)
    hit = jnp.where(contact_ref[...] == rows, 1.0, 0.0)
    return jnp.sum(hit, axis=1, keepdims=True)


def half_kernel(
    state_ref, own_acc, B_ref,
    m2, m3, m0, m1, sig_hbm, plastic_hbm, cohesion_hbm, dens_hbm, send_hbm, link_hbm, contact_hbm,
    next_ref, n2, n3, n0, n1, back_out,
    S_ref, A_ref, src32, far32, acc, send_ref, link_ref, contact_ref, back_ref,
    sig_ref, plastic_ref, cohesion_ref, dens_ref, send_vmem, sem,
):
    for m, msg in enumerate((m0, m1, m2, m3)):
        back_out[8 * m : 8 * m + 8, :] = msg[224:232, :].astype(jnp.int32)
    copies = fetch(
        [
            (back_out, back_ref),
            (send_hbm, send_ref),
            (link_hbm, link_ref),
            (contact_hbm, contact_ref),
            (sig_hbm, sig_ref),
            (plastic_hbm, plastic_ref),
            (cohesion_hbm, cohesion_ref),
            (dens_hbm, dens_ref),
            (send_hbm, send_vmem),
        ],
        sem,
    )

    def ready():
        for copy in copies:
            copy.wait()

    cross_terms(
        send_ref, link_ref, back_ref, (m0, m1, m2, m3), own_acc, S_ref, A_ref, B_ref, src32, far32, acc, ready
    )
    flags = contact_column(contact_ref)
    acc2 = acc.reshape(1024, 128)
    for c in range(4):
        at = slice(8 * c, 8 * c + 8)
        acceleration, strain = rates(state_ref, acc2, flags[at], c)
        stress = [sig_ref[32 * k + 8 * c : 32 * k + 8 * c + 8, :] for k in range(6)]
        trial = elastic_step(stress, strain, 0.5)
        for k in range(3):
            x = slice(32 * k + 8 * c, 32 * k + 8 * c + 8)
            v = slice(96 + 32 * k + 8 * c, 96 + 32 * k + 8 * c + 8)
            motion = state_ref[v, :]
            next_ref[x, :] = state_ref[x, :] + 0.5 * time_step * motion
            next_ref[v, :] = motion + 0.5 * time_step * acceleration[k]
        for k in range(6):
            next_ref[192 + 32 * k + 8 * c : 200 + 32 * k + 8 * c, :] = trial[k]
    trial = [next_ref[192 + 32 * k : 224 + 32 * k, :] for k in range(6)]
    half_stress, _ = plastic_return(trial, plastic_ref[...], cohesion_ref[...])
    dens = dens_ref[...]
    square = dens * dens
    for k in range(6):
        next_ref[192 + 32 * k : 224 + 32 * k, :] = half_stress[k] / square
    next_ref[384:512, :] = state_ref[384:512, :]
    gather_rims(send_vmem, next_ref, (n0, n1, n2, n3))


def last_kernel(
    state_ref, own_acc, B_ref,
    m2, m3, m0, m1, back_vmem, sig_hbm, plastic_hbm, cohesion_hbm, pos_hbm, vel_hbm,
    send_hbm, link_hbm, contact_hbm, counts_hbm,
    pos_out, vel_out, sig_out, plastic_out,
    S_ref, A_ref, src32, far32, acc, send_ref, link_ref, contact_ref, back_ref,
    sig_ref, plastic_ref, cohesion_ref, pos_ref, vel_ref, counts_ref, sem,
):
    copies = fetch(
        [
            (back_vmem, back_ref),
            (send_hbm, send_ref),
            (link_hbm, link_ref),
            (contact_hbm, contact_ref),
            (counts_hbm, counts_ref),
            (sig_hbm, sig_ref),
            (plastic_hbm, plastic_ref),
            (cohesion_hbm, cohesion_ref),
            (pos_hbm, pos_ref),
            (vel_hbm, vel_ref),
        ],
        sem,
    )

    def ready():
        for copy in copies:
            copy.wait()

    cross_terms(
        send_ref, link_ref, back_ref, (m0, m1, m2, m3), own_acc, S_ref, A_ref, B_ref, src32, far32, acc, ready
    )
    flags = contact_column(contact_ref)
    column = lanes_to_column(counts_ref[...].astype(f32))
    lane = lax.broadcasted_iota(jnp.int32, (8, 128), 1).astype(f32)
    acc2 = acc.reshape(1024, 128)
    for c in range(4):
        at = slice(8 * c, 8 * c + 8)
        keep = lane < column[at]
        acceleration, strain = rates(state_ref, acc2, flags[at], c)
        stress = [sig_ref[32 * k + 8 * c : 32 * k + 8 * c + 8, :] for k in range(6)]
        trial = elastic_step(stress, strain, 1.0)
        for k in range(3):
            x = slice(32 * k + 8 * c, 32 * k + 8 * c + 8)
            v = slice(96 + 32 * k + 8 * c, 96 + 32 * k + 8 * c + 8)
            pos_out[x, :] = jnp.where(keep, pos_ref[x, :] + time_step * state_ref[v, :], 0.0)
            vel_out[x, :] = jnp.where(keep, vel_ref[x, :] + time_step * acceleration[k], 0.0)
        for k in range(6):
            sig_out[32 * k + 8 * c : 32 * k + 8 * c + 8, :] = trial[k]
    keep = lax.broadcasted_iota(jnp.int32, (32, 128), 1).astype(f32) < column
    trial = [sig_out[32 * k : 32 * k + 32, :] for k in range(6)]
    new_stress, new_plastic = plastic_return(trial, plastic_ref[...], cohesion_ref[...])
    for k in range(6):
        sig_out[32 * k : 32 * k + 32, :] = jnp.where(keep, new_stress[k], 0.0)
    plastic_out[...] = jnp.where(keep, new_plastic, 0.0)


VMEM = pl.BlockSpec(memory_space=pltpu.VMEM)
HBM = pl.BlockSpec(memory_space=pltpu.HBM)
params = pltpu.CompilerParams(vmem_limit_bytes=48 * 1024 * 1024)


def in_hbm(value):
    return pltpu.with_memory_space_constraint(value, pltpu.HBM)


def shape(*dims, dtype=f32):
    return jax.ShapeDtypeStruct(dims, dtype)


def tables(count):
    return [
        pltpu.VMEM((count, 64, 128), bf16),
        pltpu.VMEM((count // 8, 128, 128), bf16),
        pltpu.VMEM((count * 32, 128), f32),
        pltpu.VMEM((count * 16, 128), f32),
    ]


def call(kernel, vmem, hbm, outs, scratch):
    return pl.pallas_call(
        kernel,
        out_shape=outs,
        in_specs=[VMEM] * len(vmem) + [HBM] * len(hbm),
        out_specs=[VMEM] * len(outs),
        scratch_shapes=scratch,
        compiler_params=params,
    )(*vmem, *hbm)


def shards(
    position, velocity, stress, plastic, particle_mass, density, cohesion,
    counts, block_pairs, pair_count, send_lists, cross_links, contact,
):
    pos = position.reshape(96, 128)
    vel = velocity.reshape(96, 128)
    sig = stress.reshape(192, 128)
    plastic_now = plastic.reshape(32, 128)
    mass = particle_mass.reshape(32, 128)
    dens = density.reshape(32, 128)
    cohesion_now = cohesion.reshape(32, 128)
    counts_now = counts.reshape(1, 32)
    pairs = jnp.swapaxes(block_pairs.reshape(128, 2), 0, 1)
    send = send_lists.reshape(4, 16)
    links = jnp.swapaxes(cross_links.reshape(2, 48, 2), 1, 2).reshape(4, 48)
    touched = contact.reshape(1, 16)

    rim = [shape(16 * ROWS, 128)] * 4
    def own(state):
        return call(
            own_kernel,
            [state, pair_count],
            [in_hbm(pairs)],
            [shape(32, 32, 128), shape(32, 240, 128, dtype=bf16)],
            tables(32)
            + [
                pltpu.VMEM((512, 128), f32),
                pltpu.VMEM((33, 32, 128), f32),
                pltpu.SMEM((2, 128), jnp.int32),
                pltpu.SMEM((2, 128), jnp.int32),
                pltpu.SemaphoreType.DMA((1,)),
            ],
        )

    state, *msgs = call(
        start_kernel,
        [],
        [in_hbm(x) for x in (send, counts_now, links, pos, vel, sig, mass, dens)],
        [shape(512, 128)] + rim,
        [
            pltpu.VMEM((4, 16), jnp.int32),
            pltpu.VMEM((1, 32), jnp.int32),
            pltpu.VMEM((4, 48), jnp.int32),
            pltpu.VMEM((192, 128), f32),
            pltpu.VMEM((32, 128), f32),
            pltpu.VMEM((32, 128), f32),
            pltpu.SemaphoreType.DMA((8,)),
        ],
    )

    def swap(msgs):
        strips = [swap_pairs(msgs[odd], "strip", odd, True) for odd in range(2)]
        depths = [swap_pairs(msgs[2 + odd], "depth", odd, False) for odd in range(2)]
        return strips + depths

    cross_scratch = tables(64) + [
        pltpu.VMEM((32, 32, 128), f32),
        pltpu.SMEM((4, 16), jnp.int32),
        pltpu.SMEM((4, 48), jnp.int32),
        pltpu.VMEM((1, 16), jnp.int32),
        pltpu.SMEM((32, 128), jnp.int32),
        pltpu.VMEM((192, 128), f32),
        pltpu.VMEM((32, 128), f32),
        pltpu.VMEM((32, 128), f32),
    ]
    fields = [in_hbm(x) for x in (sig, plastic_now, cohesion_now)]
    lists = [in_hbm(x) for x in (send, links, touched)]
    far = swap(msgs)
    own_acc, to_side = own(state)
    state, *msgs, back = call(
        half_kernel,
        [state, own_acc, to_side, *far],
        fields + [in_hbm(dens)] + lists,
        [shape(512, 128)] + rim + [shape(32, 128, dtype=jnp.int32)],
        cross_scratch
        + [pltpu.VMEM((32, 128), f32), pltpu.VMEM((4, 16), jnp.int32), pltpu.SemaphoreType.DMA((9,))],
    )
    far = swap(msgs)
    own_acc, to_side = own(state)
    new_pos, new_vel, new_sig, new_plastic = call(
        last_kernel,
        [state, own_acc, to_side, *far, back],
        fields + [in_hbm(pos), in_hbm(vel)] + lists + [in_hbm(counts_now)],
        [shape(96, 128), shape(96, 128), shape(192, 128), shape(32, 128)],
        cross_scratch
        + [
            pltpu.VMEM((96, 128), f32),
            pltpu.VMEM((96, 128), f32),
            pltpu.VMEM((1, 32), jnp.int32),
            pltpu.SemaphoreType.DMA((10,)),
        ],
    )
    return (
        new_pos.reshape(position.shape),
        new_vel.reshape(velocity.shape),
        new_sig.reshape(stress.shape),
        new_plastic.reshape(plastic.shape),
    )


def solution(mesh):
    def spec(rank):
        return P("strip", "depth", *([None] * (rank - 2)))

    return jax.shard_map(
        shards,
        mesh=mesh,
        in_specs=tuple(spec(r) for r in (5, 5, 5, 4, 4, 4, 4, 3, 4, 2, 4, 5, 3)),
        out_specs=tuple(spec(r) for r in (5, 5, 5, 4)),
        check_vma=False,
    )
```

```python
import functools

import jax
import jax.numpy as jnp
from jax import lax
from jax.experimental import pallas as pl
from jax.experimental.pallas import tpu as pltpu
from jax.sharding import PartitionSpec as P

RETURN_ITERS = 4
OWN_GROUP = 96
CROSS_GROUP = 192

smooth_len = 1.5
kernel_coef = -105.0 / (3.141592653589793 * 1.5**5)
time_step = 0.25
gravity = 1.0
spin_rate = 2.0
blade_stiff = 4.0
bulk_mod = 2.0
shear_mod = 1.5
friction = 0.25
harden_scale = 0.05
harden_mod = 0.5
relax_rate = 0.7
tau_floor = 0.5
voigt_index = ((0, 3, 5), (3, 1, 4), (5, 4, 2))
voigt_pairs = ((0, 0), (1, 1), (2, 2), (0, 1), (1, 2), (0, 2))
bf16 = jnp.bfloat16
f32 = jnp.float32


def swap_pairs(value, axis, odd, closed):
    count = lax.axis_size(axis)
    pairs = []
    for i in range(odd, count, 2):
        j = (i + 1) % count
        if j == i + 1 or closed:
            pairs += [(i, j), (j, i)]
    return lax.ppermute(value, axis, pairs)


def parity(axis):
    return lax.rem(lax.axis_index(axis), 2)


def halves(value):
    high = value.astype(bf16).astype(f32)
    return high, value - high


def source_rows(row):
    places = [row(k) for k in range(3)]
    motion = [row(3 + k) for k in range(3)]
    scaled = [row(6 + k) for k in range(6)]
    mass, volume = row(12), row(13)
    out = [mass]
    out += [mass * x for x in places]
    out += [mass * s for s in scaled]
    for k in range(3):
        dotted = scaled[voigt_index[k][0]] * places[0]
        dotted = dotted + scaled[voigt_index[k][1]] * places[1]
        dotted = dotted + scaled[voigt_index[k][2]] * places[2]
        out.append(mass * dotted)
    out.append(volume)
    out += [volume * v for v in motion]
    out += [volume * x for x in places]
    for a, b in voigt_pairs:
        out.append(volume * (0.5 * (motion[a] * places[b] + motion[b] * places[a])))
    return out


def distance_rows(row):
    places = [row(k) * (1.0 / smooth_len) for k in range(3)]
    square = places[0] * places[0] + places[1] * places[1] + places[2] * places[2]
    high, low = zip(*[halves(x) for x in places])
    n0, rest = halves(square)
    n1, n2 = halves(rest)
    one = jnp.ones_like(square)
    zero = jnp.zeros_like(square)
    from_side = [-2.0 * x for x in high + low + high] + [n0, n1, n2, one, one, one, zero]
    to_side = list(high + high + low) + [one, one, one, n0, n1, n2, zero]
    return from_side, to_side


def fill_rows(row, base, count, src32, far32, to32):
    for f, value in enumerate(source_rows(row)):
        src32[pl.ds(base * 32 + f, count, stride=32), :] = value
    from_side, to_side = distance_rows(row)
    for f, value in enumerate(from_side):
        far32[pl.ds(base * 16 + f, count, stride=16), :] = value
    if to32 is not None:
        for f, value in enumerate(to_side):
            to32[pl.ds(base * 16 + f, count, stride=16), :] = value


def finish_tables(count, src32, far32, S_ref, A_ref):
    def eight(i, carry):
        flipped = far32[pl.ds(pl.multiple_of(i * 128, 128), 128), :].T
        A_ref[i] = flipped.astype(bf16)
        for u in range(8):
            b = i * 8 + u
            value = src32[pl.ds(pl.multiple_of(b * 32, 32), 32), :]
            high = value.astype(bf16)
            S_ref[b, 0:32, :] = high
            S_ref[b, 32:64, :] = (value - high.astype(f32)).astype(bf16)
        return carry

    lax.fori_loop(0, count // 8, eight, 0)


def pad_targets(B_ref, to32):
    def one(b, carry):
        B_ref[b, 0:112, :] = jnp.zeros((112, 128), bf16)
        B_ref[b, 128:240, :] = jnp.zeros((112, 128), bf16)
        B_ref[b, 112:128, :] = to32[pl.ds(pl.multiple_of(b * 16, 16), 16), :].astype(bf16)
        return carry

    lax.fori_loop(0, 32, one, 0)


def closeness_cubed(square):
    square = jnp.maximum(square, 1e-30)
    close = jnp.maximum(1.0 - square * lax.rsqrt(square), 0.0)
    return close * close * close


def tile_group(items, S_ref, A_ref, B_ref, acc_ref):
    outs = []
    for target, into, source in items:
        if isinstance(source, int):
            start, octet = 112 - 16 * (source % 8), source // 8
        else:
            start = pl.multiple_of(112 - 16 * lax.rem(source, 8), 16)
            octet = lax.div(source, 8)
        square = jnp.dot(
            A_ref[octet], B_ref[target, pl.ds(start, 128), :], preferred_element_type=f32
        )
        kernel = closeness_cubed(square)
        high = kernel.astype(bf16)
        low = (kernel - high.astype(f32)).astype(bf16)
        rows = S_ref[source]
        both = jnp.dot(
            jnp.concatenate([rows, rows], 1),
            jnp.concatenate([high, low], 0),
            preferred_element_type=f32,
        )
        outs.append((into, both[:32] + both[32:]))
    for into, value in outs:
        acc_ref[into] += value


def lanes_to_column(values):
    n = values.shape[1]
    rows = lax.broadcasted_iota(jnp.int32, (n, n), 0)
    cols = lax.broadcasted_iota(jnp.int32, (n, n), 1)
    return jnp.sum(jnp.where(rows == cols, values, 0.0), axis=1, keepdims=True)


def gather_rims(send_ref, state_ref, msgs, rows_sent):
    send = send_ref[...].astype(f32)
    even_d, even_s = parity("depth") == 0, parity("strip") == 0
    order = [
        jnp.where(even_d, send[0:1], send[1:2]),
        jnp.where(even_d, send[1:2], send[0:1]),
        jnp.where(even_s, send[2:3], send[3:4]),
        jnp.where(even_s, send[3:4], send[2:3]),
    ]
    block = lax.rem(lax.broadcasted_iota(jnp.int32, (64, 96), 1), 32).astype(f32)
    column = jnp.concatenate([lanes_to_column(row) for row in order], 0)
    pick = jnp.where(block == column, 1.0, 0.0).astype(bf16)
    for k in range(rows_sent):
        high, rest = halves(state_ref[32 * k : 32 * k + 32, :])
        middle, low = halves(rest)
        parts = jnp.concatenate([x.astype(bf16) for x in (high, middle, low)], 0)
        rows = jnp.dot(pick, parts, preferred_element_type=f32)
        for m in range(4):
            msgs[m][16 * k : 16 * k + 16, :] = rows[16 * m : 16 * m + 16]


def fetch(pairs, sem):
    copies = [pltpu.make_async_copy(a, b, sem.at[i]) for i, (a, b) in enumerate(pairs)]
    for copy in copies:
        copy.start()
    return copies


def own_kernel(
    state_ref, count_ref, pairs_hbm, acc_ref, B_ref,
    S_ref, A_ref, src32, far32, to32, acc33, off_ref, pairs_ref, sem,
):
    copies = fetch([(pairs_hbm, pairs_ref)], sem)

    def row(k):
        return state_ref[32 * k : 32 * k + 32, :]

    fill_rows(row, 0, 32, src32, far32, to32)
    finish_tables(32, src32, far32, S_ref, A_ref)

    pad_targets(B_ref, to32)
    acc33[...] = jnp.zeros_like(acc33)
    for copy in copies:
        copy.wait()
    total = count_ref[0, 0]
    off = jnp.int32(0)
    for q in range(128):
        a = pairs_ref[0, q]
        b = pairs_ref[1, q]
        off_ref[0, off] = a
        off_ref[1, off] = b
        off = off + jnp.where(jnp.logical_and(q < total, a != b), 1, 0)
    def listed(g):
        items = []
        for u in range(OWN_GROUP // 2):
            q = g * (OWN_GROUP // 2) + u
            live = q < off
            a = jnp.where(live, off_ref[0, q], 0)
            b = jnp.where(live, off_ref[1, q], 0)
            items.append((a, jnp.where(live, a, 32), b))
            items.append((b, jnp.where(live, b, 32), a))
        return items

    def one_group(g, carry):
        tile_group(listed(g), S_ref, A_ref, B_ref, acc33)
        return carry

    tile_group([(b, b, b) for b in range(32)] + listed(0), S_ref, A_ref, B_ref, acc33)
    groups = lax.div(off + (OWN_GROUP // 2 - 1), OWN_GROUP // 2)
    lax.fori_loop(1, groups, one_group, 0)
    acc_ref[...] = acc33[0:32]


def start_kernel(
    send_hbm, counts_hbm, links_hbm, pos_hbm, vel_hbm, sig_hbm, mass_hbm, dens_hbm,
    state_ref, m1, m0, m2, m3, send_ref, counts_ref, links_ref, sig_ref, mass_ref, dens_ref, sem,
):
    copies = fetch(
        [
            (send_hbm, send_ref),
            (counts_hbm, counts_ref),
            (links_hbm, links_ref),
            (pos_hbm, state_ref.at[0:96]),
            (vel_hbm, state_ref.at[96:192]),
            (sig_hbm, sig_ref),
            (mass_hbm, mass_ref),
            (dens_hbm, dens_ref),
        ],
        sem,
    )
    for copy in copies:
        copy.wait()
    column = lanes_to_column(counts_ref[...].astype(f32))
    lane = lax.broadcasted_iota(jnp.int32, (32, 128), 1).astype(f32)
    mass = jnp.where(lane < column, mass_ref[...], 0.0)
    dens = dens_ref[...]
    square = dens * dens
    for k in range(6):
        state_ref[192 + 32 * k : 224 + 32 * k, :] = sig_ref[32 * k : 32 * k + 32, :] / square
    state_ref[384:416, :] = mass
    state_ref[416:448, :] = mass / dens
    gather_rims(send_ref, state_ref, (m0, m1, m2, m3), 14)
    links = links_ref[...].astype(f32)
    for msg in (m0, m1, m2, m3):
        msg[224:232, :] = jnp.zeros((8, 128), f32)
        msg[224:228, 0:48] = links


def cross_terms(send_ref, link_ref, back_ref, msgs, first, own_acc, S_ref, A_ref, B_ref, src32, far32, acc, ready):
    for face in range(4):
        def row(k, face=face):
            source = msgs if k < 12 else first
            return source[face][16 * k : 16 * k + 16, :]

        fill_rows(row, 16 * face, 16, src32, far32, None)
    finish_tables(64, src32, far32, S_ref, A_ref)
    acc[...] = own_acc[...]
    ready()

    depth, strip = parity("depth"), parity("strip")

    def one_group(g, carry):
        items = []
        for u in range(CROSS_GROUP // 4):
            q = g * (CROSS_GROUP // 4) + u
            back_d, back_s = 8 * (1 - depth), 16 + 8 * (1 - strip)
            for target, source in (
                (send_ref[0, link_ref[0, q]], 16 * depth + link_ref[1, q]),
                (send_ref[1, back_ref[back_d + 1, q]], 16 * (1 - depth) + back_ref[back_d, q]),
                (send_ref[2, link_ref[2, q]], 32 + 16 * strip + link_ref[3, q]),
                (send_ref[3, back_ref[back_s + 3, q]], 32 + 16 * (1 - strip) + back_ref[back_s + 2, q]),
            ):
                items.append((target, target, source))
        tile_group(items, S_ref, A_ref, B_ref, acc)
        return carry

    for g in range(48 // (CROSS_GROUP // 4)):
        one_group(g, 0)


def rates(state_ref, acc, flag, c):
    def total(f):
        at = pl.ds(8 * c * 32 + f, 8, stride=32)
        return kernel_coef * acc[at, :]

    def row(k):
        return state_ref[32 * k + 8 * c : 32 * k + 8 * c + 8, :]

    places = [row(k) for k in range(3)]
    motion = [row(3 + k) for k in range(3)]
    scaled = [row(6 + k) for k in range(6)]
    blade = (spin_rate * places[2], jnp.zeros_like(places[1]), -spin_rate * places[0])
    mass_sum = total(0)
    lever = [places[l] * mass_sum - total(1 + l) for l in range(3)]
    stress_sum = [total(4 + s) for s in range(6)]
    acceleration = []
    for k in range(3):
        force = jnp.zeros_like(mass_sum)
        for l in range(3):
            slot = voigt_index[k][l]
            force = force + scaled[slot] * lever[l]
            force = force + places[l] * stress_sum[slot]
        force = force - total(10 + k)
        force = force + blade_stiff * flag * (blade[k] - motion[k])
        if k == 2:
            force = force - gravity
        acceleration.append(force)
    volume_sum = total(13)
    motion_sum = [total(14 + k) for k in range(3)]
    place_sum = [total(17 + k) for k in range(3)]
    strain = []
    for comp, (a, b) in enumerate(voigt_pairs):
        rate = 0.5 * (places[b] * motion_sum[a] + places[a] * motion_sum[b])
        rate = rate - total(20 + comp)
        rate = rate - 0.5 * volume_sum * (motion[a] * places[b] + motion[b] * places[a])
        rate = rate + 0.5 * (motion[a] * place_sum[b] + motion[b] * place_sum[a])
        strain.append(rate)
    return acceleration, strain


def elastic_step(stress, strain, fraction):
    volumetric = strain[0] + strain[1] + strain[2]
    lame_first = bulk_mod - 2.0 * shear_mod / 3.0
    components = []
    for comp in range(6):
        change = 2.0 * shear_mod * strain[comp]
        if comp < 3:
            change = change + lame_first * volumetric
        components.append(stress[comp] + fraction * time_step * change)
    return components


def plastic_return(components, plastic, cohesion):
    for _ in range(RETURN_ITERS):
        mean = (components[0] + components[1] + components[2]) / 3.0
        dev = [components[k] - mean for k in range(3)] + list(components[3:])
        second = 0.5 * (dev[0] * dev[0] + dev[1] * dev[1] + dev[2] * dev[2])
        second = second + dev[3] * dev[3] + dev[4] * dev[4] + dev[5] * dev[5]
        shear = jnp.sqrt(second)
        limit = cohesion * (1.0 + plastic / (plastic + harden_scale))
        excess = jnp.maximum(shear + friction * 3.0 * mean - limit, 0.0)
        multiplier = (relax_rate / (shear_mod + 9.0 * bulk_mod * friction * friction + harden_mod)) * excess
        shrink = jnp.maximum(1.0 - shear_mod * multiplier / jnp.maximum(shear, tau_floor), 0.0)
        mean = mean - 3.0 * bulk_mod * friction * multiplier
        components = [dev[k] * shrink + mean for k in range(3)] + [dev[k] * shrink for k in range(3, 6)]
        plastic = plastic + multiplier
    return components, plastic


def contact_column(contact_ref):
    rows = lax.broadcasted_iota(jnp.int32, (32, 16), 0)
    hit = jnp.where(contact_ref[...] == rows, 1.0, 0.0)
    return jnp.sum(hit, axis=1, keepdims=True)


def half_kernel(
    state_ref, own_acc, B_ref,
    m1, m0, m2, m3, sig_hbm, plastic_hbm, cohesion_hbm, dens_hbm, send_hbm, link_hbm, contact_hbm,
    next_ref, n1, n0, n2, n3, back_out,
    S_ref, A_ref, src32, far32, acc, send_ref, link_ref, contact_ref, back_ref,
    sig_ref, plastic_ref, cohesion_ref, dens_ref, send_vmem, sem,
):
    for m, msg in enumerate((m0, m1, m2, m3)):
        back_out[8 * m : 8 * m + 8, :] = msg[224:232, :].astype(jnp.int32)
    copies = fetch(
        [
            (back_out, back_ref),
            (send_hbm, send_ref),
            (link_hbm, link_ref),
            (contact_hbm, contact_ref),
            (sig_hbm, sig_ref),
            (plastic_hbm, plastic_ref),
            (cohesion_hbm, cohesion_ref),
            (dens_hbm, dens_ref),
            (send_hbm, send_vmem),
        ],
        sem,
    )

    def ready():
        for copy in copies:
            copy.wait()

    cross_terms(
        send_ref, link_ref, back_ref, (m0, m1, m2, m3), (m0, m1, m2, m3), own_acc, S_ref, A_ref, B_ref, src32, far32, acc, ready
    )
    flags = contact_column(contact_ref)
    acc2 = acc.reshape(1024, 128)
    for c in range(4):
        at = slice(8 * c, 8 * c + 8)
        acceleration, strain = rates(state_ref, acc2, flags[at], c)
        stress = [sig_ref[32 * k + 8 * c : 32 * k + 8 * c + 8, :] for k in range(6)]
        trial = elastic_step(stress, strain, 0.5)
        for k in range(3):
            x = slice(32 * k + 8 * c, 32 * k + 8 * c + 8)
            v = slice(96 + 32 * k + 8 * c, 96 + 32 * k + 8 * c + 8)
            motion = state_ref[v, :]
            next_ref[x, :] = state_ref[x, :] + 0.5 * time_step * motion
            next_ref[v, :] = motion + 0.5 * time_step * acceleration[k]
        for k in range(6):
            next_ref[192 + 32 * k + 8 * c : 200 + 32 * k + 8 * c, :] = trial[k]
    trial = [next_ref[192 + 32 * k : 224 + 32 * k, :] for k in range(6)]
    half_stress, _ = plastic_return(trial, plastic_ref[...], cohesion_ref[...])
    dens = dens_ref[...]
    square = dens * dens
    for k in range(6):
        next_ref[192 + 32 * k : 224 + 32 * k, :] = half_stress[k] / square
    next_ref[384:448, :] = state_ref[384:448, :]
    gather_rims(send_vmem, next_ref, (n0, n1, n2, n3), 12)


def last_kernel(
    state_ref, own_acc, B_ref,
    m1, m0, m2, m3, f1, f0, f2, f3, back_vmem, sig_hbm, plastic_hbm, cohesion_hbm, pos_hbm, vel_hbm,
    send_hbm, link_hbm, contact_hbm, counts_hbm,
    pos_out, vel_out, sig_out, plastic_out,
    S_ref, A_ref, src32, far32, acc, send_ref, link_ref, contact_ref, back_ref,
    sig_ref, plastic_ref, cohesion_ref, pos_ref, vel_ref, counts_ref, sem,
):
    copies = fetch(
        [
            (back_vmem, back_ref),
            (send_hbm, send_ref),
            (link_hbm, link_ref),
            (contact_hbm, contact_ref),
            (counts_hbm, counts_ref),
            (sig_hbm, sig_ref),
            (plastic_hbm, plastic_ref),
            (cohesion_hbm, cohesion_ref),
            (pos_hbm, pos_ref),
            (vel_hbm, vel_ref),
        ],
        sem,
    )

    def ready():
        for copy in copies:
            copy.wait()

    cross_terms(
        send_ref, link_ref, back_ref, (m0, m1, m2, m3), (f0, f1, f2, f3), own_acc, S_ref, A_ref, B_ref, src32, far32, acc, ready
    )
    flags = contact_column(contact_ref)
    column = lanes_to_column(counts_ref[...].astype(f32))
    lane = lax.broadcasted_iota(jnp.int32, (8, 128), 1).astype(f32)
    acc2 = acc.reshape(1024, 128)
    for c in range(4):
        at = slice(8 * c, 8 * c + 8)
        keep = lane < column[at]
        acceleration, strain = rates(state_ref, acc2, flags[at], c)
        stress = [sig_ref[32 * k + 8 * c : 32 * k + 8 * c + 8, :] for k in range(6)]
        trial = elastic_step(stress, strain, 1.0)
        for k in range(3):
            x = slice(32 * k + 8 * c, 32 * k + 8 * c + 8)
            v = slice(96 + 32 * k + 8 * c, 96 + 32 * k + 8 * c + 8)
            pos_out[x, :] = jnp.where(keep, pos_ref[x, :] + time_step * state_ref[v, :], 0.0)
            vel_out[x, :] = jnp.where(keep, vel_ref[x, :] + time_step * acceleration[k], 0.0)
        for k in range(6):
            sig_out[32 * k + 8 * c : 32 * k + 8 * c + 8, :] = trial[k]
    keep = lax.broadcasted_iota(jnp.int32, (32, 128), 1).astype(f32) < column
    trial = [sig_out[32 * k : 32 * k + 32, :] for k in range(6)]
    new_stress, new_plastic = plastic_return(trial, plastic_ref[...], cohesion_ref[...])
    for k in range(6):
        sig_out[32 * k : 32 * k + 32, :] = jnp.where(keep, new_stress[k], 0.0)
    plastic_out[...] = jnp.where(keep, new_plastic, 0.0)


VMEM = pl.BlockSpec(memory_space=pltpu.VMEM)
HBM = pl.BlockSpec(memory_space=pltpu.HBM)
params = pltpu.CompilerParams(vmem_limit_bytes=48 * 1024 * 1024)


def in_hbm(value):
    return pltpu.with_memory_space_constraint(value, pltpu.HBM)


def shape(*dims, dtype=f32):
    return jax.ShapeDtypeStruct(dims, dtype)


def tables(count):
    return [
        pltpu.VMEM((count, 64, 128), bf16),
        pltpu.VMEM((count // 8, 128, 128), bf16),
        pltpu.VMEM((count * 32, 128), f32),
        pltpu.VMEM((count * 16, 128), f32),
    ]


def call(kernel, vmem, hbm, outs, scratch):
    return pl.pallas_call(
        kernel,
        out_shape=outs,
        in_specs=[VMEM] * len(vmem) + [HBM] * len(hbm),
        out_specs=[VMEM] * len(outs),
        scratch_shapes=scratch,
        compiler_params=params,
    )(*vmem, *hbm)


def shards(
    position, velocity, stress, plastic, particle_mass, density, cohesion,
    counts, block_pairs, pair_count, send_lists, cross_links, contact,
):
    pos = position.reshape(96, 128)
    vel = velocity.reshape(96, 128)
    sig = stress.reshape(192, 128)
    plastic_now = plastic.reshape(32, 128)
    mass = particle_mass.reshape(32, 128)
    dens = density.reshape(32, 128)
    cohesion_now = cohesion.reshape(32, 128)
    counts_now = counts.reshape(1, 32)
    pairs = jnp.swapaxes(block_pairs.reshape(128, 2), 0, 1)
    send = send_lists.reshape(4, 16)
    links = jnp.swapaxes(cross_links.reshape(2, 48, 2), 1, 2).reshape(4, 48)
    touched = contact.reshape(1, 16)

    rim = [shape(232, 128)] * 4
    half_rim = [shape(192, 128)] * 4
    def own(state):
        return call(
            own_kernel,
            [state, pair_count],
            [in_hbm(pairs)],
            [shape(32, 32, 128), shape(32, 240, 128, dtype=bf16)],
            tables(32)
            + [
                pltpu.VMEM((512, 128), f32),
                pltpu.VMEM((33, 32, 128), f32),
                pltpu.SMEM((2, 128), jnp.int32),
                pltpu.SMEM((2, 128), jnp.int32),
                pltpu.SemaphoreType.DMA((1,)),
            ],
        )

    state, *msgs = call(
        start_kernel,
        [],
        [in_hbm(x) for x in (send, counts_now, links, pos, vel, sig, mass, dens)],
        [shape(448, 128)] + rim,
        [
            pltpu.VMEM((4, 16), jnp.int32),
            pltpu.VMEM((1, 32), jnp.int32),
            pltpu.VMEM((4, 48), jnp.int32),
            pltpu.VMEM((192, 128), f32),
            pltpu.VMEM((32, 128), f32),
            pltpu.VMEM((32, 128), f32),
            pltpu.SemaphoreType.DMA((8,)),
        ],
    )

    def swap(msgs):
        depths = [swap_pairs(msgs[1 - odd], "depth", odd, False) for odd in (1, 0)]
        strips = [swap_pairs(msgs[2 + odd], "strip", odd, True) for odd in range(2)]
        return depths + strips

    cross_scratch = tables(64) + [
        pltpu.VMEM((32, 32, 128), f32),
        pltpu.SMEM((4, 16), jnp.int32),
        pltpu.SMEM((4, 48), jnp.int32),
        pltpu.VMEM((1, 16), jnp.int32),
        pltpu.SMEM((32, 128), jnp.int32),
        pltpu.VMEM((192, 128), f32),
        pltpu.VMEM((32, 128), f32),
        pltpu.VMEM((32, 128), f32),
    ]
    fields = [in_hbm(x) for x in (sig, plastic_now, cohesion_now)]
    lists = [in_hbm(x) for x in (send, links, touched)]
    far = swap(msgs)
    own_acc, to_side = own(state)
    state, *msgs, back = call(
        half_kernel,
        [state, own_acc, to_side, *far],
        fields + [in_hbm(dens)] + lists,
        [shape(448, 128)] + half_rim + [shape(32, 128, dtype=jnp.int32)],
        cross_scratch
        + [pltpu.VMEM((32, 128), f32), pltpu.VMEM((4, 16), jnp.int32), pltpu.SemaphoreType.DMA((9,))],
    )
    first, far = far, swap(msgs)
    own_acc, to_side = own(state)
    new_pos, new_vel, new_sig, new_plastic = call(
        last_kernel,
        [state, own_acc, to_side, *far, *first, back],
        fields + [in_hbm(pos), in_hbm(vel)] + lists + [in_hbm(counts_now)],
        [shape(96, 128), shape(96, 128), shape(192, 128), shape(32, 128)],
        cross_scratch
        + [
            pltpu.VMEM((96, 128), f32),
            pltpu.VMEM((96, 128), f32),
            pltpu.VMEM((1, 32), jnp.int32),
            pltpu.SemaphoreType.DMA((10,)),
        ],
    )
    return (
        new_pos.reshape(position.shape),
        new_vel.reshape(velocity.shape),
        new_sig.reshape(stress.shape),
        new_plastic.reshape(plastic.shape),
    )


def solution(mesh):
    def spec(rank):
        return P("strip", "depth", *([None] * (rank - 2)))

    return jax.shard_map(
        shards,
        mesh=mesh,
        in_specs=tuple(spec(r) for r in (5, 5, 5, 4, 4, 4, 4, 3, 4, 2, 4, 5, 3)),
        out_specs=tuple(spec(r) for r in (5, 5, 5, 4)),
        check_vma=False,
    )
```

```python
import functools

import jax
import jax.numpy as jnp
from jax import lax
from jax.experimental import pallas as pl
from jax.experimental.pallas import tpu as pltpu
from jax.sharding import PartitionSpec as P

RETURN_ITERS = 4
OWN_GROUP = 96
CROSS_GROUP = 192

smooth_len = 1.5
kernel_coef = -105.0 / (3.141592653589793 * 1.5**5)
time_step = 0.25
gravity = 1.0
spin_rate = 2.0
blade_stiff = 4.0
bulk_mod = 2.0
shear_mod = 1.5
friction = 0.25
harden_scale = 0.05
harden_mod = 0.5
relax_rate = 0.7
tau_floor = 0.5
voigt_index = ((0, 3, 5), (3, 1, 4), (5, 4, 2))
voigt_pairs = ((0, 0), (1, 1), (2, 2), (0, 1), (1, 2), (0, 2))
bf16 = jnp.bfloat16
f32 = jnp.float32


def swap_pairs(value, axis, odd, closed):
    count = lax.axis_size(axis)
    pairs = []
    for i in range(odd, count, 2):
        j = (i + 1) % count
        if j == i + 1 or closed:
            pairs += [(i, j), (j, i)]
    return lax.ppermute(value, axis, pairs)


def parity(axis):
    return lax.rem(lax.axis_index(axis), 2)


def halves(value):
    high = value.astype(bf16).astype(f32)
    return high, value - high


def source_rows(row):
    places = [row(k) for k in range(3)]
    motion = [row(3 + k) for k in range(3)]
    scaled = [row(6 + k) for k in range(6)]
    mass, volume = row(12), row(13)
    out = [mass]
    out += [mass * x for x in places]
    out += [mass * s for s in scaled]
    for k in range(3):
        dotted = scaled[voigt_index[k][0]] * places[0]
        dotted = dotted + scaled[voigt_index[k][1]] * places[1]
        dotted = dotted + scaled[voigt_index[k][2]] * places[2]
        out.append(mass * dotted)
    out.append(volume)
    out += [volume * v for v in motion]
    out += [volume * x for x in places]
    for a, b in voigt_pairs:
        out.append(volume * (0.5 * (motion[a] * places[b] + motion[b] * places[a])))
    return out


def distance_rows(row):
    places = [row(k) * (1.0 / smooth_len) for k in range(3)]
    square = places[0] * places[0] + places[1] * places[1] + places[2] * places[2]
    high, low = zip(*[halves(x) for x in places])
    n0, rest = halves(square)
    n1, n2 = halves(rest)
    one = jnp.ones_like(square)
    zero = jnp.zeros_like(square)
    from_side = [-2.0 * x for x in high + low + high] + [n0, n1, n2, one, one, one, zero]
    to_side = list(high + high + low) + [one, one, one, n0, n1, n2, zero]
    return from_side, to_side


def fill_rows(row, base, count, src32, far32, to32):
    for f, value in enumerate(source_rows(row)):
        src32[pl.ds(base * 32 + f, count, stride=32), :] = value
    from_side, to_side = distance_rows(row)
    for f, value in enumerate(from_side):
        far32[pl.ds(base * 16 + f, count, stride=16), :] = value
    if to32 is not None:
        for f, value in enumerate(to_side):
            to32[pl.ds(base * 16 + f, count, stride=16), :] = value


def finish_tables(count, src32, far32, S_ref, A_ref):
    def eight(i, carry):
        for half in range(2):
            rows = far32[pl.ds(pl.multiple_of(i * 128 + 64 * half, 64), 64), :]
            A_ref[2 * i + half] = rows.T.astype(bf16)
        for u in range(8):
            b = i * 8 + u
            value = src32[pl.ds(pl.multiple_of(b * 32, 32), 32), :]
            high = value.astype(bf16)
            S_ref[b, 0:32, :] = high
            S_ref[b, 32:64, :] = (value - high.astype(f32)).astype(bf16)
        return carry

    lax.fori_loop(0, count // 8, eight, 0)


def pad_targets(B_ref, to32):
    def one(b, carry):
        B_ref[b, 0:48, :] = jnp.zeros((48, 128), bf16)
        B_ref[b, 64:112, :] = jnp.zeros((48, 128), bf16)
        B_ref[b, 48:64, :] = to32[pl.ds(pl.multiple_of(b * 16, 16), 16), :].astype(bf16)
        return carry

    lax.fori_loop(0, 32, one, 0)


def closeness_cubed(square):
    square = jnp.maximum(square, 1e-30)
    close = jnp.maximum(1.0 - square * lax.rsqrt(square), 0.0)
    return close * close * close


def tile_group(items, S_ref, A_ref, B_ref, acc_ref):
    outs = []
    for target, into, source in items:
        if isinstance(source, int):
            start, quad = 48 - 16 * (source % 4), source // 4
        else:
            start = pl.multiple_of(48 - 16 * lax.rem(source, 4), 16)
            quad = lax.div(source, 4)
        square = jnp.dot(
            A_ref[quad], B_ref[target, pl.ds(start, 64), :], preferred_element_type=f32
        )
        kernel = closeness_cubed(square)
        high = kernel.astype(bf16)
        low = (kernel - high.astype(f32)).astype(bf16)
        rows = S_ref[source]
        both = jnp.dot(
            jnp.concatenate([rows, rows], 1),
            jnp.concatenate([high, low], 0),
            preferred_element_type=f32,
        )
        outs.append((into, both[:32] + both[32:]))
    for into, value in outs:
        acc_ref[into] += value


def lanes_to_column(values):
    n = values.shape[1]
    rows = lax.broadcasted_iota(jnp.int32, (n, n), 0)
    cols = lax.broadcasted_iota(jnp.int32, (n, n), 1)
    return jnp.sum(jnp.where(rows == cols, values, 0.0), axis=1, keepdims=True)


def gather_rims(send_ref, state_ref, msgs, rows_sent):
    send = send_ref[...].astype(f32)
    even_d, even_s = parity("depth") == 0, parity("strip") == 0
    order = [
        jnp.where(even_d, send[0:1], send[1:2]),
        jnp.where(even_d, send[1:2], send[0:1]),
        jnp.where(even_s, send[2:3], send[3:4]),
        jnp.where(even_s, send[3:4], send[2:3]),
    ]
    block = lax.rem(lax.broadcasted_iota(jnp.int32, (64, 96), 1), 32).astype(f32)
    column = jnp.concatenate([lanes_to_column(row) for row in order], 0)
    pick = jnp.where(block == column, 1.0, 0.0).astype(bf16)
    for k in range(rows_sent):
        high, rest = halves(state_ref[32 * k : 32 * k + 32, :])
        middle, low = halves(rest)
        parts = jnp.concatenate([x.astype(bf16) for x in (high, middle, low)], 0)
        rows = jnp.dot(pick, parts, preferred_element_type=f32)
        for m in range(4):
            msgs[m][16 * k : 16 * k + 16, :] = rows[16 * m : 16 * m + 16]


def fetch(pairs, sem):
    copies = [pltpu.make_async_copy(a, b, sem.at[i]) for i, (a, b) in enumerate(pairs)]
    for copy in copies:
        copy.start()
    return copies


def own_kernel(
    state_ref, count_ref, pairs_hbm, acc_ref, B_ref,
    S_ref, A_ref, src32, far32, to32, acc33, off_ref, pairs_ref, sem,
):
    copies = fetch([(pairs_hbm, pairs_ref)], sem)

    def row(k):
        return state_ref[32 * k : 32 * k + 32, :]

    fill_rows(row, 0, 32, src32, far32, to32)
    finish_tables(32, src32, far32, S_ref, A_ref)

    pad_targets(B_ref, to32)
    acc33[...] = jnp.zeros_like(acc33)
    for copy in copies:
        copy.wait()
    total = count_ref[0, 0]
    off = jnp.int32(0)
    for q in range(128):
        a = pairs_ref[0, q]
        b = pairs_ref[1, q]
        off_ref[0, off] = a
        off_ref[1, off] = b
        off = off + jnp.where(jnp.logical_and(q < total, a != b), 1, 0)
    def listed(g):
        items = []
        for u in range(OWN_GROUP // 2):
            q = g * (OWN_GROUP // 2) + u
            live = q < off
            a = jnp.where(live, off_ref[0, q], 0)
            b = jnp.where(live, off_ref[1, q], 0)
            items.append((a, jnp.where(live, a, 32), b))
            items.append((b, jnp.where(live, b, 32), a))
        return items

    def one_group(g, carry):
        tile_group(listed(g), S_ref, A_ref, B_ref, acc33)
        return carry

    tile_group([(b, b, b) for b in range(32)] + listed(0), S_ref, A_ref, B_ref, acc33)
    groups = lax.div(off + (OWN_GROUP // 2 - 1), OWN_GROUP // 2)
    lax.fori_loop(1, groups, one_group, 0)
    acc_ref[...] = acc33[0:32]


def start_kernel(
    send_hbm, counts_hbm, links_hbm, pos_hbm, vel_hbm, sig_hbm, mass_hbm, dens_hbm,
    state_ref, m1, m0, m2, m3, send_ref, counts_ref, links_ref, sig_ref, mass_ref, dens_ref, sem,
):
    copies = fetch(
        [
            (send_hbm, send_ref),
            (counts_hbm, counts_ref),
            (links_hbm, links_ref),
            (pos_hbm, state_ref.at[0:96]),
            (vel_hbm, state_ref.at[96:192]),
            (sig_hbm, sig_ref),
            (mass_hbm, mass_ref),
            (dens_hbm, dens_ref),
        ],
        sem,
    )
    for copy in copies:
        copy.wait()
    column = lanes_to_column(counts_ref[...].astype(f32))
    lane = lax.broadcasted_iota(jnp.int32, (32, 128), 1).astype(f32)
    mass = jnp.where(lane < column, mass_ref[...], 0.0)
    dens = dens_ref[...]
    square = dens * dens
    for k in range(6):
        state_ref[192 + 32 * k : 224 + 32 * k, :] = sig_ref[32 * k : 32 * k + 32, :] / square
    state_ref[384:416, :] = mass
    state_ref[416:448, :] = mass / dens
    gather_rims(send_ref, state_ref, (m0, m1, m2, m3), 14)
    links = links_ref[...].astype(f32)
    for msg in (m0, m1, m2, m3):
        msg[224:232, :] = jnp.zeros((8, 128), f32)
        msg[224:228, 0:48] = links


def cross_terms(send_ref, link_ref, back_ref, msgs, first, own_acc, S_ref, A_ref, B_ref, src32, far32, acc, ready):
    for face in range(4):
        def row(k, face=face):
            source = msgs if k < 12 else first
            return source[face][16 * k : 16 * k + 16, :]

        fill_rows(row, 16 * face, 16, src32, far32, None)
    finish_tables(64, src32, far32, S_ref, A_ref)
    acc[...] = own_acc[...]
    ready()

    depth, strip = parity("depth"), parity("strip")

    def one_group(g, carry):
        items = []
        for u in range(CROSS_GROUP // 4):
            q = g * (CROSS_GROUP // 4) + u
            back_d, back_s = 8 * (1 - depth), 16 + 8 * (1 - strip)
            for target, source in (
                (send_ref[0, link_ref[0, q]], 16 * depth + link_ref[1, q]),
                (send_ref[1, back_ref[back_d + 1, q]], 16 * (1 - depth) + back_ref[back_d, q]),
                (send_ref[2, link_ref[2, q]], 32 + 16 * strip + link_ref[3, q]),
                (send_ref[3, back_ref[back_s + 3, q]], 32 + 16 * (1 - strip) + back_ref[back_s + 2, q]),
            ):
                items.append((target, target, source))
        tile_group(items, S_ref, A_ref, B_ref, acc)
        return carry

    for g in range(48 // (CROSS_GROUP // 4)):
        one_group(g, 0)


def rates(state_ref, acc, flag, c):
    def total(f):
        at = pl.ds(8 * c * 32 + f, 8, stride=32)
        return kernel_coef * acc[at, :]

    def row(k):
        return state_ref[32 * k + 8 * c : 32 * k + 8 * c + 8, :]

    places = [row(k) for k in range(3)]
    motion = [row(3 + k) for k in range(3)]
    scaled = [row(6 + k) for k in range(6)]
    blade = (spin_rate * places[2], jnp.zeros_like(places[1]), -spin_rate * places[0])
    mass_sum = total(0)
    lever = [places[l] * mass_sum - total(1 + l) for l in range(3)]
    stress_sum = [total(4 + s) for s in range(6)]
    acceleration = []
    for k in range(3):
        force = jnp.zeros_like(mass_sum)
        for l in range(3):
            slot = voigt_index[k][l]
            force = force + scaled[slot] * lever[l]
            force = force + places[l] * stress_sum[slot]
        force = force - total(10 + k)
        force = force + blade_stiff * flag * (blade[k] - motion[k])
        if k == 2:
            force = force - gravity
        acceleration.append(force)
    volume_sum = total(13)
    motion_sum = [total(14 + k) for k in range(3)]
    place_sum = [total(17 + k) for k in range(3)]
    strain = []
    for comp, (a, b) in enumerate(voigt_pairs):
        rate = 0.5 * (places[b] * motion_sum[a] + places[a] * motion_sum[b])
        rate = rate - total(20 + comp)
        rate = rate - 0.5 * volume_sum * (motion[a] * places[b] + motion[b] * places[a])
        rate = rate + 0.5 * (motion[a] * place_sum[b] + motion[b] * place_sum[a])
        strain.append(rate)
    return acceleration, strain


def elastic_step(stress, strain, fraction):
    volumetric = strain[0] + strain[1] + strain[2]
    lame_first = bulk_mod - 2.0 * shear_mod / 3.0
    components = []
    for comp in range(6):
        change = 2.0 * shear_mod * strain[comp]
        if comp < 3:
            change = change + lame_first * volumetric
        components.append(stress[comp] + fraction * time_step * change)
    return components


def plastic_return(components, plastic, cohesion):
    for _ in range(RETURN_ITERS):
        mean = (components[0] + components[1] + components[2]) / 3.0
        dev = [components[k] - mean for k in range(3)] + list(components[3:])
        second = 0.5 * (dev[0] * dev[0] + dev[1] * dev[1] + dev[2] * dev[2])
        second = second + dev[3] * dev[3] + dev[4] * dev[4] + dev[5] * dev[5]
        shear = jnp.sqrt(second)
        limit = cohesion * (1.0 + plastic / (plastic + harden_scale))
        excess = jnp.maximum(shear + friction * 3.0 * mean - limit, 0.0)
        multiplier = (relax_rate / (shear_mod + 9.0 * bulk_mod * friction * friction + harden_mod)) * excess
        shrink = jnp.maximum(1.0 - shear_mod * multiplier / jnp.maximum(shear, tau_floor), 0.0)
        mean = mean - 3.0 * bulk_mod * friction * multiplier
        components = [dev[k] * shrink + mean for k in range(3)] + [dev[k] * shrink for k in range(3, 6)]
        plastic = plastic + multiplier
    return components, plastic


def contact_column(contact_ref):
    rows = lax.broadcasted_iota(jnp.int32, (32, 16), 0)
    hit = jnp.where(contact_ref[...] == rows, 1.0, 0.0)
    return jnp.sum(hit, axis=1, keepdims=True)


def half_kernel(
    state_ref, own_acc, B_ref,
    m1, m0, m2, m3, sig_hbm, plastic_hbm, cohesion_hbm, dens_hbm, send_hbm, link_hbm, contact_hbm,
    next_ref, n1, n0, n2, n3, back_out,
    S_ref, A_ref, src32, far32, acc, send_ref, link_ref, contact_ref, back_ref,
    sig_ref, plastic_ref, cohesion_ref, dens_ref, send_vmem, sem,
):
    for m, msg in enumerate((m0, m1, m2, m3)):
        back_out[8 * m : 8 * m + 8, :] = msg[224:232, :].astype(jnp.int32)
    copies = fetch(
        [
            (back_out, back_ref),
            (send_hbm, send_ref),
            (link_hbm, link_ref),
            (contact_hbm, contact_ref),
            (sig_hbm, sig_ref),
            (plastic_hbm, plastic_ref),
            (cohesion_hbm, cohesion_ref),
            (dens_hbm, dens_ref),
            (send_hbm, send_vmem),
        ],
        sem,
    )

    def ready():
        for copy in copies:
            copy.wait()

    cross_terms(
        send_ref, link_ref, back_ref, (m0, m1, m2, m3), (m0, m1, m2, m3), own_acc, S_ref, A_ref, B_ref, src32, far32, acc, ready
    )
    flags = contact_column(contact_ref)
    acc2 = acc.reshape(1024, 128)
    for c in range(4):
        at = slice(8 * c, 8 * c + 8)
        acceleration, strain = rates(state_ref, acc2, flags[at], c)
        stress = [sig_ref[32 * k + 8 * c : 32 * k + 8 * c + 8, :] for k in range(6)]
        trial = elastic_step(stress, strain, 0.5)
        for k in range(3):
            x = slice(32 * k + 8 * c, 32 * k + 8 * c + 8)
            v = slice(96 + 32 * k + 8 * c, 96 + 32 * k + 8 * c + 8)
            motion = state_ref[v, :]
            next_ref[x, :] = state_ref[x, :] + 0.5 * time_step * motion
            next_ref[v, :] = motion + 0.5 * time_step * acceleration[k]
        for k in range(6):
            next_ref[192 + 32 * k + 8 * c : 200 + 32 * k + 8 * c, :] = trial[k]
    trial = [next_ref[192 + 32 * k : 224 + 32 * k, :] for k in range(6)]
    half_stress, _ = plastic_return(trial, plastic_ref[...], cohesion_ref[...])
    dens = dens_ref[...]
    square = dens * dens
    for k in range(6):
        next_ref[192 + 32 * k : 224 + 32 * k, :] = half_stress[k] / square
    next_ref[384:448, :] = state_ref[384:448, :]
    gather_rims(send_vmem, next_ref, (n0, n1, n2, n3), 12)


def last_kernel(
    state_ref, own_acc, B_ref,
    m1, m0, m2, m3, f1, f0, f2, f3, back_vmem, sig_hbm, plastic_hbm, cohesion_hbm, pos_hbm, vel_hbm,
    send_hbm, link_hbm, contact_hbm, counts_hbm,
    pos_hbm_out, vel_hbm_out, sig_hbm_out, plastic_hbm_out,
    S_ref, A_ref, src32, far32, acc, send_ref, link_ref, contact_ref, back_ref,
    sig_ref, plastic_ref, cohesion_ref, pos_ref, vel_ref, counts_ref,
    pos_out, vel_out, sig_out, plastic_out, out_sem, late_sem, sem,
):
    copies = fetch(
        [
            (back_vmem, back_ref),
            (send_hbm, send_ref),
            (link_hbm, link_ref),
            (contact_hbm, contact_ref),
            (counts_hbm, counts_ref),
            (sig_hbm, sig_ref),
            (plastic_hbm, plastic_ref),
            (cohesion_hbm, cohesion_ref),
            (pos_hbm, pos_ref),
            (vel_hbm, vel_ref),
        ],
        sem,
    )

    def ready():
        for copy in copies:
            copy.wait()

    cross_terms(
        send_ref, link_ref, back_ref, (m0, m1, m2, m3), (f0, f1, f2, f3), own_acc, S_ref, A_ref, B_ref, src32, far32, acc, ready
    )
    flags = contact_column(contact_ref)
    column = lanes_to_column(counts_ref[...].astype(f32))
    lane = lax.broadcasted_iota(jnp.int32, (8, 128), 1).astype(f32)
    acc2 = acc.reshape(1024, 128)
    for c in range(4):
        at = slice(8 * c, 8 * c + 8)
        keep = lane < column[at]
        acceleration, strain = rates(state_ref, acc2, flags[at], c)
        stress = [sig_ref[32 * k + 8 * c : 32 * k + 8 * c + 8, :] for k in range(6)]
        trial = elastic_step(stress, strain, 1.0)
        for k in range(3):
            x = slice(32 * k + 8 * c, 32 * k + 8 * c + 8)
            v = slice(96 + 32 * k + 8 * c, 96 + 32 * k + 8 * c + 8)
            pos_out[x, :] = jnp.where(keep, pos_ref[x, :] + time_step * state_ref[v, :], 0.0)
            vel_out[x, :] = jnp.where(keep, vel_ref[x, :] + time_step * acceleration[k], 0.0)
        for k in range(6):
            sig_out[32 * k + 8 * c : 32 * k + 8 * c + 8, :] = trial[k]
    sent = fetch([(pos_out, pos_hbm_out), (vel_out, vel_hbm_out)], out_sem)
    keep = lax.broadcasted_iota(jnp.int32, (32, 128), 1).astype(f32) < column
    trial = [sig_out[32 * k : 32 * k + 32, :] for k in range(6)]
    new_stress, new_plastic = plastic_return(trial, plastic_ref[...], cohesion_ref[...])
    for k in range(6):
        sig_out[32 * k : 32 * k + 32, :] = jnp.where(keep, new_stress[k], 0.0)
    plastic_out[...] = jnp.where(keep, new_plastic, 0.0)
    for copy in sent + fetch([(sig_out, sig_hbm_out), (plastic_out, plastic_hbm_out)], late_sem):
        copy.wait()


VMEM = pl.BlockSpec(memory_space=pltpu.VMEM)
HBM = pl.BlockSpec(memory_space=pltpu.HBM)
params = pltpu.CompilerParams(vmem_limit_bytes=48 * 1024 * 1024)


def in_hbm(value):
    return pltpu.with_memory_space_constraint(value, pltpu.HBM)


def shape(*dims, dtype=f32):
    return jax.ShapeDtypeStruct(dims, dtype)


def tables(count):
    return [
        pltpu.VMEM((count, 64, 128), bf16),
        pltpu.VMEM((count // 4, 128, 64), bf16),
        pltpu.VMEM((count * 32, 128), f32),
        pltpu.VMEM((count * 16, 128), f32),
    ]


def call(kernel, vmem, hbm, outs, scratch, place=VMEM):
    return pl.pallas_call(
        kernel,
        out_shape=outs,
        in_specs=[VMEM] * len(vmem) + [HBM] * len(hbm),
        out_specs=[place] * len(outs),
        scratch_shapes=scratch,
        compiler_params=params,
    )(*vmem, *hbm)


def shards(
    position, velocity, stress, plastic, particle_mass, density, cohesion,
    counts, block_pairs, pair_count, send_lists, cross_links, contact,
):
    pos = position.reshape(96, 128)
    vel = velocity.reshape(96, 128)
    sig = stress.reshape(192, 128)
    plastic_now = plastic.reshape(32, 128)
    mass = particle_mass.reshape(32, 128)
    dens = density.reshape(32, 128)
    cohesion_now = cohesion.reshape(32, 128)
    counts_now = counts.reshape(1, 32)
    pairs = jnp.swapaxes(block_pairs.reshape(128, 2), 0, 1)
    send = send_lists.reshape(4, 16)
    links = jnp.swapaxes(cross_links.reshape(2, 48, 2), 1, 2).reshape(4, 48)
    touched = contact.reshape(1, 16)

    rim = [shape(232, 128)] * 4
    half_rim = [shape(192, 128)] * 4
    def own(state):
        return call(
            own_kernel,
            [state, pair_count],
            [in_hbm(pairs)],
            [shape(32, 32, 128), shape(32, 112, 128, dtype=bf16)],
            tables(32)
            + [
                pltpu.VMEM((512, 128), f32),
                pltpu.VMEM((33, 32, 128), f32),
                pltpu.SMEM((2, 128), jnp.int32),
                pltpu.SMEM((2, 128), jnp.int32),
                pltpu.SemaphoreType.DMA((1,)),
            ],
        )

    state, *msgs = call(
        start_kernel,
        [],
        [in_hbm(x) for x in (send, counts_now, links, pos, vel, sig, mass, dens)],
        [shape(448, 128)] + rim,
        [
            pltpu.VMEM((4, 16), jnp.int32),
            pltpu.VMEM((1, 32), jnp.int32),
            pltpu.VMEM((4, 48), jnp.int32),
            pltpu.VMEM((192, 128), f32),
            pltpu.VMEM((32, 128), f32),
            pltpu.VMEM((32, 128), f32),
            pltpu.SemaphoreType.DMA((8,)),
        ],
    )

    def swap(msgs):
        depths = [swap_pairs(msgs[1 - odd], "depth", odd, False) for odd in (1, 0)]
        strips = [swap_pairs(msgs[2 + odd], "strip", odd, True) for odd in range(2)]
        return depths + strips

    cross_scratch = tables(64) + [
        pltpu.VMEM((32, 32, 128), f32),
        pltpu.SMEM((4, 16), jnp.int32),
        pltpu.SMEM((4, 48), jnp.int32),
        pltpu.VMEM((1, 16), jnp.int32),
        pltpu.SMEM((32, 128), jnp.int32),
        pltpu.VMEM((192, 128), f32),
        pltpu.VMEM((32, 128), f32),
        pltpu.VMEM((32, 128), f32),
    ]
    fields = [in_hbm(x) for x in (sig, plastic_now, cohesion_now)]
    lists = [in_hbm(x) for x in (send, links, touched)]
    far = swap(msgs)
    own_acc, to_side = own(state)
    state, *msgs, back = call(
        half_kernel,
        [state, own_acc, to_side, *far],
        fields + [in_hbm(dens)] + lists,
        [shape(448, 128)] + half_rim + [shape(32, 128, dtype=jnp.int32)],
        cross_scratch
        + [pltpu.VMEM((32, 128), f32), pltpu.VMEM((4, 16), jnp.int32), pltpu.SemaphoreType.DMA((9,))],
    )
    first, far = far, swap(msgs)
    own_acc, to_side = own(state)
    new_pos, new_vel, new_sig, new_plastic = call(
        last_kernel,
        [state, own_acc, to_side, *far, *first, back],
        fields + [in_hbm(pos), in_hbm(vel)] + lists + [in_hbm(counts_now)],
        [shape(96, 128), shape(96, 128), shape(192, 128), shape(32, 128)],
        cross_scratch
        + [
            pltpu.VMEM((96, 128), f32),
            pltpu.VMEM((96, 128), f32),
            pltpu.VMEM((1, 32), jnp.int32),
            pltpu.VMEM((96, 128), f32),
            pltpu.VMEM((96, 128), f32),
            pltpu.VMEM((192, 128), f32),
            pltpu.VMEM((32, 128), f32),
            pltpu.SemaphoreType.DMA((2,)),
            pltpu.SemaphoreType.DMA((2,)),
            pltpu.SemaphoreType.DMA((10,)),
        ],
        HBM,
    )
    return (
        new_pos.reshape(position.shape),
        new_vel.reshape(velocity.shape),
        new_sig.reshape(stress.shape),
        new_plastic.reshape(plastic.shape),
    )


def solution(mesh):
    def spec(rank):
        return P("strip", "depth", *([None] * (rank - 2)))

    return jax.shard_map(
        shards,
        mesh=mesh,
        in_specs=tuple(spec(r) for r in (5, 5, 5, 4, 4, 4, 4, 3, 4, 2, 4, 5, 3)),
        out_specs=tuple(spec(r) for r in (5, 5, 5, 4)),
        check_vma=False,
    )
```
